32 devices in a mesh: grp: 4 (over x, core), tile: 8 (over z, y).
Axes of the slice: x: 2, y: 2, z: 4, core: 2. Of those that a mesh axis runs over, the one named last changes fastest.
Arguments:
- air_state: float32 [256, 128, 768], P('tile', 'grp'), may hold values from -400 to 400
- cotangent: float32 [256, 128, 768], P('tile', 'grp'), may hold values from -0.0625 to 0.0625
- cost_count: int32 [256, 128], P('tile', 'grp'), may hold values from 1 to 2, as said below
- assignment: int32 [256, 128], P('tile', 'grp'), may hold values from 0 to 1023, as said below
- orientation: int32 [8, 4], P('tile', 'grp'), may hold values from 0 to 3
- weight_in: bfloat16 [768, 512], replicated, may hold values from -0.21875 to 0.21875
- weight_out: bfloat16 [512, 768], replicated, may hold values from -0.25 to 0.25
Outputs:
- tendency: float32 [32768, 768], P(('grp', 'tile'))
- weight_in_grad: float32 [393216], P(('grp', 'tile'))
- weight_out_grad: float32 [393216], P(('grp', 'tile'))
The draws below stay inside these ranges and needn't reach their ends.
Inputs may be any that keep to these rules, and one draw needn't show every extreme that they name: `cost_count`: every batch receives exactly 256 columns of cost 2; one device holds at most 512 of them, and some device exactly that many. `assignment`: on every device the values form a permutation of 0 to 1023.
All inputs are finite; a program needn't handle non-finite values.
Results may differ from the reference program's by a relative error of at most 0.0035.
Values sent between devices are 32-bit elements; how exact they have to be, the bound alone decides.
No kernel may reach another device: no remote copies, remote signals or barrier semaphores. Data moves between devices by JAX's collectives and lax.ppermute only.
A program may use at most 128 MiB of HBM per device.

```python
import math
import jax
import jax.numpy as jnp
from jax import lax

V = 8
L = 96
H = 512
SIDE = 32
DSTEPS = 2
F = 768
COLS = 1024
K2 = 256
TILES = 32
PAIR = 32
XG = 256
YG = 128
N_GRP = 4
N_TILE = 8


def draw_air_state(key, part):
    k_feat, k_cell, k_base, k_wind = jax.random.split(jax.random.fold_in(key, 11), 4)
    feat_scale = jnp.exp(jax.random.uniform(k_feat, (F,), jnp.float32, 0.0, math.log(10.0)))
    cell_scale = jnp.exp(jax.random.uniform(k_cell, (XG, YG, 1), jnp.float32, 0.0, math.log(10.0)))
    wind_scale = jax.random.uniform(k_wind, (F,), jnp.float32, 0.4, 1.0)
    base_draw = jax.random.truncated_normal(k_base, -4.0, 4.0, (XG, YG, F), jnp.float32)
    is_wind = jnp.arange(F) < 2 * L
    spread_scale = jnp.where(is_wind, wind_scale, feat_scale * cell_scale)
    return base_draw * spread_scale


def column_plan(key):
    base_key = jax.random.fold_in(key, 5)
    k_sign, k_size, k_order, k_label = jax.random.split(base_key, 4)
    half_count = TILES // 2
    spread = jax.random.randint(k_size, (half_count,), 0, K2 + 1)
    spread = spread.at[0].set(K2)
    sign_flip = 1 - 2 * jax.random.randint(k_sign, (half_count,), 0, 2)
    heavy_count = jnp.stack([K2 + sign_flip * spread, K2 - sign_flip * spread], axis=1).reshape(TILES)
    rank_order = jax.vmap(lambda sub_key: jax.random.permutation(sub_key, COLS))(jax.random.split(k_order, TILES))
    rank_order = rank_order.astype(jnp.int32)
    cost_rows = 1 + (rank_order < heavy_count[:, None]).astype(jnp.int32)
    offset = (jnp.cumsum(heavy_count) - heavy_count) % TILES
    local_batch = (rank_order + offset[:, None]) % TILES
    relabel = jax.random.permutation(k_label, TILES).astype(jnp.int32)
    destination = relabel[local_batch] * PAIR + rank_order // TILES
    return (cost_rows, destination)


def tile_grid(per_tile):
    cycle_size = XG // SIDE
    band_count = YG // SIDE
    shaped = per_tile.reshape(band_count, cycle_size, SIDE, SIDE)
    return shaped.transpose(1, 2, 0, 3).reshape(XG, YG).astype(jnp.int32)


def draw_cost_count(key, part):
    return tile_grid(column_plan(key)[0])


def draw_assignment(key, part):
    return tile_grid(column_plan(key)[1])


def with_ends(drawn, rng, low, top_value):
    place = [jax.random.randint(jax.random.fold_in(rng, axis), (), 0, length) for axis, length in enumerate(drawn.shape)]
    main_axis = drawn.shape.index(max(drawn.shape))
    next_to = place[:main_axis] + [(place[main_axis] + 1) % drawn.shape[main_axis]] + place[main_axis + 1:]
    return drawn.at[tuple(place)].set(low).at[tuple(next_to)].set(top_value)


def shard_levels(rng, dims, shards, low, top_value):
    level, own = 1.0, jax.random.fold_in(rng, 6)
    for axis_at, blocks in shards:
        steps = jnp.exp(jax.random.uniform(jax.random.fold_in(own, axis_at), (blocks,), jnp.float32, low / len(shards), top_value / len(shards)))
        level = level * jnp.repeat(steps, dims[axis_at] // blocks).reshape([-1 if axis == axis_at else 1 for axis in range(len(dims))])
    return level


def bell_draw(rng, dims, deviation, reach, cuts=(), kind=jnp.bfloat16):
    gain = shard_levels(rng, dims, cuts, -0.22, 0.18) if cuts else 1.0
    result = jax.random.normal(rng, dims, jnp.float32) * deviation * gain
    return jnp.minimum(jnp.maximum(result, -reach), reach).astype(kind)


def setup_inputs(seed: int = 0) -> dict:
    seeds = jax.random.split(jax.random.key(seed), 8)
    air_state = draw_air_state(jax.random.fold_in(seeds[7], 71), 0)
    cotangent = bell_draw(seeds[1], (XG, YG, F), (2.0 * (N_GRP * N_TILE * SIDE * SIDE) ** -0.5), 0.0625, ((0, 8), (1, 4)), jnp.float32)
    cost_count = draw_cost_count(jax.random.fold_in(seeds[7], 71), 0)
    assignment = draw_assignment(jax.random.fold_in(seeds[7], 71), 0)
    orientation = with_ends(jax.random.randint(seeds[4], (N_TILE, N_GRP), 0, 4), jax.random.fold_in(seeds[4], 1), 0, 3).astype(jnp.int32)
    weight_in = bell_draw(seeds[5], (F, H), F ** -0.5, 0.21875)
    weight_out = bell_draw(seeds[6], (H, F), H ** -0.5, 0.25)
    return dict(air_state=air_state, cotangent=cotangent, cost_count=cost_count, assignment=assignment, orientation=orientation, weight_in=weight_in, weight_out=weight_out)


tau_rate = 0.5
courant = 0.1
eps_norm = 1e-06

def turn_frame(field_in, quarter_turns):

    def make_turn(turn_count):

        def apply_turn(block_in):
            rotated = jnp.rot90(block_in, turn_count, axes=(0, 1))
            east_wind = rotated[:, :, 0:L]
            north_wind = rotated[:, :, L:2 * L]
            for repeat in range(turn_count):
                east_wind, north_wind = (-north_wind, east_wind)
            return jnp.concatenate([east_wind, north_wind, rotated[:, :, 2 * L:]], axis=2)
        return apply_turn
    return lax.switch(quarter_turns, [make_turn(0), make_turn(1), make_turn(2), make_turn(3)], field_in)

def advance(padded):
    east_wind = padded[:, :, 0:L]
    north_wind = padded[:, :, L:2 * L]
    face_x = jnp.tile(0.5 * (east_wind[:-1, 1:-1] + east_wind[1:, 1:-1]), (1, 1, V))
    flux_x = jnp.maximum(face_x, 0.0) * padded[:-1, 1:-1] + jnp.minimum(face_x, 0.0) * padded[1:, 1:-1]
    face_y = jnp.tile(0.5 * (north_wind[1:-1, :-1] + north_wind[1:-1, 1:]), (1, 1, V))
    flux_y = jnp.maximum(face_y, 0.0) * padded[1:-1, :-1] + jnp.minimum(face_y, 0.0) * padded[1:-1, 1:]
    return padded[1:-1, 1:-1] - courant * (flux_x[1:] - flux_x[:-1] + (flux_y[:, 1:] - flux_y[:, :-1]))

def forward_rows(rows, weight_in, weight_out):
    inv_rms = lax.rsqrt(lax.optimization_barrier(jnp.mean(rows * rows, axis=1, keepdims=True)) + eps_norm)
    unit_rows = rows * inv_rms
    normed = unit_rows.astype(jnp.bfloat16)
    preact = jnp.dot(normed, weight_in, preferred_element_type=jnp.float32)
    hidden = jax.nn.silu(preact).astype(jnp.bfloat16)
    output = tau_rate * jnp.dot(hidden, weight_out, preferred_element_type=jnp.float32)
    return (output, normed, preact, hidden, inv_rms, unit_rows)

def error_signals(grad_rows, preact, weight_out):
    err_out = (tau_rate * grad_rows).astype(jnp.bfloat16)
    back_prop = jnp.dot(err_out, weight_out.T, preferred_element_type=jnp.float32)
    logistic = jax.nn.sigmoid(preact)
    err_in = (back_prop * logistic * (1.0 + preact * (1.0 - logistic))).astype(jnp.bfloat16)
    return (err_out, err_in)

def backward_rows(grad_rows, saved, weight_in, weight_out):
    normed, preact, hidden, inv_rms, unit_rows = saved
    err_out, err_in = error_signals(grad_rows, preact, weight_out)
    grad_out = jnp.dot(hidden.T, err_out, preferred_element_type=jnp.float32)
    grad_in = jnp.dot(normed.T, err_in, preferred_element_type=jnp.float32)
    d_normed = jnp.dot(err_in, weight_in.T, preferred_element_type=jnp.float32)
    input_grad = inv_rms * (d_normed - unit_rows * lax.optimization_barrier(jnp.mean(d_normed * unit_rows, axis=1, keepdims=True)))
    return (grad_out, grad_in, input_grad)

def column_physics(start_rows, cot_rows, picked, keep_mask, first, weight_in, weight_out):
    h_one, normed, preact, hidden = first
    x_one = start_rows + h_one
    level_two = forward_rows(x_one, weight_in, weight_out)
    x_two = x_one + level_two[0]
    level_three = forward_rows(x_two[picked], weight_in, weight_out)
    weight_col = keep_mask[:, None]
    tendency = h_one + level_two[0] + jnp.zeros_like(h_one).at[picked].add(level_three[0] * weight_col)
    out_three, in_three, back_three = backward_rows(cot_rows[picked] * weight_col, level_three[1:], weight_in, weight_out)
    carried = jnp.zeros_like(start_rows).at[picked].add(back_three * weight_col)
    g_two = cot_rows + carried
    out_two, in_two, back_two = backward_rows(g_two, level_two[1:], weight_in, weight_out)
    g_one = g_two + back_two
    err_out, err_in = error_signals(g_one, preact, weight_out)
    grad_out = out_three + out_two + jnp.dot(hidden.T, err_out, preferred_element_type=jnp.float32)
    grad_in = in_three + in_two + jnp.dot(normed.T, err_in, preferred_element_type=jnp.float32)
    return (tendency, grad_in, grad_out)

def to_tiles(grid):
    cycle_size = XG // SIDE
    band_count = YG // SIDE
    shaped = grid.reshape((cycle_size, SIDE, band_count, SIDE) + grid.shape[2:])
    return jnp.swapaxes(shaped, 1, 2).reshape((cycle_size * band_count, SIDE, SIDE) + grid.shape[2:])

def from_tiles(blocks):
    cycle_size = XG // SIDE
    band_count = YG // SIDE
    shaped = blocks.reshape((cycle_size, band_count, SIDE, SIDE) + blocks.shape[3:])
    return jnp.swapaxes(shaped, 1, 2).reshape((XG, YG) + blocks.shape[3:])

def batch_order(grid):
    cycle_size = XG // SIDE
    band_count = YG // SIDE
    blocks = to_tiles(grid).reshape((cycle_size, band_count, COLS) + grid.shape[2:])
    return jnp.swapaxes(blocks, 0, 1).reshape((band_count * cycle_size, COLS) + grid.shape[2:])

def reference(air_state, cotangent, cost_count, assignment, orientation, weight_in, weight_out):
    quarter_turns = orientation.reshape(-1)
    rotated = lax.map(lambda couple: turn_frame(couple[0], couple[1]), (to_tiles(air_state), quarter_turns))
    band_field = from_tiles(rotated)
    for repeat in range(DSTEPS):
        band_field = advance(jnp.pad(band_field, ((1, 1), (1, 1), (0, 0)), mode='wrap'))
    restored = lax.map(lambda couple: turn_frame(couple[0], (4 - couple[1]) % 4), (to_tiles(band_field), quarter_turns))
    columns = batch_order(from_tiles(restored))
    cot_tiles = batch_order(cotangent)
    cost_tiles = batch_order(cost_count)
    dest_tiles = batch_order(assignment)
    source = jnp.arange(TILES, dtype=jnp.int32)[:, None]
    position = (dest_tiles // PAIR * COLS + source * PAIR + dest_tiles % PAIR).reshape(-1).astype(jnp.int32)
    start_all = jnp.zeros((TILES * COLS, F), jnp.float32).at[position].set(columns.reshape(-1, F))
    cot_all = jnp.zeros((TILES * COLS, F), jnp.float32).at[position].set(cot_tiles.reshape(-1, F))
    cost_all = jnp.zeros((TILES * COLS,), jnp.int32).at[position].set(cost_tiles.reshape(-1))

    def per_batch(totals, pieces):
        start_rows, cot_rows, cost_rows = pieces
        picked = jnp.nonzero(cost_rows == 2, size=K2, fill_value=0)[0].astype(jnp.int32)
        keep_mask = jnp.ones((K2,), jnp.float32)
        first = forward_rows(start_rows, weight_in, weight_out)[:4]
        tendency, grad_in, grad_out = column_physics(start_rows, cot_rows, picked, keep_mask, first, weight_in, weight_out)
        return ((totals[0] + grad_in, totals[1] + grad_out), tendency)
    zero_in = jnp.zeros((F, H), jnp.float32)
    zero_out = jnp.zeros((H, F), jnp.float32)
    totals, tendency = lax.scan(per_batch, (zero_in, zero_out), (start_all.reshape(TILES, COLS, F), cot_all.reshape(TILES, COLS, F), cost_all.reshape(TILES, COLS)))
    return (tendency.reshape(TILES * COLS, F), totals[0].reshape(-1), totals[1].reshape(-1))
```

```python
import functools
import jax
import jax.numpy as jnp
from jax import lax
from jax.experimental import pallas as pl
from jax.experimental.pallas import tpu as pltpu
from jax.sharding import PartitionSpec as P

V = 8
TAU = 0.5
COURANT = 0.1
EPS = 1e-06
LANES = 128
COL = 256
F32 = jnp.float32
BF16 = jnp.bfloat16
SIDE_WINDS = (((0, 1.0), (1, 1.0)), ((1, 1.0), (0, -1.0)), ((0, -1.0), (1, -1.0)), ((1, -1.0), (0, 1.0)))

VMEM = pl.BlockSpec(memory_space=pltpu.VMEM)
SMEM = pl.BlockSpec(memory_space=pltpu.SMEM)


def params(mib):
    return pltpu.CompilerParams(vmem_limit_bytes=mib * 1024 * 1024)


def side_cells(k, n):
    pick = lambda a, b, c, e: jnp.where(k == 0, a, jnp.where(k == 1, b, jnp.where(k == 2, c, e)))
    base = pick(0, (n - 1) * n, n * n - 1, n - 1)
    return base, pick(1, -n, -1, n), pick(n, 1, -n, -1)


def turn_winds(ref, rows, quarter, levels):
    start, size = rows
    width = -(-2 * levels // LANES) * LANES
    w = ref[start : start + size, 0:width]
    lane = lax.broadcasted_iota(jnp.int32, w.shape, 1)
    swapped = jnp.where(lane < levels, pltpu.roll(w, width - levels, 1), pltpu.roll(w, levels, 1))
    cos = ((quarter == 0).astype(F32) - (quarter == 2).astype(F32))
    sin = ((quarter == 1).astype(F32) - (quarter == 3).astype(F32))
    turned = w * cos + swapped * jnp.where(lane < levels, -sin, sin)
    ref[start : start + size, 0:width] = jnp.where(lane < 2 * levels, turned, w)


def copy_rows(dst, dst_base, src, cell, step, count):
    def body(s, carry):
        dst[pl.ds(dst_base + s, 1), :] = src[pl.ds(cell + s * step, 1), :]
        return carry

    lax.fori_loop(0, count, body, 0, unroll=8)


def wind_row(src, a, which, levels):
    start = which * levels
    chunk, off = start // LANES, start % LANES
    first = src[a, :, chunk * LANES : (chunk + 1) * LANES]
    if off == 0:
        return first
    second = src[a, :, (chunk + 1) * LANES : (chunk + 2) * LANES]
    lane = lax.broadcasted_iota(jnp.int32, first.shape, 1)
    shift = LANES - off
    return jnp.where(lane < shift, pltpu.roll(first, shift, 1), pltpu.roll(second, shift, 1))


def repeat_levels(face, levels, chunks):
    lane = lax.broadcasted_iota(jnp.int32, face.shape, 1)
    rolls = {0: face}
    out = []
    for c in range(chunks):
        result, at = None, 0
        while at < LANES:
            index = (c * LANES + at) % levels
            shift = (at - index) % LANES
            if shift not in rolls:
                rolls[shift] = pltpu.roll(face, shift, 1)
            result = rolls[shift] if result is None else jnp.where(lane < at, result, rolls[shift])
            at += levels - index
        out.append(result)
    return out


def transport(src, dst, face_lead, face_sub, lo, hi, winds, levels):
    (lead, lead_sign), (sub, sub_sign) = winds
    size, feats = src.shape[1], src.shape[2]
    chunks = feats // LANES
    period = face_lead.shape[2] // LANES

    def faces(a, carry):
        here, there = wind_row(src, a, lead, levels), wind_row(src, a + 1, lead, levels)
        for c, part in enumerate(repeat_levels((0.5 * lead_sign) * (here + there), levels, period)):
            face_lead[a, :, c * LANES : (c + 1) * LANES] = part
        here = wind_row(src, a, sub, levels)
        ahead = pltpu.roll(here, size - 1, 0)
        for c, part in enumerate(repeat_levels((0.5 * sub_sign) * (here + ahead), levels, period)):
            face_sub[a, :, c * LANES : (c + 1) * LANES] = part
        return carry

    lax.fori_loop(lo - 1, hi, faces, 0)

    def update(a, carry):
        for c3 in range(period):
            lanes3 = slice(c3 * LANES, (c3 + 1) * LANES)
            high, low, side = face_lead[a, :, lanes3], face_lead[a - 1, :, lanes3], face_sub[a, :, lanes3]
            high_p, high_m = jnp.maximum(high, 0.0), jnp.minimum(high, 0.0)
            low_p, low_m = jnp.maximum(low, 0.0), jnp.minimum(low, 0.0)
            side_p, side_m = jnp.maximum(side, 0.0), jnp.minimum(side, 0.0)
            for c in range(c3, chunks, period):
                lanes = slice(c * LANES, (c + 1) * LANES)
                q = src[a, :, lanes]
                flux_high = high_p * q + high_m * src[a + 1, :, lanes]
                flux_low = low_p * src[a - 1, :, lanes] + low_m * q
                flux_side = side_p * q + side_m * pltpu.roll(q, size - 1, 0)
                flux_back = pltpu.roll(flux_side, 1, 0)
                dst[a, :, lanes] = q - COURANT * ((flux_high - flux_low) + (flux_side - flux_back))
        return carry

    lax.fori_loop(lo, hi, update, 0)


def network_forward(x, mask, w_in, w_out, normed, scale, slope, hidden, hsum, rows):
    total = None
    for use in range(3):
        inv = lax.rsqrt(jnp.mean(x * x, axis=1, keepdims=True) + EPS)
        unit = (x * inv).astype(BF16)
        normed[use, rows, :] = unit
        if use > 0:
            scale[use - 1, rows, :] = jnp.broadcast_to(inv, (x.shape[0], LANES))
        p = jnp.dot(unit, w_in, preferred_element_type=F32)
        s = 0.5 + 0.5 * jnp.tanh(0.5 * p)
        silu = p * s
        slope[use, rows, :] = s + silu * (1.0 - s)
        h = silu.astype(BF16)
        hidden[use, rows, :] = h
        if use < 2:
            total = h.astype(F32) if use == 0 else total + h.astype(F32)
            x = x + TAU * jnp.dot(h, w_out, preferred_element_type=F32)
        else:
            hsum[rows, :] = total + h.astype(F32) * mask


def pack_kernel(n, levels, turn, air, s0, s1, s2, s3, c0, c1, c2, c3):
    o = turn[0]
    for k, out in enumerate((s0, s1, s2, s3)):
        base, cm, cd = side_cells((k - o + 4) % 4, n)
        for d in range(2):
            copy_rows(out, d * n, air, base + cd * d + cm * (n - 1), -cm, n)
        turn_winds(out, (0, 2 * n), o, levels)
    c0[...] = s2[n - 1 : n, :]
    c1[...] = s2[0:1, :]
    c2[...] = s0[n - 1 : n, :]
    c3[...] = s0[0:1, :]


def inner_kernel(n, levels, turn, dest, air, air_rows, mask, w_in, w_out,
                 own, mask_rim, normed, scale, slope, hidden, outgoing,
                 q_one, q_two, face_lead, face_sub, hsum):
    o = turn[0]
    winds = ((0, 1.0), (1, 1.0))
    transport(air, q_one, face_lead, face_sub, 1, n - 1, winds, levels)
    transport(q_one, q_two, face_lead, face_sub, 2, n - 2, winds, levels)
    inner = n - 4
    parts = 2
    size = inner // parts * n
    feats = air.shape[2]

    def chunk(part, carry):
        rows = pl.ds(pl.multiple_of(part * size, size), size)
        x = q_two[pl.ds(2 + part * (inner // parts), inner // parts), :, :].reshape(size, feats)
        m = mask[pl.ds(pl.multiple_of(2 * n + part * size, 8), size), 0:1]
        network_forward(x, m, w_in[...], w_out[...], normed, scale, slope, hidden, hsum, rows)
        return carry

    lax.fori_loop(0, parts, chunk, 0)

    def place(i, carry):
        for j in range(2, n - 2):
            outgoing[pl.ds(dest[i * n + j], 1), :] = hsum[pl.ds((i - 2) * n + j, 1), :]
        return carry

    lax.fori_loop(2, n - 2, place, 0)
    for k in range(4):
        base, cm, cd = side_cells((k - o + 4) % 4, n)
        for d in range(4):
            copy_rows(own, (k * 4 + d) * n, air_rows, base + cd * d, cm, n)
        for d in range(2):
            copy_rows(mask_rim, (k * 2 + d) * n, mask, base + cd * d, cm, n)
        turn_winds(own, (k * 4 * n, 4 * n), o, levels)


def rim_kernel(n, levels, turn, dest, h0, h1, h2, h3, c_mm, c_mp, c_pp, c_pm, own, mask_rim, w_in, w_out, before,
               normed, scale, slope, hidden, outgoing,
               wide, wide_one, wide_two, slim, slim_one, slim_two, lead_wide, sub_wide, lead_slim, sub_slim, x_rim, hsum):
    outgoing[...] = before[...]
    o = turn[0]
    halo = (h0, h1, h2, h3)
    for k in range(4):
        ends = k % 2 == 0
        src, one, two = (wide, wide_one, wide_two) if ends else (slim, slim_one, slim_two)
        lead, sub = (lead_wide, sub_wide) if ends else (lead_slim, sub_slim)
        for depth in range(6):
            d = depth - 2
            row = halo[k][(1 - depth) * n : (2 - depth) * n, :] if d < 0 else own[(k * 4 + d) * n : (k * 4 + d + 1) * n, :]
            src[depth, 0:n, :] = row
            if ends:
                src[depth, n + 2 : n + 8, :] = row[0:6, :]
                src[depth, n + 8 : n + 14, :] = row[n - 6 : n, :]
                first, last = (c_mm, c_mp) if k == 0 else (c_pp, c_pm)
                for e in range(2):
                    if d < 0:
                        src[depth, n + 1 - e : n + 2 - e, :] = first[...]
                        src[depth, n + 14 + e : n + 15 + e, :] = last[...]
                    else:
                        at = e * n + n - 1 - d
                        src[depth, n + 1 - e : n + 2 - e, :] = halo[(k + 1) % 4][at : at + 1, :]
                        at = e * n + d
                        src[depth, n + 14 + e : n + 15 + e, :] = halo[(k + 3) % 4][at : at + 1, :]
        transport(src, one, lead, sub, 1, 5, SIDE_WINDS[k], levels)
        transport(one, two, lead, sub, 2, 4, SIDE_WINDS[k], levels)
        for d in range(2):
            at = (k * 2 + d) * n
            x_rim[at : at + n, :] = two[2 + d, 0:n, :]
            if ends:
                x_rim[at : at + 2, :] = two[2 + d, n + 2 : n + 4, :]
                x_rim[at + n - 2 : at + n, :] = two[2 + d, n + 12 : n + 14, :]
    turn_winds(x_rim, (0, 8 * n), (4 - o) % 4, levels)
    network_forward(x_rim[...], mask_rim[:, 0:1], w_in[...], w_out[...], normed, scale, slope, hidden, hsum,
                    slice(0, 8 * n))
    for k in range(4):
        base, cm, cd = side_cells((k - o + 4) % 4, n)
        skip = 2 * (k % 2)
        for d in range(2):
            for m in range(skip, n - skip):
                at = (k * 2 + d) * n + m
                outgoing[pl.ds(dest[base + cd * d + cm * m], 1), :] = hsum[at : at + 1, :]


def contract_rows(a, b):
    return lax.dot_general(a, b, (((0,), (0,)), ((), ())), preferred_element_type=F32)


def contract_last(a, b):
    return lax.dot_general(a, b, (((1,), (1,)), ((), ())), preferred_element_type=F32)


def network_backward(cot, mask, w_in, w_out, normed, scale, slope, err_out, err_in, rows):
    grad = cot * mask
    for use in (2, 1, 0):
        e = (TAU * grad).astype(BF16)
        err_out[use, rows, :] = e
        inner = (contract_last(e, w_out) * slope[use, rows, :]).astype(BF16)
        err_in[use, rows, :] = inner
        if use > 0:
            d = contract_last(inner, w_in)
            unit = normed[use, rows, :].astype(F32)
            d = scale[use - 1, rows, 0:1] * (d - unit * jnp.mean(d * unit, axis=1, keepdims=True))
            grad = (cot if use == 2 else grad) + d


def backward_kernel(n, grid_shape, place, turn, cot, mask, mask_rim, w_in, w_out, n_i, s_i, g_i, h_i, n_r, s_r, g_r, h_r,
                    keep, send, eo_i, ei_i, eo_r, ei_r, cot_rim, grad_in, grad_out):
    o = turn[0]
    inner = n - 4
    parts = 2
    size = inner // parts * n
    for k in range(4):
        base, cm, cd = side_cells((k - o + 4) % 4, n)
        for d in range(2):
            copy_rows(cot_rim, (k * 2 + d) * n, cot, base + cd * d, cm, n)

    def chunk(part, carry):
        rows = pl.ds(pl.multiple_of(part * size, size), size)
        at = pl.ds(pl.multiple_of(2 * n + part * size, 8), size)
        j = lax.broadcasted_iota(jnp.int32, (size, 1), 0) % n
        valid = ((j >= 2) & (j < n - 2)).astype(F32)
        network_backward(cot[at, :] * valid, mask[at, 0:1], w_in[...], w_out[...], n_i, s_i, g_i, eo_i, ei_i, rows)
        return carry

    lax.fori_loop(0, parts, chunk, 0)
    e = lax.broadcasted_iota(jnp.int32, (8 * n, 1), 0)
    m = e % n
    valid = (((e // (2 * n)) % 2 == 0) | ((m >= 2) & (m < n - 2))).astype(F32)
    network_backward(cot_rim[...] * valid, mask_rim[:, 0:1], w_in[...], w_out[...], n_r, s_r, g_r, eo_r, ei_r,
                     slice(0, 8 * n))
    flat = lambda ref: ref[...].reshape(ref.shape[0] * ref.shape[1], ref.shape[2])
    grad_out[...] = contract_rows(flat(h_i), flat(eo_i)) + contract_rows(flat(h_r), flat(eo_r))
    grad_in[...] = contract_rows(flat(n_i), flat(ei_i)) + contract_rows(flat(n_r), flat(ei_r))
    groups, tiles = grid_shape
    count = groups * tiles
    feats, units = grad_in.shape
    rows_in, rows_out = feats // count, units // count
    for g in range(groups):
        for t in range(tiles):
            p = g * tiles + t
            rg, rt = place[0] ^ g, place[1] ^ t
            at = ((rg // 2) * 2 + rt % 2) * (tiles // 2) + rt // 2
            pieces = []
            for c in range(units // COL):
                pieces.append(grad_in[p * rows_in : (p + 1) * rows_in, c * COL : (c + 1) * COL])
            for c in range(feats // COL):
                pieces.append(grad_out[p * rows_out : (p + 1) * rows_out, c * COL : (c + 1) * COL])

            def store(ref, pieces=pieces, at=at):
                row = 0
                for piece in pieces:
                    ref[at, row : row + piece.shape[0], :] = piece
                    row += piece.shape[0]

            pl.when(rg % 2 == 0)(functools.partial(store, keep))
            pl.when(rg % 2 == 1)(functools.partial(store, send))


def output_kernel(rows, w_out, out):
    x = rows[...]
    high = x.astype(BF16)
    low = (x - high.astype(F32)).astype(BF16)
    w = w_out[...]
    out[...] = TAU * (jnp.dot(high, w, preferred_element_type=F32) + jnp.dot(low, w, preferred_element_type=F32))


def shift_perm(count, by):
    return [(i, (i + by) % count) for i in range(count)]


def joint_perm(groups, tiles, move):
    return [(g * tiles + t, (lambda h: h[0] * tiles + h[1])(move(g, t))) for g in range(groups) for t in range(tiles)]


def per_device(air_state, cotangent, cost_count, assignment, orientation, weight_in, weight_out):
    groups, tiles = lax.axis_size("grp"), lax.axis_size("tile")
    count = groups * tiles
    n, feats = air_state.shape[0], air_state.shape[2]
    units = weight_in.shape[1]
    levels = feats // V
    cells, rim, inner = n * n, 8 * n, (n - 4) * n
    period = next(c for c in range(1, feats // LANES + 1) if c * LANES % levels == 0)
    shape = jax.ShapeDtypeStruct

    turn = orientation.reshape(1)
    dest = assignment.reshape(cells)
    air_rows = air_state.reshape(cells, feats)
    cot_rows = cotangent.reshape(cells, feats)
    mask = jnp.broadcast_to((cost_count.reshape(cells, 1) == 2).astype(F32), (cells, LANES))

    strips = pl.pallas_call(
        functools.partial(pack_kernel, n, levels),
        out_shape=[shape((2 * n, feats), F32)] * 4 + [shape((1, feats), F32)] * 4,
        in_specs=[SMEM, VMEM],
        out_specs=[VMEM] * 8,
        compiler_params=params(32),
        name="pack_strips",
    )(turn, air_rows)

    both = ("grp", "tile")
    halo = [
        lax.ppermute(strips[2], "tile", shift_perm(tiles, 1)),
        lax.ppermute(strips[3], "grp", shift_perm(groups, 1)),
        lax.ppermute(strips[0], "tile", shift_perm(tiles, -1)),
        lax.ppermute(strips[1], "grp", shift_perm(groups, -1)),
    ]
    corners = [
        lax.ppermute(strips[4 + i], both, joint_perm(groups, tiles, lambda g, t: ((g + dg) % groups, (t + dt) % tiles)))
        for i, (dt, dg) in enumerate(((1, 1), (1, -1), (-1, -1), (-1, 1)))
    ]

    def state(rows):
        return [
            shape((3, rows, feats), BF16),
            shape((2, rows, LANES), F32),
            shape((3, rows, units), F32),
            shape((3, rows, units), BF16),
        ]

    flops = 10 * inner * feats * units
    own, mask_rim, *saved_inner, outgoing = pl.pallas_call(
        functools.partial(inner_kernel, n, levels),
        out_shape=[shape((16 * n, feats), F32), shape((rim, LANES), F32), *state(inner), shape((cells, units), F32)],
        in_specs=[SMEM, SMEM] + [VMEM] * 5,
        out_specs=[VMEM] * 7,
        scratch_shapes=[
            pltpu.VMEM((n, n, feats), F32),
            pltpu.VMEM((n, n, feats), F32),
            pltpu.VMEM((n, n, period * LANES), F32),
            pltpu.VMEM((n, n, period * LANES), F32),
            pltpu.VMEM((inner, units), F32),
        ],
        compiler_params=params(56),
        cost_estimate=pl.CostEstimate(flops=flops * 2, bytes_accessed=40 << 20, transcendentals=0),
        name="inner_columns",
    )(turn, dest, air_state, air_rows, mask, weight_in, weight_out)

    wide, slim = n + 16, n
    *saved_rim, outgoing = pl.pallas_call(
        functools.partial(rim_kernel, n, levels),
        out_shape=[*state(rim), shape((cells, units), F32)],
        in_specs=[SMEM, SMEM] + [VMEM] * 13,
        out_specs=[VMEM] * 5,
        scratch_shapes=[pltpu.VMEM((6, wide, feats), F32)] * 3
        + [pltpu.VMEM((6, slim, feats), F32)] * 3
        + [pltpu.VMEM((6, wide, period * LANES), F32)] * 2
        + [pltpu.VMEM((6, slim, period * LANES), F32)] * 2
        + [pltpu.VMEM((rim, feats), F32), pltpu.VMEM((rim, units), F32)],
        compiler_params=params(48),
        cost_estimate=pl.CostEstimate(flops=10 * rim * feats * units, bytes_accessed=20 << 20, transcendentals=0),
        name="rim_columns",
    )(turn, dest, *halo, *corners, own, mask_rim, weight_in, weight_out, outgoing)

    arrived = lax.all_to_all(
        outgoing.reshape(count, cells // count, units), both, split_axis=0, concat_axis=0, tiled=True
    ).reshape(cells, units)

    place = jnp.stack([lax.axis_index("grp"), lax.axis_index("tile")]).astype(jnp.int32)
    rows_in, rows_out = feats // count, units // count
    piece = rows_in * (units // COL) + rows_out * (feats // COL)
    keep, send = pl.pallas_call(
        functools.partial(backward_kernel, n, (groups, tiles)),
        out_shape=[shape((count // 2, piece, COL), F32)] * 2,
        in_specs=[SMEM, SMEM] + [VMEM] * 13,
        out_specs=[VMEM] * 2,
        scratch_shapes=[
            pltpu.VMEM((3, inner, feats), BF16),
            pltpu.VMEM((3, inner, units), BF16),
            pltpu.VMEM((3, rim, feats), BF16),
            pltpu.VMEM((3, rim, units), BF16),
            pltpu.VMEM((rim, feats), F32),
            pltpu.VMEM((feats, units), F32),
            pltpu.VMEM((units, feats), F32),
        ],
        compiler_params=params(60),
        cost_estimate=pl.CostEstimate(flops=22 * cells * feats * units, bytes_accessed=40 << 20, transcendentals=0),
        name="columns_backward",
    )(place, turn, cot_rows, mask, mask_rim, weight_in, weight_out, *saved_inner, *saved_rim)

    sums = keep + lax.ppermute(send, "grp", [(i, i ^ 1) for i in range(groups)])
    sums = sums.reshape(groups // 2, 2, tiles // 2, piece, COL)
    total = sums[0, 0]
    for x in range(groups // 2):
        for y in range(2):
            if x or y:
                total = total + lax.ppermute(
                    sums[x, y], both, joint_perm(groups, tiles, lambda g, t: (g ^ (2 * x), t ^ y))
                )
    mine = total[0]
    for z in range(1, tiles // 2):
        mine = mine + lax.ppermute(total[z], "tile", [(t, t ^ (2 * z)) for t in range(tiles)])
    split = rows_in * (units // COL)
    flat = lambda part, rows: part.reshape(-1, rows, COL).transpose(1, 0, 2).reshape(-1)
    summed_in, summed_out = flat(mine[:split], rows_in), flat(mine[split:], rows_out)

    block = cells // 4
    tendency = pl.pallas_call(
        output_kernel,
        out_shape=shape((cells, feats), F32),
        grid=(cells // block,),
        in_specs=[pl.BlockSpec((block, units), lambda i: (i, 0)), pl.BlockSpec((units, feats), lambda i: (0, 0))],
        out_specs=pl.BlockSpec((block, feats), lambda i: (i, 0)),
        compiler_params=params(32),
        cost_estimate=pl.CostEstimate(flops=4 * cells * feats * units, bytes_accessed=6 << 20, transcendentals=0),
        name="tendency_rows",
    )(arrived, weight_out)
    return (tendency, summed_in, summed_out)


def solution(mesh):
    in_specs = (
        P("tile", "grp", None),
        P("tile", "grp", None),
        P("tile", "grp"),
        P("tile", "grp"),
        P("tile", "grp"),
        P(),
        P(),
    )
    out_specs = (P(("grp", "tile"), None), P(("grp", "tile")), P(("grp", "tile")))
    return jax.shard_map(
        per_device, mesh=mesh, in_specs=in_specs, out_specs=out_specs, check_vma=False
    )
```

```python
import functools
import jax
import jax.numpy as jnp
from jax import lax
from jax.experimental import pallas as pl
from jax.experimental.pallas import tpu as pltpu
from jax.sharding import PartitionSpec as P

V = 8
TAU = 0.5
COURANT = 0.1
EPS = 1e-06
LANES = 128
COL = 256
F32 = jnp.float32
BF16 = jnp.bfloat16
SIDE_WINDS = (((0, 1.0), (1, 1.0)), ((1, 1.0), (0, -1.0)), ((0, -1.0), (1, -1.0)), ((1, -1.0), (0, 1.0)))

VMEM = pl.BlockSpec(memory_space=pltpu.VMEM)
SMEM = pl.BlockSpec(memory_space=pltpu.SMEM)


def params(mib):
    return pltpu.CompilerParams(vmem_limit_bytes=mib * 1024 * 1024)


def side_cells(k, n):
    pick = lambda a, b, c, e: jnp.where(k == 0, a, jnp.where(k == 1, b, jnp.where(k == 2, c, e)))
    return (pick(0, n - 1, n - 1, 0), pick(1, 0, -1, 0), pick(0, -1, 0, 1)), (
        pick(0, 0, n - 1, n - 1), pick(0, 1, 0, -1), pick(1, 0, -1, 0))


def side_rows(k, n):
    (bi, di, mi), (bj, dj, mj) = side_cells(k, n)
    return bi * n + bj, mi * n + mj, di * n + dj


def turn_winds(ref, rows, quarter, levels):
    start, size = rows
    width = -(-2 * levels // LANES) * LANES
    w = ref[start : start + size, 0:width]
    lane = lax.broadcasted_iota(jnp.int32, w.shape, 1)
    swapped = jnp.where(lane < levels, pltpu.roll(w, width - levels, 1), pltpu.roll(w, levels, 1))
    cos = ((quarter == 0).astype(F32) - (quarter == 2).astype(F32))
    sin = ((quarter == 1).astype(F32) - (quarter == 3).astype(F32))
    turned = w * cos + swapped * jnp.where(lane < levels, -sin, sin)
    ref[start : start + size, 0:width] = jnp.where(lane < 2 * levels, turned, w)


def copy_rows(dst, dst_base, src, cell, step, count):
    def body(s, carry):
        dst[pl.ds(dst_base + s, 1), :] = src[pl.ds(cell + s * step, 1), :]
        return carry

    lax.fori_loop(0, count, body, 0, unroll=8)


def wind_row(src, a, which, levels):
    start = which * levels
    chunk, off = start // LANES, start % LANES
    first = src[a, :, chunk * LANES : (chunk + 1) * LANES]
    if off == 0:
        return first
    second = src[a, :, (chunk + 1) * LANES : (chunk + 2) * LANES]
    lane = lax.broadcasted_iota(jnp.int32, first.shape, 1)
    shift = LANES - off
    return jnp.where(lane < shift, pltpu.roll(first, shift, 1), pltpu.roll(second, shift, 1))


def repeat_levels(face, levels, chunks):
    lane = lax.broadcasted_iota(jnp.int32, face.shape, 1)
    rolls = {0: face}
    out = []
    for c in range(chunks):
        result, at = None, 0
        while at < LANES:
            index = (c * LANES + at) % levels
            shift = (at - index) % LANES
            if shift not in rolls:
                rolls[shift] = pltpu.roll(face, shift, 1)
            result = rolls[shift] if result is None else jnp.where(lane < at, result, rolls[shift])
            at += levels - index
        out.append(result)
    return out


def transport(src, dst, face_lead, face_sub, lo, hi, winds, levels):
    (lead, lead_sign), (sub, sub_sign) = winds
    size, feats = src.shape[1], src.shape[2]
    chunks = feats // LANES
    period = face_lead.shape[2] // LANES
    block = next(b for b in range(face_sub.shape[0], 0, -1) if (hi - lo) % b == 0)

    def store(ref, at, face):
        for c, part in enumerate(repeat_levels(face, levels, period)):
            ref[at, :, c * LANES : (c + 1) * LANES] = part

    def body(b, carry):
        first = lo + b * block
        for r in range(block + 1):
            wind = wind_row(src, first - 1 + r, lead, levels) + wind_row(src, first + r, lead, levels)
            store(face_lead, r, (0.5 * COURANT * lead_sign) * wind)
        for r in range(block):
            wind = wind_row(src, first + r, sub, levels)
            store(face_sub, r, (0.5 * COURANT * sub_sign) * (wind + pltpu.roll(wind, size - 1, 0)))
        for c3 in range(period):
            lanes3 = slice(c3 * LANES, (c3 + 1) * LANES)
            group = [slice(c * LANES, (c + 1) * LANES) for c in range(c3, chunks, period)]
            face = face_lead[0, :, lanes3]
            q = [src[first, :, lanes] for lanes in group]
            before = [face * jnp.where(face > 0.0, src[first - 1, :, lanes], here) for lanes, here in zip(group, q)]
            for r in range(block):
                face, side = face_lead[r + 1, :, lanes3], face_sub[r, :, lanes3]
                for i, lanes in enumerate(group):
                    ahead = src[first + r + 1, :, lanes]
                    flux = face * jnp.where(face > 0.0, q[i], ahead)
                    cross = side * jnp.where(side > 0.0, q[i], pltpu.roll(q[i], size - 1, 0))
                    dst[first + r, :, lanes] = q[i] - ((flux - before[i]) + (cross - pltpu.roll(cross, 1, 0)))
                    q[i], before[i] = ahead, flux
        return carry

    lax.fori_loop(0, (hi - lo) // block, body, 0)


def network_forward(x, mask, w_in, w_out, normed, scale, slope, hidden, hsum, rows):
    total = None
    for use in range(3):
        inv = lax.rsqrt(jnp.mean(x * x, axis=1, keepdims=True) + EPS)
        unit = (x * inv).astype(BF16)
        normed[use, rows, :] = unit
        if use > 0:
            scale[use - 1, rows, :] = jnp.broadcast_to(inv, (x.shape[0], LANES))
        p = jnp.dot(unit, w_in, preferred_element_type=F32)
        s = 0.5 + 0.5 * jnp.tanh(0.5 * p)
        silu = p * s
        slope[use, rows, :] = s + silu * (1.0 - s)
        h = silu.astype(BF16)
        hidden[use, rows, :] = h
        if use < 2:
            total = h.astype(F32) if use == 0 else total + h.astype(F32)
            x = x + TAU * jnp.dot(h, w_out, preferred_element_type=F32)
        else:
            hsum[rows, :] = total + h.astype(F32) * mask


def pack_strip(n, levels, k, o, air, out):
    base, cm, cd = side_rows((k - o + 4) % 4, n)
    for d in range(2):
        copy_rows(out, d * n, air, base + cd * d + cm * (n - 1), -cm, n)
    turn_winds(out, (0, 2 * n), o, levels)


def pack_kernel(n, levels, turn, air, s1, s3):
    pack_strip(n, levels, 1, turn[0, 0], air, s1)
    pack_strip(n, levels, 3, turn[0, 0], air, s3)


def pack_with_corners_kernel(n, levels, turn, air, h1, h3, order, s0, s2):
    del order
    pack_strip(n, levels, 0, turn[0, 0], air, s0)
    pack_strip(n, levels, 2, turn[0, 0], air, s2)
    s0[2 * n : 2 * n + 1, :] = h1[n - 1 : n, :]
    s0[2 * n + 1 : 2 * n + 2, :] = h3[0:1, :]
    s2[2 * n : 2 * n + 1, :] = h1[0:1, :]
    s2[2 * n + 1 : 2 * n + 2, :] = h3[n - 1 : n, :]


def inner_transport_kernel(n, levels, turn, cost, air_rows, moved, own, mask, mask_rim, q_one, face_lead, face_sub):
    o = turn[0, 0]
    air = air_rows.reshape(n, n, air_rows.shape[1])
    winds = ((0, 1.0), (1, 1.0))
    transport(air, q_one, face_lead, face_sub, 1, n - 1, winds, levels)
    transport(q_one, moved, face_lead, face_sub, 2, n - 2, winds, levels)
    diagonal = lax.broadcasted_iota(jnp.int32, (n, n), 0) == lax.broadcasted_iota(jnp.int32, (n, n), 1)

    def mask_row(i, carry):
        two = jnp.broadcast_to((cost[pl.ds(i, 1), :] == 2).astype(F32), (n, n))
        column = jnp.sum(jnp.where(diagonal, two, 0.0), axis=1, keepdims=True)
        mask[pl.ds(pl.multiple_of(i * n, 8), n), :] = jnp.broadcast_to(column, (n, LANES))
        return carry

    lax.fori_loop(0, n, mask_row, 0, unroll=8)
    for k in range(4):
        base, cm, cd = side_rows((k - o + 4) % 4, n)
        for d in range(4):
            copy_rows(own, (k * 4 + d) * n, air_rows, base + cd * d, cm, n)
        for d in range(2):
            copy_rows(mask_rim, (k * 2 + d) * n, mask, base + cd * d, cm, n)
        turn_winds(own, (k * 4 * n, 4 * n), o, levels)


def inner_network_kernel(n, dest, moved, mask, w_in, w_out, normed, scale, slope, hidden, outgoing, hsum):
    inner = n - 4
    parts = 2
    size = inner // parts * n
    feats = moved.shape[2]

    def chunk(part, carry):
        rows = pl.ds(pl.multiple_of(part * size, size), size)
        x = moved[pl.ds(2 + part * (inner // parts), inner // parts), :, :].reshape(size, feats)
        m = mask[pl.ds(pl.multiple_of(2 * n + part * size, 8), size), 0:1]
        network_forward(x, m, w_in[...], w_out[...], normed, scale, slope, hidden, hsum, rows)
        return carry

    lax.fori_loop(0, parts, chunk, 0)

    def place(i, carry):
        for j in range(2, n - 2):
            outgoing[pl.ds(dest[i, j], 1), :] = hsum[pl.ds((i - 2) * n + j, 1), :]
        return carry

    lax.fori_loop(2, n - 2, place, 0)


def rim_kernel(n, levels, turn, dest, h0, h1, h2, h3, own, mask_rim, w_in, w_out, before,
               normed, scale, slope, hidden, outgoing,
               wide, wide_one, wide_two, slim, slim_one, slim_two, lead_wide, sub_wide, lead_slim, sub_slim, x_rim, hsum):
    outgoing[...] = before[...]
    o = turn[0, 0]
    halo = (h0, h1, h2, h3)
    for k in range(4):
        ends = k % 2 == 0
        src, one, two = (wide, wide_one, wide_two) if ends else (slim, slim_one, slim_two)
        lead, sub = (lead_wide, sub_wide) if ends else (lead_slim, sub_slim)
        for depth in range(6):
            d = depth - 2
            row = halo[k][(1 - depth) * n : (2 - depth) * n, :] if d < 0 else own[(k * 4 + d) * n : (k * 4 + d + 1) * n, :]
            src[depth, 0:n, :] = row
            if ends:
                src[depth, n + 2 : n + 8, :] = row[0:6, :]
                src[depth, n + 8 : n + 14, :] = row[n - 6 : n, :]
                for e in range(2):
                    if d < 0:
                        at = 2 * n + k // 2
                        src[depth, n + 1 - e : n + 2 - e, :] = halo[k][at : at + 1, :]
                        at = 2 * n + 1 - k // 2
                        src[depth, n + 14 + e : n + 15 + e, :] = halo[k][at : at + 1, :]
                    else:
                        at = e * n + n - 1 - d
                        src[depth, n + 1 - e : n + 2 - e, :] = halo[(k + 1) % 4][at : at + 1, :]
                        at = e * n + d
                        src[depth, n + 14 + e : n + 15 + e, :] = halo[(k + 3) % 4][at : at + 1, :]
        transport(src, one, lead, sub, 1, 5, SIDE_WINDS[k], levels)
        transport(one, two, lead, sub, 2, 4, SIDE_WINDS[k], levels)
        for d in range(2):
            at = (k * 2 + d) * n
            x_rim[at : at + n, :] = two[2 + d, 0:n, :]
            if ends:
                x_rim[at : at + 2, :] = two[2 + d, n + 2 : n + 4, :]
                x_rim[at + n - 2 : at + n, :] = two[2 + d, n + 12 : n + 14, :]
    turn_winds(x_rim, (0, 8 * n), (4 - o) % 4, levels)
    network_forward(x_rim[...], mask_rim[:, 0:1], w_in[...], w_out[...], normed, scale, slope, hidden, hsum,
                    slice(0, 8 * n))
    for k in range(4):
        (bi, di, mi), (bj, dj, mj) = side_cells((k - o + 4) % 4, n)
        skip = 2 * (k % 2)
        for d in range(2):
            for m in range(skip, n - skip):
                at = (k * 2 + d) * n + m
                row = dest[bi + di * d + mi * m, bj + dj * d + mj * m]
                outgoing[pl.ds(row, 1), :] = hsum[at : at + 1, :]


def contract_rows(a, b):
    return lax.dot_general(a, b, (((0,), (0,)), ((), ())), preferred_element_type=F32)


def contract_last(a, b):
    return lax.dot_general(a, b, (((1,), (1,)), ((), ())), preferred_element_type=F32)


def network_backward(cot, mask, w_in, w_out, normed, scale, slope, err_out, err_in, rows):
    grad = cot * mask
    for use in (2, 1, 0):
        e = (TAU * grad).astype(BF16)
        err_out[use, rows, :] = e
        inner = (contract_last(e, w_out) * slope[use, rows, :]).astype(BF16)
        err_in[use, rows, :] = inner
        if use > 0:
            d = contract_last(inner, w_in)
            unit = normed[use, rows, :].astype(F32)
            d = scale[use - 1, rows, 0:1] * (d - unit * jnp.mean(d * unit, axis=1, keepdims=True))
            grad = (cot if use == 2 else grad) + d


def backward_kernel(n, grid_shape, place, turn, cot, mask, mask_rim, w_in, w_out, n_i, s_i, g_i, h_i, n_r, s_r, g_r, h_r,
                    keep, send, eo_i, ei_i, eo_r, ei_r, cot_rim, grad_in, grad_out):
    o = turn[0, 0]
    inner = n - 4
    parts = 2
    size = inner // parts * n
    for k in range(4):
        base, cm, cd = side_rows((k - o + 4) % 4, n)
        for d in range(2):
            copy_rows(cot_rim, (k * 2 + d) * n, cot, base + cd * d, cm, n)

    def chunk(part, carry):
        rows = pl.ds(pl.multiple_of(part * size, size), size)
        at = pl.ds(pl.multiple_of(2 * n + part * size, 8), size)
        j = lax.broadcasted_iota(jnp.int32, (size, 1), 0) % n
        valid = ((j >= 2) & (j < n - 2)).astype(F32)
        network_backward(cot[at, :] * valid, mask[at, 0:1], w_in[...], w_out[...], n_i, s_i, g_i, eo_i, ei_i, rows)
        return carry

    lax.fori_loop(0, parts, chunk, 0)
    e = lax.broadcasted_iota(jnp.int32, (8 * n, 1), 0)
    m = e % n
    valid = (((e // (2 * n)) % 2 == 0) | ((m >= 2) & (m < n - 2))).astype(F32)
    network_backward(cot_rim[...] * valid, mask_rim[:, 0:1], w_in[...], w_out[...], n_r, s_r, g_r, eo_r, ei_r,
                     slice(0, 8 * n))
    flat = lambda ref: ref[...].reshape(ref.shape[0] * ref.shape[1], ref.shape[2])
    grad_out[...] = contract_rows(flat(h_i), flat(eo_i)) + contract_rows(flat(h_r), flat(eo_r))
    grad_in[...] = contract_rows(flat(n_i), flat(ei_i)) + contract_rows(flat(n_r), flat(ei_r))
    groups, tiles = grid_shape
    count = groups * tiles
    feats, units = grad_in.shape
    rows_in, rows_out = feats // count, units // count
    for g in range(groups):
        for t in range(tiles):
            p = g * tiles + t
            rg, rt = place[0] ^ g, place[1] ^ t
            at = ((rg // 2) * 2 + rt % 2) * (tiles // 2) + rt // 2
            pieces = []
            for c in range(units // COL):
                pieces.append(grad_in[p * rows_in : (p + 1) * rows_in, c * COL : (c + 1) * COL])
            for c in range(feats // COL):
                pieces.append(grad_out[p * rows_out : (p + 1) * rows_out, c * COL : (c + 1) * COL])

            def store(ref, pieces=pieces, at=at):
                row = 0
                for piece in pieces:
                    ref[at, row : row + piece.shape[0], :] = piece
                    row += piece.shape[0]

            pl.when(rg % 2 == 0)(functools.partial(store, keep))
            pl.when(rg % 2 == 1)(functools.partial(store, send))


def output_kernel(rows, w_out, out):
    x = rows[...]
    high = x.astype(BF16)
    low = (x - high.astype(F32)).astype(BF16)
    w = w_out[...]
    out[...] = TAU * (jnp.dot(high, w, preferred_element_type=F32) + jnp.dot(low, w, preferred_element_type=F32))


def shift_perm(count, by):
    return [(i, (i + by) % count) for i in range(count)]


def joint_perm(groups, tiles, move):
    return [(g * tiles + t, (lambda h: h[0] * tiles + h[1])(move(g, t))) for g in range(groups) for t in range(tiles)]


def per_device(air_state, cotangent, cost_count, assignment, orientation, weight_in, weight_out):
    groups, tiles = lax.axis_size("grp"), lax.axis_size("tile")
    count = groups * tiles
    n, feats = air_state.shape[0], air_state.shape[2]
    units = weight_in.shape[1]
    levels = feats // V
    cells, rim, inner = n * n, 8 * n, (n - 4) * n
    period = next(c for c in range(1, feats // LANES + 1) if c * LANES % levels == 0)
    shape = jax.ShapeDtypeStruct

    air_rows = air_state.reshape(cells, feats)
    cot_rows = cotangent.reshape(cells, feats)
    both = ("grp", "tile")

    def state(rows):
        return [
            pltpu.VMEM((3, rows, feats), BF16),
            pltpu.VMEM((2, rows, LANES), F32),
            pltpu.VMEM((3, rows, units), F32),
            pltpu.VMEM((3, rows, units), BF16),
        ]

    strips = pl.pallas_call(
        functools.partial(pack_kernel, n, levels),
        out_shape=[shape((2 * n, feats), F32)] * 2,
        in_specs=[SMEM, VMEM],
        out_specs=[VMEM] * 2,
        compiler_params=params(8),
        name="pack_strips",
    )(orientation, air_rows)
    from_left = lax.ppermute(strips[1], "grp", shift_perm(groups, 1))
    from_right = lax.ppermute(strips[0], "grp", shift_perm(groups, -1))

    moved, own, mask, mask_rim = pl.pallas_call(
        functools.partial(inner_transport_kernel, n, levels),
        out_shape=[
            pltpu.VMEM((n, n, feats), F32),
            pltpu.VMEM((16 * n, feats), F32),
            pltpu.VMEM((cells, LANES), F32),
            pltpu.VMEM((rim, LANES), F32),
        ],
        in_specs=[SMEM] + [VMEM] * 2,
        out_specs=[VMEM] * 4,
        scratch_shapes=[
            pltpu.VMEM((n, n, feats), F32),
            pltpu.VMEM((8, n, period * LANES), F32),
            pltpu.VMEM((7, n, period * LANES), F32),
        ],
        compiler_params=params(20),
        cost_estimate=pl.CostEstimate(flops=60 * cells * feats, bytes_accessed=16 << 20, transcendentals=0),
        name="inner_transport",
    )(orientation, cost_count, air_rows)

    strips = pl.pallas_call(
        functools.partial(pack_with_corners_kernel, n, levels),
        out_shape=[shape((2 * n + 8, feats), F32)] * 2,
        in_specs=[SMEM] + [VMEM] * 4,
        out_specs=[VMEM] * 2,
        compiler_params=params(8),
        name="pack_strips_corners",
    )(orientation, air_rows, from_left, from_right, mask_rim)
    from_above = lax.ppermute(strips[1], "tile", shift_perm(tiles, 1))
    from_below = lax.ppermute(strips[0], "tile", shift_perm(tiles, -1))

    *saved_inner, outgoing = pl.pallas_call(
        functools.partial(inner_network_kernel, n),
        out_shape=[*state(inner), pltpu.VMEM((cells, units), F32)],
        in_specs=[SMEM] + [VMEM] * 4,
        out_specs=[VMEM] * 5,
        scratch_shapes=[pltpu.VMEM((inner, units), F32)],
        compiler_params=params(16),
        cost_estimate=pl.CostEstimate(
            flops=10 * inner * feats * units, bytes_accessed=16 << 20, transcendentals=3 * inner * units
        ),
        name="inner_network",
    )(assignment, moved, mask, weight_in, weight_out)

    wide, slim = n + 16, n
    *saved_rim, outgoing = pl.pallas_call(
        functools.partial(rim_kernel, n, levels),
        out_shape=[*state(rim), shape((cells, units), F32)],
        in_specs=[SMEM, SMEM] + [VMEM] * 9,
        out_specs=[VMEM] * 5,
        scratch_shapes=[pltpu.VMEM((6, wide, feats), F32)] * 3
        + [pltpu.VMEM((6, slim, feats), F32)] * 3
        + [pltpu.VMEM((5, wide, period * LANES), F32), pltpu.VMEM((4, wide, period * LANES), F32)]
        + [pltpu.VMEM((5, slim, period * LANES), F32), pltpu.VMEM((4, slim, period * LANES), F32)]
        + [pltpu.VMEM((rim, feats), F32), pltpu.VMEM((rim, units), F32)],
        compiler_params=params(16),
        cost_estimate=pl.CostEstimate(
            flops=10 * rim * feats * units, bytes_accessed=20 << 20, transcendentals=3 * rim * units
        ),
        name="rim_columns",
    )(orientation, assignment, from_above, from_left, from_below, from_right, own, mask_rim, weight_in, weight_out, outgoing)

    arrived = lax.all_to_all(
        outgoing.reshape(count, cells // count, units), both, split_axis=0, concat_axis=0, tiled=True
    ).reshape(cells, units)

    place = jnp.stack([lax.axis_index("grp"), lax.axis_index("tile")]).astype(jnp.int32)
    rows_in, rows_out = feats // count, units // count
    piece = rows_in * (units // COL) + rows_out * (feats // COL)
    keep, send = pl.pallas_call(
        functools.partial(backward_kernel, n, (groups, tiles)),
        out_shape=[shape((count // 2, piece, COL), F32)] * 2,
        in_specs=[SMEM, SMEM] + [VMEM] * 13,
        out_specs=[VMEM] * 2,
        scratch_shapes=[
            pltpu.VMEM((3, inner, feats), BF16),
            pltpu.VMEM((3, inner, units), BF16),
            pltpu.VMEM((3, rim, feats), BF16),
            pltpu.VMEM((3, rim, units), BF16),
            pltpu.VMEM((rim, feats), F32),
            pltpu.VMEM((feats, units), F32),
            pltpu.VMEM((units, feats), F32),
        ],
        compiler_params=params(36),
        cost_estimate=pl.CostEstimate(flops=22 * cells * feats * units, bytes_accessed=40 << 20, transcendentals=0),
        name="columns_backward",
    )(place, orientation, cot_rows, mask, mask_rim, weight_in, weight_out, *saved_inner, *saved_rim)

    sums = keep + lax.ppermute(send, "grp", [(i, i ^ 1) for i in range(groups)])
    sums = sums.reshape(groups // 2, 2, tiles // 2, piece, COL)
    total = sums[0, 0]
    for x in range(groups // 2):
        for y in range(2):
            if x or y:
                total = total + lax.ppermute(
                    sums[x, y], both, joint_perm(groups, tiles, lambda g, t: (g ^ (2 * x), t ^ y))
                )
    mine = total[0]
    for z in range(1, tiles // 2):
        mine = mine + lax.ppermute(total[z], "tile", [(t, t ^ (2 * z)) for t in range(tiles)])
    split = rows_in * (units // COL)
    flat = lambda part, rows: part.reshape(-1, rows, COL).transpose(1, 0, 2).reshape(-1)
    summed_in, summed_out = flat(mine[:split], rows_in), flat(mine[split:], rows_out)

    block = cells // 4
    tendency = pl.pallas_call(
        output_kernel,
        out_shape=shape((cells, feats), F32),
        grid=(cells // block,),
        in_specs=[pl.BlockSpec((block, units), lambda i: (i, 0)), pl.BlockSpec((units, feats), lambda i: (0, 0))],
        out_specs=pl.BlockSpec((block, feats), lambda i: (i, 0)),
        compiler_params=params(32),
        cost_estimate=pl.CostEstimate(flops=4 * cells * feats * units, bytes_accessed=6 << 20, transcendentals=0),
        name="tendency_rows",
    )(arrived, weight_out)
    return (tendency, summed_in, summed_out)


def solution(mesh):
    in_specs = (
        P("tile", "grp", None),
        P("tile", "grp", None),
        P("tile", "grp"),
        P("tile", "grp"),
        P("tile", "grp"),
        P(),
        P(),
    )
    out_specs = (P(("grp", "tile"), None), P(("grp", "tile")), P(("grp", "tile")))
    return jax.shard_map(
        per_device, mesh=mesh, in_specs=in_specs, out_specs=out_specs, check_vma=False
    )
```

```python
import functools
import jax
import jax.numpy as jnp
from jax import lax
from jax.experimental import pallas as pl
from jax.experimental.pallas import tpu as pltpu
from jax.sharding import PartitionSpec as P

V = 8
TAU = 0.5
COURANT = 0.1
EPS = 1e-06
LANES = 128
COL = 256
F32 = jnp.float32
BF16 = jnp.bfloat16
SIDE_WINDS = (((0, 1.0), (1, 1.0)), ((1, 1.0), (0, -1.0)), ((0, -1.0), (1, -1.0)), ((1, -1.0), (0, 1.0)))

VMEM = pl.BlockSpec(memory_space=pltpu.VMEM)
HBM = pl.BlockSpec(memory_space=pltpu.HBM)
SMEM = pl.BlockSpec(memory_space=pltpu.SMEM)


def params(mib):
    return pltpu.CompilerParams(vmem_limit_bytes=mib * 1024 * 1024)


def side_cells(k, n):
    pick = lambda a, b, c, e: jnp.where(k == 0, a, jnp.where(k == 1, b, jnp.where(k == 2, c, e)))
    return (pick(0, n - 1, n - 1, 0), pick(1, 0, -1, 0), pick(0, -1, 0, 1)), (
        pick(0, 0, n - 1, n - 1), pick(0, 1, 0, -1), pick(1, 0, -1, 0))


def side_rows(k, n):
    (bi, di, mi), (bj, dj, mj) = side_cells(k, n)
    return bi * n + bj, mi * n + mj, di * n + dj


def turn_winds(ref, rows, quarter, levels):
    start, size = rows
    width = -(-2 * levels // LANES) * LANES
    w = ref[start : start + size, 0:width]
    lane = lax.broadcasted_iota(jnp.int32, w.shape, 1)
    swapped = jnp.where(lane < levels, pltpu.roll(w, width - levels, 1), pltpu.roll(w, levels, 1))
    cos = ((quarter == 0).astype(F32) - (quarter == 2).astype(F32))
    sin = ((quarter == 1).astype(F32) - (quarter == 3).astype(F32))
    turned = w * cos + swapped * jnp.where(lane < levels, -sin, sin)
    ref[start : start + size, 0:width] = jnp.where(lane < 2 * levels, turned, w)


def copy_rows(dst, dst_base, src, cell, step, count):
    def body(s, carry):
        dst[pl.ds(dst_base + s, 1), :] = src[pl.ds(cell + s * step, 1), :]
        return carry

    lax.fori_loop(0, count, body, 0, unroll=8)


def wind_row(src, a, which, levels):
    start = which * levels
    chunk, off = start // LANES, start % LANES
    first = src[a, :, chunk * LANES : (chunk + 1) * LANES]
    if off == 0:
        return first
    second = src[a, :, (chunk + 1) * LANES : (chunk + 2) * LANES]
    lane = lax.broadcasted_iota(jnp.int32, first.shape, 1)
    shift = LANES - off
    return jnp.where(lane < shift, pltpu.roll(first, shift, 1), pltpu.roll(second, shift, 1))


def repeat_levels(face, levels, chunks):
    lane = lax.broadcasted_iota(jnp.int32, face.shape, 1)
    rolls = {0: face}
    out = []
    for c in range(chunks):
        result, at = None, 0
        while at < LANES:
            index = (c * LANES + at) % levels
            shift = (at - index) % LANES
            if shift not in rolls:
                rolls[shift] = pltpu.roll(face, shift, 1)
            result = rolls[shift] if result is None else jnp.where(lane < at, result, rolls[shift])
            at += levels - index
        out.append(result)
    return out


def transport(src, dst, face_lead, face_sub, lo, hi, winds, levels):
    (lead, lead_sign), (sub, sub_sign) = winds
    size, feats = src.shape[1], src.shape[2]
    chunks = feats // LANES
    period = face_lead.shape[2] // LANES
    block = next(b for b in range(face_sub.shape[0], 0, -1) if (hi - lo) % b == 0)

    def store(ref, at, face):
        for c, part in enumerate(repeat_levels(face, levels, period)):
            ref[at, :, c * LANES : (c + 1) * LANES] = part

    def body(b, carry):
        first = lo + b * block
        for r in range(block + 1):
            wind = wind_row(src, first - 1 + r, lead, levels) + wind_row(src, first + r, lead, levels)
            store(face_lead, r, (0.5 * COURANT * lead_sign) * wind)
        for r in range(block):
            wind = wind_row(src, first + r, sub, levels)
            store(face_sub, r, (0.5 * COURANT * sub_sign) * (wind + pltpu.roll(wind, size - 1, 0)))
        for c3 in range(period):
            lanes3 = slice(c3 * LANES, (c3 + 1) * LANES)
            group = [slice(c * LANES, (c + 1) * LANES) for c in range(c3, chunks, period)]
            face = face_lead[0, :, lanes3]
            q = [src[first, :, lanes] for lanes in group]
            before = [face * jnp.where(face > 0.0, src[first - 1, :, lanes], here) for lanes, here in zip(group, q)]
            for r in range(block):
                face, side = face_lead[r + 1, :, lanes3], face_sub[r, :, lanes3]
                for i, lanes in enumerate(group):
                    ahead = src[first + r + 1, :, lanes]
                    flux = face * jnp.where(face > 0.0, q[i], ahead)
                    cross = side * jnp.where(side > 0.0, q[i], pltpu.roll(q[i], size - 1, 0))
                    dst[first + r, :, lanes] = q[i] - ((flux - before[i]) + (cross - pltpu.roll(cross, 1, 0)))
                    q[i], before[i] = ahead, flux
        return carry

    lax.fori_loop(0, (hi - lo) // block, body, 0)


def network_forward(x, mask, w_in, w_out, state, hsum, rows, kept):
    normed, scale, slope, hidden = state
    total = None
    for use in range(3):
        inv = lax.rsqrt(jnp.mean(x * x, axis=1, keepdims=True) + EPS)
        unit = (x * inv).astype(BF16)
        normed[use, rows, :] = unit
        scale[use, rows, :] = mask if use == 0 else jnp.broadcast_to(inv, (x.shape[0], LANES))
        p = jnp.dot(unit, w_in, preferred_element_type=F32)
        s = 0.5 + 0.5 * jnp.tanh(0.5 * p)
        silu = p * s
        slope[use, rows, :] = (s + silu * (1.0 - s)).astype(BF16)
        h = silu.astype(BF16)
        hidden[use, rows, :] = h
        kept(use)
        if use < 2:
            total = h.astype(F32) if use == 0 else total + h.astype(F32)
            x = x + TAU * jnp.dot(h, w_out, preferred_element_type=F32)
        else:
            hsum[rows, :] = total + h.astype(F32) * mask[:, 0:1]


def state_copies(source, target, sems, use, part, rows):
    return [
        pltpu.make_async_copy(a.at[use, rows, :], b.at[use, rows, :], sems.at[part, use, i])
        for i, (a, b) in enumerate(zip(source, target))
    ]


def pack_strip(n, levels, k, o, air, out):
    base, cm, cd = side_rows((k - o + 4) % 4, n)
    for d in range(2):
        copy_rows(out, d * n, air, base + cd * d + cm * (n - 1), -cm, n)
    turn_winds(out, (0, 2 * n), o, levels)


def pack_kernel(n, levels, turn, air, s1, s3):
    pack_strip(n, levels, 1, turn[0, 0], air, s1)
    pack_strip(n, levels, 3, turn[0, 0], air, s3)


def pack_with_corners_kernel(n, levels, turn, air, h1, h3, order, s0, s2):
    del order
    pack_strip(n, levels, 0, turn[0, 0], air, s0)
    pack_strip(n, levels, 2, turn[0, 0], air, s2)
    s0[2 * n : 2 * n + 1, :] = h1[n - 1 : n, :]
    s0[2 * n + 1 : 2 * n + 2, :] = h3[0:1, :]
    s2[2 * n : 2 * n + 1, :] = h1[0:1, :]
    s2[2 * n + 1 : 2 * n + 2, :] = h3[n - 1 : n, :]


def inner_transport_kernel(n, levels, turn, air_rows, moved, own, token, q_one, face_lead, face_sub):
    o = turn[0, 0]
    air = air_rows.reshape(n, n, air_rows.shape[1])
    winds = ((0, 1.0), (1, 1.0))
    transport(air, q_one, face_lead, face_sub, 1, n - 1, winds, levels)
    transport(q_one, moved, face_lead, face_sub, 2, n - 2, winds, levels)
    for k in range(4):
        base, cm, cd = side_rows((k - o + 4) % 4, n)
        for d in range(4):
            copy_rows(own, (k * 4 + d) * n, air_rows, base + cd * d, cm, n)
        turn_winds(own, (k * 4 * n, 4 * n), o, levels)
    token[...] = jnp.zeros_like(token)


def cost_mask(n, cost, mask):
    diagonal = lax.broadcasted_iota(jnp.int32, (n, n), 0) == lax.broadcasted_iota(jnp.int32, (n, n), 1)

    def mask_row(i, carry):
        two = jnp.broadcast_to((cost[pl.ds(i, 1), :] == 2).astype(F32), (n, n))
        column = jnp.sum(jnp.where(diagonal, two, 0.0), axis=1, keepdims=True)
        mask[pl.ds(pl.multiple_of(i * n, 8), n), :] = jnp.broadcast_to(column, (n, LANES))
        return carry

    lax.fori_loop(0, n, mask_row, 0, unroll=8)


def inner_parts(n):
    inner, parts = n - 4, 2
    size = inner // parts * n
    return [(part, part * size, size) for part in range(parts)]


def inner_network_kernel(n, dest, turn, moved, cost, w_in, w_out, n_o, s_o, g_o, h_o, outgoing, mask_rim,
                         normed, scale, slope, hidden, hsum, mask, sems):
    state, out = (normed, scale, slope, hidden), (n_o, s_o, g_o, h_o)
    feats = moved.shape[2]
    cost_mask(n, cost, mask)
    for k in range(4):
        base, cm, cd = side_rows((k - turn[0, 0] + 4) % 4, n)
        for d in range(2):
            copy_rows(mask_rim, (k * 2 + d) * n, mask, base + cd * d, cm, n)
    copies = []
    for part, start, size in inner_parts(n):
        rows = slice(start, start + size)
        x = moved[2 + start // n : 2 + (start + size) // n, :, :].reshape(size, feats)
        m = mask[2 * n + start : 2 * n + start + size, :]

        def kept(use, part=part, rows=pl.ds(start, size)):
            for copy in state_copies(state, out, sems, use, part, rows):
                copy.start()
                copies.append(copy)

        network_forward(x, m, w_in[...], w_out[...], state, hsum, rows, kept)

    def place(i, carry):
        for j in range(2, n - 2):
            outgoing[pl.ds(dest[i, j], 1), :] = hsum[pl.ds((i - 2) * n + j, 1), :]
        return carry

    lax.fori_loop(2, n - 2, place, 0)
    for copy in copies:
        copy.wait()


def rim_kernel(n, levels, turn, dest, h0, h1, h2, h3, own, mask_rim, w_in, w_out, before,
               n_o, s_o, g_o, h_o, outgoing, sent,
               normed, scale, slope, hidden, sems,
               wide, wide_one, wide_two, slim, slim_one, slim_two, lead_wide, sub_wide, lead_slim, sub_slim, x_rim, hsum):
    del before
    state, out = (normed, scale, slope, hidden), (n_o, s_o, g_o, h_o)
    o = turn[0, 0]
    halo = (h0, h1, h2, h3)
    for k in range(4):
        ends = k % 2 == 0
        src, one, two = (wide, wide_one, wide_two) if ends else (slim, slim_one, slim_two)
        lead, sub = (lead_wide, sub_wide) if ends else (lead_slim, sub_slim)
        for depth in range(6):
            d = depth - 2
            row = halo[k][(1 - depth) * n : (2 - depth) * n, :] if d < 0 else own[(k * 4 + d) * n : (k * 4 + d + 1) * n, :]
            src[depth, 0:n, :] = row
            if ends:
                src[depth, n + 2 : n + 8, :] = row[0:6, :]
                src[depth, n + 8 : n + 14, :] = row[n - 6 : n, :]
                for e in range(2):
                    if d < 0:
                        at = 2 * n + k // 2
                        src[depth, n + 1 - e : n + 2 - e, :] = halo[k][at : at + 1, :]
                        at = 2 * n + 1 - k // 2
                        src[depth, n + 14 + e : n + 15 + e, :] = halo[k][at : at + 1, :]
                    else:
                        at = e * n + n - 1 - d
                        src[depth, n + 1 - e : n + 2 - e, :] = halo[(k + 1) % 4][at : at + 1, :]
                        at = e * n + d
                        src[depth, n + 14 + e : n + 15 + e, :] = halo[(k + 3) % 4][at : at + 1, :]
        transport(src, one, lead, sub, 1, 5, SIDE_WINDS[k], levels)
        transport(one, two, lead, sub, 2, 4, SIDE_WINDS[k], levels)
        for d in range(2):
            at = (k * 2 + d) * n
            x_rim[at : at + n, :] = two[2 + d, 0:n, :]
            if ends:
                x_rim[at : at + 2, :] = two[2 + d, n + 2 : n + 4, :]
                x_rim[at + n - 2 : at + n, :] = two[2 + d, n + 12 : n + 14, :]
    turn_winds(x_rim, (0, 8 * n), (4 - o) % 4, levels)
    copies = []

    def kept(use):
        for copy in state_copies(state, out, sems, use, 0, pl.ds(0, 8 * n)):
            copy.start()
            copies.append(copy)

    network_forward(x_rim[...], mask_rim[...], w_in[...], w_out[...], state, hsum, slice(0, 8 * n), kept)
    for k in range(4):
        (bi, di, mi), (bj, dj, mj) = side_cells((k - o + 4) % 4, n)
        skip = 2 * (k % 2)
        for d in range(2):
            for m in range(skip, n - skip):
                at = (k * 2 + d) * n + m
                row = dest[bi + di * d + mi * m, bj + dj * d + mj * m]
                outgoing[pl.ds(row, 1), :] = hsum[at : at + 1, :]
    copies.append(pltpu.make_async_copy(outgoing, sent, sems.at[1, 0, 0]))
    copies[-1].start()
    for copy in copies:
        copy.wait()


def contract_rows(a, b):
    return lax.dot_general(a, b, (((0,), (0,)), ((), ())), preferred_element_type=F32)


def contract_last(a, b):
    return lax.dot_general(a, b, (((1,), (1,)), ((), ())), preferred_element_type=F32)


def network_backward(cot, valid, w_in, w_out, state, err_out, err_in, rows, at, arrived):
    normed, scale, slope, _ = state
    arrived("chain")
    cot = cot * valid
    grad = cot * scale[0, rows, 0:1]
    for use in (2, 1, 0):
        e = (TAU * grad).astype(BF16)
        err_out[use, at, :] = e
        inner = (contract_last(e, w_out) * slope[use, rows, :].astype(F32)).astype(BF16)
        err_in[use, rows, :] = inner
        if use > 0:
            d = contract_last(inner, w_in)
            unit = normed[use, rows, :].astype(F32)
            d = scale[use, rows, 0:1] * (d - unit * jnp.mean(d * unit, axis=1, keepdims=True))
            grad = (cot if use == 2 else grad) + d


def store_pieces(grid_shape, me, grad, keep, send):
    groups, tiles = grid_shape
    rows = grad.shape[0] // (groups * tiles)
    bits = (tiles // 2).bit_length() - 1
    for g in range(groups):
        for t in range(tiles):
            p = g * tiles + t
            rg, rt = me[0] ^ g, me[1] ^ t
            at = (rg // 2) * 2 + rt % 2
            for b in range(bits):
                at = at * 2 + (rt >> (b + 1)) % 2

            def store(ref, p=p, at=at):
                for c in range(grad.shape[1] // COL):
                    ref[at, c * rows : (c + 1) * rows, :] = grad[p * rows : (p + 1) * rows, c * COL : (c + 1) * COL]

            pl.when(rg % 2 == 0)(functools.partial(store, keep))
            pl.when(rg % 2 == 1)(functools.partial(store, send))


def backward_kernel(n, grid_shape, me, turn, cot_in, w_in, w_out, in_ni, in_si, in_gi, in_nr, in_sr, in_gr,
                    keep, send, err_out, n_i, s_i, g_i, n_r, s_r, g_r, sems, ei_i, ei_r, cot, cot_rim, grad_in):
    o = turn[0, 0]
    parts = inner_parts(n)
    inner = (n - 4) * n
    edge = 2 * n
    index = 0

    def fetch(source, target):
        nonlocal index
        copy = pltpu.make_async_copy(source, target, sems.at[index])
        index += 1
        copy.start()
        return copy

    chain, late = {}, []
    groups = [(part, (in_ni, in_si, in_gi), (n_i, s_i, g_i), start, size) for part, start, size in parts]
    groups.append((len(parts), (in_nr, in_sr, in_gr), (n_r, s_r, g_r), 0, 8 * n))
    for part, source, here, start, size in groups:
        rows = pl.ds(start, size)
        chain[part] = []
        if part < len(parts):
            at = pl.ds(edge + start, size)
            chain[part].append(fetch(cot_in.at[at, :], cot.at[at, :]))
        else:
            for at in (pl.ds(0, edge), pl.ds(edge + inner, edge)):
                chain[part].append(fetch(cot_in.at[at, :], cot.at[at, :]))
        chain[part].append(fetch(source[1].at[:, rows, :], here[1].at[:, rows, :]))
        chain[part].append(fetch(source[2].at[:, rows, :], here[2].at[:, rows, :]))
        chain[part].append(fetch(source[0].at[pl.ds(1, 2), rows, :], here[0].at[pl.ds(1, 2), rows, :]))
    for part, source, here, start, size in groups:
        rows = pl.ds(start, size)
        late.append(fetch(source[0].at[0, rows, :], here[0].at[0, rows, :]))

    def wait_for(part):
        def arrived(_):
            for copy in chain[part]:
                copy.wait()

        return arrived

    for part, start, size in parts:
        wait_for(part)(None)
        at = slice(edge + start, edge + start + size)
        j = lax.broadcasted_iota(jnp.int32, (size, 1), 0) % n
        valid = ((j >= 2) & (j < n - 2)).astype(F32)
        network_backward(cot[at, :], valid, w_in[...], w_out[...], (n_i, s_i, g_i, None), err_out, ei_i,
                         slice(start, start + size), slice(start, start + size), lambda _: None)
    wait_for(len(parts))(None)
    for k in range(4):
        base, cm, cd = side_rows((k - o + 4) % 4, n)
        for d in range(2):
            copy_rows(cot_rim, (k * 2 + d) * n, cot, base + cd * d, cm, n)
    e = lax.broadcasted_iota(jnp.int32, (8 * n, 1), 0)
    m = e % n
    valid = (((e // (2 * n)) % 2 == 0) | ((m >= 2) & (m < n - 2))).astype(F32)
    network_backward(cot_rim[...], valid, w_in[...], w_out[...], (n_r, s_r, g_r, None), err_out, ei_r,
                     slice(0, 8 * n), slice(inner, inner + 8 * n), lambda _: None)
    for copy in late:
        copy.wait()
    flat = lambda ref: ref[...].reshape(ref.shape[0] * ref.shape[1], ref.shape[2])
    grad_in[...] = contract_rows(flat(n_i), flat(ei_i)) + contract_rows(flat(n_r), flat(ei_r))
    store_pieces(grid_shape, me, grad_in, keep, send)


def output_gradient_kernel(n, grid_shape, me, err_out, in_hi, in_hr, keep, send, h, grad_out, sems):
    inner = (n - 4) * n
    copies = []
    for use in (2, 1, 0):
        for source, rows in ((in_hi, pl.ds(0, inner)), (in_hr, pl.ds(inner, 8 * n))):
            copy = pltpu.make_async_copy(source.at[use], h.at[use, rows, :], sems.at[len(copies)])
            copy.start()
            copies.append(copy)
    for copy in copies:
        copy.wait()
    flat = lambda ref: ref[...].reshape(ref.shape[0] * ref.shape[1], ref.shape[2])
    grad_out[...] = contract_rows(flat(h), flat(err_out))
    store_pieces(grid_shape, me, grad_out, keep, send)


def sum_over_devices(keep, send, groups, tiles):
    both = ("grp", "tile")
    piece = keep.shape[1:]
    sums = keep + lax.ppermute(send, "grp", [(i, i ^ 1) for i in range(groups)])
    sums = sums.reshape(groups // 2, 2, tiles // 2, *piece)
    total = sums[0, 0]
    for x in range(groups // 2):
        for y in range(2):
            if x or y:
                total = total + lax.ppermute(
                    sums[x, y], both, joint_perm(groups, tiles, lambda g, t: (g ^ (2 * x), t ^ y))
                )
    step = 2
    while step < tiles:
        half = total.shape[0] // 2
        total = total[:half] + lax.ppermute(total[half:], "tile", [(t, t ^ step) for t in range(tiles)])
        step *= 2
    return total[0]


def output_kernel(rows, w_out, out):
    x = rows[...]
    high = x.astype(BF16)
    low = (x - high.astype(F32)).astype(BF16)
    w = w_out[...]
    out[...] = TAU * (jnp.dot(high, w, preferred_element_type=F32) + jnp.dot(low, w, preferred_element_type=F32))


def shift_perm(count, by):
    return [(i, (i + by) % count) for i in range(count)]


def joint_perm(groups, tiles, move):
    return [(g * tiles + t, (lambda h: h[0] * tiles + h[1])(move(g, t))) for g in range(groups) for t in range(tiles)]


def per_device(air_state, cotangent, cost_count, assignment, orientation, weight_in, weight_out):
    groups, tiles = lax.axis_size("grp"), lax.axis_size("tile")
    count = groups * tiles
    n, feats = air_state.shape[0], air_state.shape[2]
    units = weight_in.shape[1]
    levels = feats // V
    cells, rim, inner = n * n, 8 * n, (n - 4) * n
    period = next(c for c in range(1, feats // LANES + 1) if c * LANES % levels == 0)
    shape = jax.ShapeDtypeStruct

    air_rows = air_state.reshape(cells, feats)
    cot_rows = cotangent.reshape(cells, feats)
    both = ("grp", "tile")

    def state(space, rows):
        return [
            space((3, rows, feats), BF16),
            space((3, rows, LANES), F32),
            space((3, rows, units), BF16),
            space((3, rows, units), BF16),
        ]

    parts = len(inner_parts(n))
    strips = pl.pallas_call(
        functools.partial(pack_kernel, n, levels),
        out_shape=[shape((2 * n, feats), F32)] * 2,
        in_specs=[SMEM, VMEM],
        out_specs=[VMEM] * 2,
        compiler_params=params(8),
        name="pack_strips",
    )(orientation, air_rows)
    from_left = lax.ppermute(strips[1], "grp", shift_perm(groups, 1))
    from_right = lax.ppermute(strips[0], "grp", shift_perm(groups, -1))

    moved, own, token = pl.pallas_call(
        functools.partial(inner_transport_kernel, n, levels),
        out_shape=[
            pltpu.VMEM((n, n, feats), F32),
            pltpu.VMEM((16 * n, feats), F32),
            shape((8, LANES), F32),
        ],
        in_specs=[SMEM, VMEM],
        out_specs=[VMEM] * 3,
        scratch_shapes=[
            pltpu.VMEM((n, n, feats), F32),
            pltpu.VMEM((8, n, period * LANES), F32),
            pltpu.VMEM((7, n, period * LANES), F32),
        ],
        compiler_params=params(10),
        cost_estimate=pl.CostEstimate(flops=60 * cells * feats, bytes_accessed=16 << 20, transcendentals=0),
        name="inner_transport",
    )(orientation, air_rows)

    strips = pl.pallas_call(
        functools.partial(pack_with_corners_kernel, n, levels),
        out_shape=[shape((2 * n + 8, feats), F32)] * 2,
        in_specs=[SMEM] + [VMEM] * 4,
        out_specs=[VMEM] * 2,
        compiler_params=params(8),
        name="pack_strips_corners",
    )(orientation, air_rows, from_left, from_right, token)
    from_above = lax.ppermute(strips[1], "tile", shift_perm(tiles, 1))
    from_below = lax.ppermute(strips[0], "tile", shift_perm(tiles, -1))

    *saved_inner, outgoing, mask_rim = pl.pallas_call(
        functools.partial(inner_network_kernel, n),
        out_shape=[*state(pltpu.HBM, inner), pltpu.VMEM((cells, units), F32), pltpu.VMEM((rim, LANES), F32)],
        in_specs=[SMEM] * 2 + [VMEM] * 4,
        out_specs=[HBM] * 4 + [VMEM] * 2,
        scratch_shapes=[
            *state(pltpu.VMEM, inner),
            pltpu.VMEM((inner, units), F32),
            pltpu.VMEM((cells, LANES), F32),
            pltpu.SemaphoreType.DMA((parts, 3, 4)),
        ],
        compiler_params=params(24),
        cost_estimate=pl.CostEstimate(
            flops=10 * inner * feats * units, bytes_accessed=16 << 20, transcendentals=3 * inner * units
        ),
        name="inner_network",
    )(assignment, orientation, moved, cost_count, weight_in, weight_out)

    wide, slim = n + 16, n
    *saved_rim, _, outgoing = pl.pallas_call(
        functools.partial(rim_kernel, n, levels),
        out_shape=[*state(pltpu.HBM, rim), pltpu.VMEM((cells, units), F32), pltpu.HBM((cells, units), F32)],
        in_specs=[SMEM, SMEM] + [VMEM] * 9,
        out_specs=[HBM] * 4 + [VMEM, HBM],
        input_output_aliases={10: 4},
        scratch_shapes=[*state(pltpu.VMEM, rim), pltpu.SemaphoreType.DMA((2, 3, 4))]
        + [pltpu.VMEM((6, wide, feats), F32)] * 3
        + [pltpu.VMEM((6, slim, feats), F32)] * 3
        + [pltpu.VMEM((5, wide, period * LANES), F32), pltpu.VMEM((4, wide, period * LANES), F32)]
        + [pltpu.VMEM((5, slim, period * LANES), F32), pltpu.VMEM((4, slim, period * LANES), F32)]
        + [pltpu.VMEM((rim, feats), F32), pltpu.VMEM((rim, units), F32)],
        compiler_params=params(16),
        cost_estimate=pl.CostEstimate(
            flops=10 * rim * feats * units, bytes_accessed=20 << 20, transcendentals=3 * rim * units
        ),
        name="rim_columns",
    )(orientation, assignment, from_above, from_left, from_below, from_right, own, mask_rim, weight_in, weight_out, outgoing)

    arrived = lax.all_to_all(
        outgoing.reshape(count, cells // count, units), both, split_axis=0, concat_axis=0, tiled=True
    ).reshape(cells, units)

    me = jnp.stack([lax.axis_index("grp"), lax.axis_index("tile")]).astype(jnp.int32)
    n_i, s_i, g_i, h_i = saved_inner
    n_r, s_r, g_r, h_r = saved_rim
    saved = lambda rows: state(pltpu.VMEM, rows)[:3]
    halves = lambda rows, columns: [shape((count // 2, rows // count * (columns // COL), COL), F32)] * 2
    *pieces_in, err_out = pl.pallas_call(
        functools.partial(backward_kernel, n, (groups, tiles)),
        out_shape=[*halves(feats, units), pltpu.VMEM((3, inner + rim, feats), BF16)],
        in_specs=[SMEM, SMEM, HBM, VMEM, VMEM] + [HBM] * 6,
        out_specs=[VMEM] * 3,
        scratch_shapes=[
            *saved(inner),
            *saved(rim),
            pltpu.SemaphoreType.DMA((5 * parts + 6,)),
            pltpu.VMEM((3, inner, units), BF16),
            pltpu.VMEM((3, rim, units), BF16),
            pltpu.VMEM((cells, feats), F32),
            pltpu.VMEM((rim, feats), F32),
            pltpu.VMEM((feats, units), F32),
        ],
        compiler_params=params(36),
        cost_estimate=pl.CostEstimate(flops=16 * cells * feats * units, bytes_accessed=20 << 20, transcendentals=0),
        name="columns_backward",
    )(me, orientation, cot_rows, weight_in, weight_out, n_i, s_i, g_i, n_r, s_r, g_r)
    pieces_out = pl.pallas_call(
        functools.partial(output_gradient_kernel, n, (groups, tiles)),
        out_shape=halves(units, feats),
        in_specs=[SMEM, VMEM, HBM, HBM],
        out_specs=[VMEM] * 2,
        scratch_shapes=[
            pltpu.VMEM((3, inner + rim, units), BF16),
            pltpu.VMEM((units, feats), F32),
            pltpu.SemaphoreType.DMA((6,)),
        ],
        compiler_params=params(24),
        cost_estimate=pl.CostEstimate(flops=6 * cells * feats * units, bytes_accessed=8 << 20, transcendentals=0),
        name="output_gradient",
    )(me, err_out, h_i, h_r)

    flat = lambda part, rows: part.reshape(-1, rows, COL).transpose(1, 0, 2).reshape(-1)
    summed_in = flat(sum_over_devices(*pieces_in, groups, tiles), feats // count)
    summed_out = flat(sum_over_devices(*pieces_out, groups, tiles), units // count)

    block = cells // 4
    tendency = pl.pallas_call(
        output_kernel,
        out_shape=shape((cells, feats), F32),
        grid=(cells // block,),
        in_specs=[pl.BlockSpec((block, units), lambda i: (i, 0)), pl.BlockSpec((units, feats), lambda i: (0, 0))],
        out_specs=pl.BlockSpec((block, feats), lambda i: (i, 0)),
        compiler_params=params(32),
        cost_estimate=pl.CostEstimate(flops=4 * cells * feats * units, bytes_accessed=6 << 20, transcendentals=0),
        name="tendency_rows",
    )(arrived, weight_out)
    return (tendency, summed_in, summed_out)


def solution(mesh):
    in_specs = (
        P("tile", "grp", None),
        P("tile", "grp", None),
        P("tile", "grp"),
        P("tile", "grp"),
        P("tile", "grp"),
        P(),
        P(),
    )
    out_specs = (P(("grp", "tile"), None), P(("grp", "tile")), P(("grp", "tile")))
    return jax.shard_map(
        per_device, mesh=mesh, in_specs=in_specs, out_specs=out_specs, check_vma=False
    )
```

```python
import functools
import jax
import jax.numpy as jnp
from jax import lax
from jax.experimental import pallas as pl
from jax.experimental.pallas import tpu as pltpu
from jax.sharding import PartitionSpec as P

V = 8
TAU = 0.5
COURANT = 0.1
EPS = 1e-06
LANES = 128
COL = 256
F32 = jnp.float32
BF16 = jnp.bfloat16
SIDE_WINDS = (((0, 1.0), (1, 1.0)), ((1, 1.0), (0, -1.0)), ((0, -1.0), (1, -1.0)), ((1, -1.0), (0, 1.0)))

VMEM = pl.BlockSpec(memory_space=pltpu.VMEM)
HBM = pl.BlockSpec(memory_space=pltpu.HBM)
SMEM = pl.BlockSpec(memory_space=pltpu.SMEM)


def params(mib):
    return pltpu.CompilerParams(vmem_limit_bytes=mib * 1024 * 1024)


def side_cells(k, n):
    pick = lambda a, b, c, e: jnp.where(k == 0, a, jnp.where(k == 1, b, jnp.where(k == 2, c, e)))
    return (pick(0, n - 1, n - 1, 0), pick(1, 0, -1, 0), pick(0, -1, 0, 1)), (
        pick(0, 0, n - 1, n - 1), pick(0, 1, 0, -1), pick(1, 0, -1, 0))


def side_rows(k, n):
    (bi, di, mi), (bj, dj, mj) = side_cells(k, n)
    return bi * n + bj, mi * n + mj, di * n + dj


def turn_winds(ref, rows, quarter, levels):
    start, size = rows
    width = -(-2 * levels // LANES) * LANES
    w = ref[start : start + size, 0:width]
    lane = lax.broadcasted_iota(jnp.int32, w.shape, 1)
    swapped = jnp.where(lane < levels, pltpu.roll(w, width - levels, 1), pltpu.roll(w, levels, 1))
    cos = ((quarter == 0).astype(F32) - (quarter == 2).astype(F32))
    sin = ((quarter == 1).astype(F32) - (quarter == 3).astype(F32))
    turned = w * cos + swapped * jnp.where(lane < levels, -sin, sin)
    ref[start : start + size, 0:width] = jnp.where(lane < 2 * levels, turned, w)


def copy_rows(dst, dst_base, src, cell, step, count):
    def body(s, carry):
        dst[pl.ds(dst_base + s, 1), :] = src[pl.ds(cell + s * step, 1), :]
        return carry

    lax.fori_loop(0, count, body, 0, unroll=8)


def wind_row(src, a, which, levels):
    start = which * levels
    chunk, off = start // LANES, start % LANES
    first = src[a, :, chunk * LANES : (chunk + 1) * LANES]
    if off == 0:
        return first
    second = src[a, :, (chunk + 1) * LANES : (chunk + 2) * LANES]
    lane = lax.broadcasted_iota(jnp.int32, first.shape, 1)
    shift = LANES - off
    return jnp.where(lane < shift, pltpu.roll(first, shift, 1), pltpu.roll(second, shift, 1))


def repeat_levels(face, levels, chunks):
    lane = lax.broadcasted_iota(jnp.int32, face.shape, 1)
    rolls = {0: face}
    out = []
    for c in range(chunks):
        result, at = None, 0
        while at < LANES:
            index = (c * LANES + at) % levels
            shift = (at - index) % LANES
            if shift not in rolls:
                rolls[shift] = pltpu.roll(face, shift, 1)
            result = rolls[shift] if result is None else jnp.where(lane < at, result, rolls[shift])
            at += levels - index
        out.append(result)
    return out


def transport(src, dst, face_lead, face_sub, lo, hi, winds, levels):
    (lead, lead_sign), (sub, sub_sign) = winds
    size, feats = src.shape[1], src.shape[2]
    chunks = feats // LANES
    period = face_lead.shape[2] // LANES
    block = next(b for b in range(face_sub.shape[0], 0, -1) if (hi - lo) % b == 0)

    def store(ref, at, face):
        for c, part in enumerate(repeat_levels(face, levels, period)):
            ref[at, :, c * LANES : (c + 1) * LANES] = part

    def body(b, carry):
        first = lo + b * block
        for r in range(block + 1):
            wind = wind_row(src, first - 1 + r, lead, levels) + wind_row(src, first + r, lead, levels)
            store(face_lead, r, (0.5 * COURANT * lead_sign) * wind)
        for r in range(block):
            wind = wind_row(src, first + r, sub, levels)
            store(face_sub, r, (0.5 * COURANT * sub_sign) * (wind + pltpu.roll(wind, size - 1, 0)))
        for c3 in range(period):
            lanes3 = slice(c3 * LANES, (c3 + 1) * LANES)
            group = [slice(c * LANES, (c + 1) * LANES) for c in range(c3, chunks, period)]
            face = face_lead[0, :, lanes3]
            q = [src[first, :, lanes] for lanes in group]
            before = [face * jnp.where(face > 0.0, src[first - 1, :, lanes], here) for lanes, here in zip(group, q)]
            for r in range(block):
                face, side = face_lead[r + 1, :, lanes3], face_sub[r, :, lanes3]
                for i, lanes in enumerate(group):
                    ahead = src[first + r + 1, :, lanes]
                    flux = face * jnp.where(face > 0.0, q[i], ahead)
                    cross = side * jnp.where(side > 0.0, q[i], pltpu.roll(q[i], size - 1, 0))
                    dst[first + r, :, lanes] = q[i] - ((flux - before[i]) + (cross - pltpu.roll(cross, 1, 0)))
                    q[i], before[i] = ahead, flux
        return carry

    lax.fori_loop(0, (hi - lo) // block, body, 0)


def network_forward(x, mask, w_in, w_out, state, hsum, rows, kept):
    normed, scale, slope, hidden = state
    x, total = x(), None
    for use in range(3):
        inv = lax.rsqrt(jnp.mean(x * x, axis=1, keepdims=True) + EPS)
        unit = (x * inv).astype(BF16)
        normed[use, rows, :] = unit
        if use == 0:
            packed = mask()
            lane = lax.broadcasted_iota(jnp.int32, packed.shape, 1)
        else:
            packed = jnp.where(lane < 32 * use, packed, inv)
        yield
        p = jnp.dot(unit, w_in[...], preferred_element_type=F32)
        yield
        s = 0.5 + 0.5 * jnp.tanh(0.5 * p)
        silu = p * s
        slope[use, rows, :] = s + silu * (1.0 - s)
        h = silu.astype(BF16)
        hidden[use, rows, :] = h
        if use == 2:
            scale[rows, :] = packed
        kept(use)
        if use < 2:
            total = h.astype(F32) if use == 0 else total + h.astype(F32)
            yield
            x = x + TAU * jnp.dot(h, w_out[...], preferred_element_type=F32)
            yield
        else:
            hsum[rows, :] = total + h.astype(F32) * mask()[:, 0:1]


def run_together(steps, lag):
    steps = list(steps)
    live, tick = set(range(len(steps))), 0
    while live:
        for i in sorted(live):
            if tick >= lag * i and next(steps[i], 1) == 1:
                live.discard(i)
        tick += 1


def state_copies(source, target, sems, use, part, rows):
    copies = []
    for i, (a, b) in enumerate(zip(source, target)):
        if i == 1 and use < 2:
            continue
        at = (rows, slice(None)) if i == 1 else (use, rows, slice(None))
        copies.append(pltpu.make_async_copy(a.at[at], b.at[at], sems.at[part, use, i]))
    return copies


def pack_strip(n, levels, k, o, air, out):
    base, cm, cd = side_rows((k - o + 4) % 4, n)
    for d in range(2):
        copy_rows(out, d * n, air, base + cd * d + cm * (n - 1), -cm, n)
    turn_winds(out, (0, 2 * n), o, levels)


def pack_kernel(n, levels, turn, air, s1, s3):
    pack_strip(n, levels, 1, turn[0, 0], air, s1)
    pack_strip(n, levels, 3, turn[0, 0], air, s3)


def pack_with_corners_kernel(n, levels, turn, air, h1, h3, order, s0, s2):
    del order
    pack_strip(n, levels, 0, turn[0, 0], air, s0)
    pack_strip(n, levels, 2, turn[0, 0], air, s2)
    s0[2 * n : 2 * n + 1, :] = h1[n - 1 : n, :]
    s0[2 * n + 1 : 2 * n + 2, :] = h3[0:1, :]
    s2[2 * n : 2 * n + 1, :] = h1[0:1, :]
    s2[2 * n + 1 : 2 * n + 2, :] = h3[n - 1 : n, :]


def inner_transport_kernel(n, levels, turn, air_rows, moved, own, token, q_one, face_lead, face_sub):
    o = turn[0, 0]
    air = air_rows.reshape(n, n, air_rows.shape[1])
    winds = ((0, 1.0), (1, 1.0))
    transport(air, q_one, face_lead, face_sub, 1, n - 1, winds, levels)
    transport(q_one, moved, face_lead, face_sub, 2, n - 2, winds, levels)
    for k in range(4):
        base, cm, cd = side_rows((k - o + 4) % 4, n)
        for d in range(4):
            copy_rows(own, (k * 4 + d) * n, air_rows, base + cd * d, cm, n)
        turn_winds(own, (k * 4 * n, 4 * n), o, levels)
    token[...] = jnp.zeros_like(token)


def cost_mask(n, cost, mask):
    diagonal = lax.broadcasted_iota(jnp.int32, (n, n), 0) == lax.broadcasted_iota(jnp.int32, (n, n), 1)

    def mask_row(i, carry):
        two = jnp.broadcast_to((cost[pl.ds(i, 1), :] == 2).astype(F32), (n, n))
        column = jnp.sum(jnp.where(diagonal, two, 0.0), axis=1, keepdims=True)
        mask[pl.ds(pl.multiple_of(i * n, 8), n), :] = jnp.broadcast_to(column, (n, LANES))
        return carry

    lax.fori_loop(0, n, mask_row, 0, unroll=8)


PARTS = 2
LAG = 0


def inner_parts(n):
    inner = n - 4
    size = inner // PARTS * n
    return [(part, part * size, size) for part in range(PARTS)]


def inner_network_kernel(n, dest, turn, moved, cost, w_in, w_out, n_o, s_o, g_o, h_o, outgoing, mask_rim,
                         normed, scale, slope, hidden, hsum, mask, sems):
    state, out = (normed, scale, slope, hidden), (n_o, s_o, g_o, h_o)
    feats = moved.shape[2]
    cost_mask(n, cost, mask)
    for k in range(4):
        base, cm, cd = side_rows((k - turn[0, 0] + 4) % 4, n)
        for d in range(2):
            copy_rows(mask_rim, (k * 2 + d) * n, mask, base + cd * d, cm, n)
    copies = []
    steps = []
    for part, start, size in inner_parts(n):
        rows = slice(start, start + size)
        x = lambda start=start, size=size: moved[2 + start // n : 2 + (start + size) // n, :, :].reshape(size, feats)
        m = lambda start=start, size=size: mask[2 * n + start : 2 * n + start + size, :]

        def kept(use, part=part, rows=pl.ds(start, size)):
            for copy in state_copies(state, out, sems, use, part, rows):
                copy.start()
                copies.append(copy)

        steps.append(network_forward(x, m, w_in, w_out, state, hsum, rows, kept))
    run_together(steps, LAG)

    def place(i, carry):
        for j in range(2, n - 2):
            outgoing[pl.ds(dest[i, j], 1), :] = hsum[pl.ds((i - 2) * n + j, 1), :]
        return carry

    lax.fori_loop(2, n - 2, place, 0)
    for copy in copies:
        copy.wait()


def rim_kernel(n, levels, turn, dest, h0, h1, h2, h3, own, mask_rim, w_in, w_out, before,
               n_o, s_o, g_o, h_o, outgoing, sent,
               normed, scale, slope, hidden, sems,
               wide, wide_one, wide_two, slim, slim_one, slim_two, lead_wide, sub_wide, lead_slim, sub_slim, x_rim, hsum):
    del before
    state, out = (normed, scale, slope, hidden), (n_o, s_o, g_o, h_o)
    o = turn[0, 0]
    halo = (h0, h1, h2, h3)
    for k in range(4):
        ends = k % 2 == 0
        src, one, two = (wide, wide_one, wide_two) if ends else (slim, slim_one, slim_two)
        lead, sub = (lead_wide, sub_wide) if ends else (lead_slim, sub_slim)
        for depth in range(6):
            d = depth - 2
            row = halo[k][(1 - depth) * n : (2 - depth) * n, :] if d < 0 else own[(k * 4 + d) * n : (k * 4 + d + 1) * n, :]
            src[depth, 0:n, :] = row
            if ends:
                src[depth, n + 2 : n + 8, :] = row[0:6, :]
                src[depth, n + 8 : n + 14, :] = row[n - 6 : n, :]
                for e in range(2):
                    if d < 0:
                        at = 2 * n + k // 2
                        src[depth, n + 1 - e : n + 2 - e, :] = halo[k][at : at + 1, :]
                        at = 2 * n + 1 - k // 2
                        src[depth, n + 14 + e : n + 15 + e, :] = halo[k][at : at + 1, :]
                    else:
                        at = e * n + n - 1 - d
                        src[depth, n + 1 - e : n + 2 - e, :] = halo[(k + 1) % 4][at : at + 1, :]
                        at = e * n + d
                        src[depth, n + 14 + e : n + 15 + e, :] = halo[(k + 3) % 4][at : at + 1, :]
        transport(src, one, lead, sub, 1, 5, SIDE_WINDS[k], levels)
        transport(one, two, lead, sub, 2, 4, SIDE_WINDS[k], levels)
        for d in range(2):
            at = (k * 2 + d) * n
            x_rim[at : at + n, :] = two[2 + d, 0:n, :]
            if ends:
                x_rim[at : at + 2, :] = two[2 + d, n + 2 : n + 4, :]
                x_rim[at + n - 2 : at + n, :] = two[2 + d, n + 12 : n + 14, :]
    turn_winds(x_rim, (0, 8 * n), (4 - o) % 4, levels)
    copies = []

    def kept(use):
        for copy in state_copies(state, out, sems, use, 0, pl.ds(0, 8 * n)):
            copy.start()
            copies.append(copy)

    rows = slice(0, 8 * n)
    run_together(
        [network_forward(lambda: x_rim[...], lambda: mask_rim[...], w_in, w_out, state, hsum, rows, kept)], 0
    )
    for k in range(4):
        (bi, di, mi), (bj, dj, mj) = side_cells((k - o + 4) % 4, n)
        skip = 2 * (k % 2)
        for d in range(2):
            for m in range(skip, n - skip):
                at = (k * 2 + d) * n + m
                row = dest[bi + di * d + mi * m, bj + dj * d + mj * m]
                outgoing[pl.ds(row, 1), :] = hsum[at : at + 1, :]
    copies.append(pltpu.make_async_copy(outgoing, sent, sems.at[1, 0, 0]))
    copies[-1].start()
    for copy in copies:
        copy.wait()


def contract_rows(a, b):
    return lax.dot_general(a, b, (((0,), (0,)), ((), ())), preferred_element_type=F32)


def contract_last(a, b):
    return lax.dot_general(a, b, (((1,), (1,)), ((), ())), preferred_element_type=F32)


def network_backward(cot, valid, w_in, w_out, state, err_out, err_in, rows, at, arrived):
    normed, scale, slope = state
    arrived("cotangent")
    cot = cot() * valid
    grad = cot * scale[rows, 0:1]
    for use in (2, 1, 0):
        e = (TAU * grad).astype(BF16)
        err_out[use, at, :] = e
        yield
        back = contract_last(e, w_out[...])
        yield
        arrived(("slope", use))
        inner = (back * slope[use, rows, :]).astype(BF16)
        err_in[use, rows, :] = inner
        yield
        if use > 0:
            d = contract_last(inner, w_in[...])
            yield
            arrived(("normed", use))
            unit = normed[use, rows, :].astype(F32)
            d = scale[rows, 32 * use : 32 * use + 1] * (d - unit * jnp.mean(d * unit, axis=1, keepdims=True))
            grad = (cot if use == 2 else grad) + d


def exchange_order(groups, tiles, tile_first):
    bits = lambda axis, low, count: [(axis, low << b) for b in range(((count // low) - 1).bit_length())]
    plane = [bits("grp", 2, groups), [("tile", 1)]]
    first, second = plane[::-1] if tile_first else plane
    return [("grp", 1)] + first + second + bits("tile", 2, tiles)


def store_pieces(grid_shape, me, order, grad, keep, send):
    groups, tiles = grid_shape
    rows = grad.shape[0] // (groups * tiles)
    for g in range(groups):
        for t in range(tiles):
            p = g * tiles + t
            away = {"grp": me[0] ^ g, "tile": me[1] ^ t}
            at = 0
            for axis, bit in order[1:]:
                at = at * 2 + (away[axis] // bit) % 2

            def store(ref, p=p, at=at):
                for c in range(grad.shape[1] // COL):
                    ref[at, c * rows : (c + 1) * rows, :] = grad[p * rows : (p + 1) * rows, c * COL : (c + 1) * COL]

            pl.when(away["grp"] % 2 == 0)(functools.partial(store, keep))
            pl.when(away["grp"] % 2 == 1)(functools.partial(store, send))


def backward_kernel(n, grid_shape, order, me, turn, cot_in, in_weights, out_weights, in_ni, in_si, in_gi, in_hi,
                    in_nr, in_sr, in_gr, in_hr, keep, send, err_out, h, n_i, s_i, g_i, n_r, s_r, g_r, sems,
                    w_in, w_out, ei_i, ei_r, cot, cot_rim, grad_in):
    o = turn[0, 0]
    parts = inner_parts(n)
    inner = (n - 4) * n
    edge = 2 * n
    pairs = ((in_ni, n_i), (in_nr, n_r)), ((in_gi, g_i), (in_gr, g_r))
    normed = lambda use: [(a.at[use], b.at[use]) for a, b in pairs[0]]
    slope = lambda use: [(a.at[use], b.at[use]) for a, b in pairs[1]]
    plan = [
        ("cotangent", [(out_weights, w_out), (cot_in, cot), (in_si, s_i), (in_sr, s_r)]),
        (("slope", 2), [(in_weights, w_in), *slope(2)]),
        (("normed", 2), normed(2)),
        (("slope", 1), slope(1)),
        (("normed", 1), normed(1)),
        (("slope", 0), slope(0)),
        ("rest", [*normed(0), (in_hi, h.at[:, pl.ds(0, inner), :]), (in_hr, h.at[:, pl.ds(inner, 8 * n), :])]),
    ]
    index = 0
    flight = []

    def start_next():
        nonlocal index
        if plan:
            name, refs = plan.pop(0)
            copies = []
            for source, target in refs:
                copies.append(pltpu.make_async_copy(source, target, sems.at[index]))
                copies[-1].start()
                index += 1
            flight.append((name, copies))

    def arrived(name):
        if flight and flight[0][0] == name:
            for copy in flight.pop(0)[1]:
                copy.wait()
            start_next()

    start_next()
    start_next()
    steps = []
    for part, start, size in parts:
        at = slice(edge + start, edge + start + size)
        j = lax.broadcasted_iota(jnp.int32, (size, 1), 0) % n
        valid = ((j >= 2) & (j < n - 2)).astype(F32)
        rows = slice(start, start + size)
        steps.append(network_backward(lambda at=at: cot[at, :], valid, w_in, w_out, (n_i, s_i, g_i), err_out, ei_i,
                                      rows, rows, arrived))

    def rim_cotangent():
        for k in range(4):
            base, cm, cd = side_rows((k - o + 4) % 4, n)
            for d in range(2):
                copy_rows(cot_rim, (k * 2 + d) * n, cot, base + cd * d, cm, n)
        return cot_rim[...]

    e = lax.broadcasted_iota(jnp.int32, (8 * n, 1), 0)
    m = e % n
    valid = (((e // (2 * n)) % 2 == 0) | ((m >= 2) & (m < n - 2))).astype(F32)
    steps.append(network_backward(rim_cotangent, valid, w_in, w_out, (n_r, s_r, g_r), err_out, ei_r,
                                  slice(0, 8 * n), slice(inner, inner + 8 * n), arrived))
    run_together(steps, LAG)
    arrived("rest")
    flat = lambda ref: ref[...].reshape(ref.shape[0] * ref.shape[1], ref.shape[2])
    grad_in[...] = contract_rows(flat(n_i), flat(ei_i)) + contract_rows(flat(n_r), flat(ei_r))
    store_pieces(grid_shape, me, order, grad_in, keep, send)


def output_gradient_kernel(grid_shape, order, me, err_out, h, keep, send, grad_out):
    flat = lambda ref: ref[...].reshape(ref.shape[0] * ref.shape[1], ref.shape[2])
    grad_out[...] = contract_rows(flat(h), flat(err_out))
    store_pieces(grid_shape, me, order, grad_out, keep, send)


def sum_over_devices(keep, send, order, sizes):
    total = None
    for axis, bit in order:
        if total is not None:
            half = total.shape[0] // 2
            keep, send = total[:half], total[half:]
        total = keep + lax.ppermute(send, axis, [(i, i ^ bit) for i in range(sizes[axis])])
    return total[0]


def output_kernel(rows, w_out, out):
    x = rows[...]
    high = x.astype(BF16)
    low = (x - high.astype(F32)).astype(BF16)
    w = w_out[...]
    out[...] = TAU * (jnp.dot(high, w, preferred_element_type=F32) + jnp.dot(low, w, preferred_element_type=F32))


def shift_perm(count, by):
    return [(i, (i + by) % count) for i in range(count)]


def joint_perm(groups, tiles, move):
    return [(g * tiles + t, (lambda h: h[0] * tiles + h[1])(move(g, t))) for g in range(groups) for t in range(tiles)]


def per_device(air_state, cotangent, cost_count, assignment, orientation, weight_in, weight_out):
    groups, tiles = lax.axis_size("grp"), lax.axis_size("tile")
    count = groups * tiles
    n, feats = air_state.shape[0], air_state.shape[2]
    units = weight_in.shape[1]
    levels = feats // V
    cells, rim, inner = n * n, 8 * n, (n - 4) * n
    period = next(c for c in range(1, feats // LANES + 1) if c * LANES % levels == 0)
    shape = jax.ShapeDtypeStruct

    air_rows = air_state.reshape(cells, feats)
    cot_rows = cotangent.reshape(cells, feats)
    both = ("grp", "tile")

    def state(space, rows):
        return [
            space((3, rows, feats), BF16),
            space((rows, LANES), F32),
            space((3, rows, units), F32),
            space((3, rows, units), BF16),
        ]

    parts = len(inner_parts(n))
    strips = pl.pallas_call(
        functools.partial(pack_kernel, n, levels),
        out_shape=[shape((2 * n, feats), F32)] * 2,
        in_specs=[SMEM, VMEM],
        out_specs=[VMEM] * 2,
        compiler_params=params(8),
        name="pack_strips",
    )(orientation, air_rows)
    from_left = lax.ppermute(strips[1], "grp", shift_perm(groups, 1))
    from_right = lax.ppermute(strips[0], "grp", shift_perm(groups, -1))

    moved, own, token = pl.pallas_call(
        functools.partial(inner_transport_kernel, n, levels),
        out_shape=[
            pltpu.VMEM((n, n, feats), F32),
            pltpu.VMEM((16 * n, feats), F32),
            shape((8, LANES), F32),
        ],
        in_specs=[SMEM, VMEM],
        out_specs=[VMEM] * 3,
        scratch_shapes=[
            pltpu.VMEM((n, n, feats), F32),
            pltpu.VMEM((8, n, period * LANES), F32),
            pltpu.VMEM((7, n, period * LANES), F32),
        ],
        compiler_params=params(10),
        cost_estimate=pl.CostEstimate(flops=60 * cells * feats, bytes_accessed=16 << 20, transcendentals=0),
        name="inner_transport",
    )(orientation, air_rows)

    strips = pl.pallas_call(
        functools.partial(pack_with_corners_kernel, n, levels),
        out_shape=[shape((2 * n + 8, feats), F32)] * 2,
        in_specs=[SMEM] + [VMEM] * 4,
        out_specs=[VMEM] * 2,
        compiler_params=params(8),
        name="pack_strips_corners",
    )(orientation, air_rows, from_left, from_right, token)
    from_above = lax.ppermute(strips[1], "tile", shift_perm(tiles, 1))
    from_below = lax.ppermute(strips[0], "tile", shift_perm(tiles, -1))

    *saved_inner, outgoing, mask_rim = pl.pallas_call(
        functools.partial(inner_network_kernel, n),
        out_shape=[*state(pltpu.HBM, inner), pltpu.VMEM((cells, units), F32), pltpu.VMEM((rim, LANES), F32)],
        in_specs=[SMEM] * 2 + [VMEM] * 4,
        out_specs=[HBM] * 4 + [VMEM] * 2,
        scratch_shapes=[
            *state(pltpu.VMEM, inner),
            pltpu.VMEM((inner, units), F32),
            pltpu.VMEM((cells, LANES), F32),
            pltpu.SemaphoreType.DMA((parts, 3, 4)),
        ],
        compiler_params=params(24),
        cost_estimate=pl.CostEstimate(
            flops=10 * inner * feats * units, bytes_accessed=16 << 20, transcendentals=3 * inner * units
        ),
        name="inner_network",
    )(assignment, orientation, moved, cost_count, weight_in, weight_out)

    wide, slim = n + 16, n
    *saved_rim, _, outgoing = pl.pallas_call(
        functools.partial(rim_kernel, n, levels),
        out_shape=[*state(pltpu.HBM, rim), pltpu.VMEM((cells, units), F32), pltpu.HBM((cells, units), F32)],
        in_specs=[SMEM, SMEM] + [VMEM] * 9,
        out_specs=[HBM] * 4 + [VMEM, HBM],
        input_output_aliases={10: 4},
        scratch_shapes=[*state(pltpu.VMEM, rim), pltpu.SemaphoreType.DMA((2, 3, 4))]
        + [pltpu.VMEM((6, wide, feats), F32)] * 3
        + [pltpu.VMEM((6, slim, feats), F32)] * 3
        + [pltpu.VMEM((5, wide, period * LANES), F32), pltpu.VMEM((4, wide, period * LANES), F32)]
        + [pltpu.VMEM((5, slim, period * LANES), F32), pltpu.VMEM((4, slim, period * LANES), F32)]
        + [pltpu.VMEM((rim, feats), F32), pltpu.VMEM((rim, units), F32)],
        compiler_params=params(16),
        cost_estimate=pl.CostEstimate(
            flops=10 * rim * feats * units, bytes_accessed=20 << 20, transcendentals=3 * rim * units
        ),
        name="rim_columns",
    )(orientation, assignment, from_above, from_left, from_below, from_right, own, mask_rim, weight_in, weight_out, outgoing)

    arrived = lax.all_to_all(
        outgoing.reshape(count, cells // count, units), both, split_axis=0, concat_axis=0, tiled=True
    ).reshape(cells, units)

    me = jnp.stack([lax.axis_index("grp"), lax.axis_index("tile")]).astype(jnp.int32)
    stay = lambda x: pltpu.with_memory_space_constraint(x, pltpu.HBM)
    saved = lambda rows: state(pltpu.VMEM, rows)[:3]
    halves = lambda rows, columns: [shape((count // 2, rows // count * (columns // COL), COL), F32)] * 2
    orders = [exchange_order(groups, tiles, tile_first) for tile_first in (False, True)]
    *pieces_in, err_out, hidden = pl.pallas_call(
        functools.partial(backward_kernel, n, (groups, tiles), orders[0]),
        out_shape=[
            *halves(feats, units),
            pltpu.VMEM((3, inner + rim, feats), BF16),
            pltpu.VMEM((3, inner + rim, units), BF16),
        ],
        in_specs=[SMEM, SMEM] + [HBM] * 11,
        out_specs=[VMEM] * 4,
        scratch_shapes=[
            *saved(inner),
            *saved(rim),
            pltpu.SemaphoreType.DMA((19,)),
            pltpu.VMEM((feats, units), BF16),
            pltpu.VMEM((units, feats), BF16),
            pltpu.VMEM((3, inner, units), BF16),
            pltpu.VMEM((3, rim, units), BF16),
            pltpu.VMEM((cells, feats), F32),
            pltpu.VMEM((rim, feats), F32),
            pltpu.VMEM((feats, units), F32),
        ],
        compiler_params=params(36),
        cost_estimate=pl.CostEstimate(flops=16 * cells * feats * units, bytes_accessed=20 << 20, transcendentals=0),
        name="columns_backward",
    )(me, orientation, *map(stay, (cot_rows, weight_in, weight_out, *saved_inner, *saved_rim)))
    pieces_out = pl.pallas_call(
        functools.partial(output_gradient_kernel, (groups, tiles), orders[1]),
        out_shape=halves(units, feats),
        in_specs=[SMEM, VMEM, VMEM],
        out_specs=[VMEM] * 2,
        scratch_shapes=[pltpu.VMEM((units, feats), F32)],
        compiler_params=params(24),
        cost_estimate=pl.CostEstimate(flops=6 * cells * feats * units, bytes_accessed=8 << 20, transcendentals=0),
        name="output_gradient",
    )(me, err_out, hidden)

    flat = lambda part, rows: part.reshape(-1, rows, COL).transpose(1, 0, 2).reshape(-1)
    sizes = {"grp": groups, "tile": tiles}
    summed_in = flat(sum_over_devices(*pieces_in, orders[0], sizes), feats // count)
    summed_out = flat(sum_over_devices(*pieces_out, orders[1], sizes), units // count)

    block = cells // 4
    tendency = pl.pallas_call(
        output_kernel,
        out_shape=shape((cells, feats), F32),
        grid=(cells // block,),
        in_specs=[pl.BlockSpec((block, units), lambda i: (i, 0)), pl.BlockSpec((units, feats), lambda i: (0, 0))],
        out_specs=pl.BlockSpec((block, feats), lambda i: (i, 0)),
        compiler_params=params(32),
        cost_estimate=pl.CostEstimate(flops=4 * cells * feats * units, bytes_accessed=6 << 20, transcendentals=0),
        name="tendency_rows",
    )(arrived, weight_out)
    return (tendency, summed_in, summed_out)


def solution(mesh):
    in_specs = (
        P("tile", "grp", None),
        P("tile", "grp", None),
        P("tile", "grp"),
        P("tile", "grp"),
        P("tile", "grp"),
        P(),
        P(),
    )
    out_specs = (P(("grp", "tile"), None), P(("grp", "tile")), P(("grp", "tile")))
    return jax.shard_map(
        per_device, mesh=mesh, in_specs=in_specs, out_specs=out_specs, check_vma=False
    )
```

```python
import functools
import jax
import jax.numpy as jnp
from jax import lax
from jax.experimental import pallas as pl
from jax.experimental.pallas import tpu as pltpu
from jax.sharding import PartitionSpec as P

V = 8
TAU = 0.5
COURANT = 0.1
EPS = 1e-06
LANES = 128
COL = 256
F32 = jnp.float32
BF16 = jnp.bfloat16
SIDE_WINDS = (((0, 1.0), (1, 1.0)), ((1, 1.0), (0, -1.0)), ((0, -1.0), (1, -1.0)), ((1, -1.0), (0, 1.0)))

VMEM = pl.BlockSpec(memory_space=pltpu.VMEM)
HBM = pl.BlockSpec(memory_space=pltpu.HBM)
SMEM = pl.BlockSpec(memory_space=pltpu.SMEM)


def params(mib):
    return pltpu.CompilerParams(vmem_limit_bytes=mib * 1024 * 1024)


def side_cells(k, ni, nj):
    pick = lambda a, b, c, e: jnp.where(k == 0, a, jnp.where(k == 1, b, jnp.where(k == 2, c, e)))
    return (pick(0, ni - 1, ni - 1, 0), pick(1, 0, -1, 0), pick(0, -1, 0, 1)), (
        pick(0, 0, nj - 1, nj - 1), pick(0, 1, 0, -1), pick(1, 0, -1, 0))


def side_rows(k, ni, nj=None):
    nj = ni if nj is None else nj
    (bi, di, mi), (bj, dj, mj) = side_cells(k, ni, nj)
    return bi * nj + bj, mi * nj + mj, di * nj + dj


def turn_winds(ref, rows, quarter, levels):
    start, size = rows
    width = -(-2 * levels // LANES) * LANES
    w = ref[start : start + size, 0:width]
    lane = lax.broadcasted_iota(jnp.int32, w.shape, 1)
    swapped = jnp.where(lane < levels, pltpu.roll(w, width - levels, 1), pltpu.roll(w, levels, 1))
    cos = ((quarter == 0).astype(F32) - (quarter == 2).astype(F32))
    sin = ((quarter == 1).astype(F32) - (quarter == 3).astype(F32))
    turned = w * cos + swapped * jnp.where(lane < levels, -sin, sin)
    ref[start : start + size, 0:width] = jnp.where(lane < 2 * levels, turned, w)


def copy_rows(dst, dst_base, src, cell, step, count):
    def body(s, carry):
        dst[pl.ds(dst_base + s, 1), :] = src[pl.ds(cell + s * step, 1), :]
        return carry

    lax.fori_loop(0, count, body, 0, unroll=8)


def wind_row(src, a, which, levels):
    start = which * levels
    chunk, off = start // LANES, start % LANES
    first = src[a, :, chunk * LANES : (chunk + 1) * LANES]
    if off == 0:
        return first
    second = src[a, :, (chunk + 1) * LANES : (chunk + 2) * LANES]
    lane = lax.broadcasted_iota(jnp.int32, first.shape, 1)
    shift = LANES - off
    return jnp.where(lane < shift, pltpu.roll(first, shift, 1), pltpu.roll(second, shift, 1))


def repeat_levels(face, levels, chunks):
    lane = lax.broadcasted_iota(jnp.int32, face.shape, 1)
    rolls = {0: face}
    out = []
    for c in range(chunks):
        result, at = None, 0
        while at < LANES:
            index = (c * LANES + at) % levels
            shift = (at - index) % LANES
            if shift not in rolls:
                rolls[shift] = pltpu.roll(face, shift, 1)
            result = rolls[shift] if result is None else jnp.where(lane < at, result, rolls[shift])
            at += levels - index
        out.append(result)
    return out


def transport(src, dst, face_lead, face_sub, lo, hi, winds, levels):
    (lead, lead_sign), (sub, sub_sign) = winds
    size, feats = src.shape[1], src.shape[2]
    chunks = feats // LANES
    period = face_lead.shape[2] // LANES
    block = next(b for b in range(face_sub.shape[0], 0, -1) if (hi - lo) % b == 0)

    def store(ref, at, face):
        for c, part in enumerate(repeat_levels(face, levels, period)):
            ref[at, :, c * LANES : (c + 1) * LANES] = part

    def body(b, carry):
        first = lo + b * block
        for r in range(block + 1):
            wind = wind_row(src, first - 1 + r, lead, levels) + wind_row(src, first + r, lead, levels)
            store(face_lead, r, (0.5 * COURANT * lead_sign) * wind)
        for r in range(block):
            wind = wind_row(src, first + r, sub, levels)
            store(face_sub, r, (0.5 * COURANT * sub_sign) * (wind + pltpu.roll(wind, size - 1, 0)))
        for c3 in range(period):
            lanes3 = slice(c3 * LANES, (c3 + 1) * LANES)
            group = [slice(c * LANES, (c + 1) * LANES) for c in range(c3, chunks, period)]
            face = face_lead[0, :, lanes3]
            q = [src[first, :, lanes] for lanes in group]
            before = [face * jnp.where(face > 0.0, src[first - 1, :, lanes], here) for lanes, here in zip(group, q)]
            for r in range(block):
                face, side = face_lead[r + 1, :, lanes3], face_sub[r, :, lanes3]
                for i, lanes in enumerate(group):
                    ahead = src[first + r + 1, :, lanes]
                    flux = face * jnp.where(face > 0.0, q[i], ahead)
                    cross = side * jnp.where(side > 0.0, q[i], pltpu.roll(q[i], size - 1, 0))
                    dst[first + r, :, lanes] = q[i] - ((flux - before[i]) + (cross - pltpu.roll(cross, 1, 0)))
                    q[i], before[i] = ahead, flux
        return carry

    if hi - lo == block:
        body(0, 0)
    else:
        lax.fori_loop(0, (hi - lo) // block, body, 0)


def network_forward(x, mask, w_in, w_out, state, hsum, rows, kept):
    normed, scale, slope, hidden = state
    x, total = x(), None
    for use in range(3):
        inv = lax.rsqrt(jnp.mean(x * x, axis=1, keepdims=True) + EPS)
        unit = (x * inv).astype(BF16)
        normed[use, rows, :] = unit
        if use == 0:
            packed = mask()
            lane = lax.broadcasted_iota(jnp.int32, packed.shape, 1)
        else:
            packed = jnp.where(lane < 32 * use, packed, inv)
        yield
        p = jnp.dot(unit, w_in[...], preferred_element_type=F32)
        yield
        s = 0.5 + 0.5 * jnp.tanh(0.5 * p)
        silu = p * s
        slope[use, rows, :] = s + silu * (1.0 - s)
        h = silu.astype(BF16)
        hidden[use, rows, :] = h
        if use == 2:
            scale[rows, :] = packed
        kept(use)
        if use < 2:
            total = h.astype(F32) if use == 0 else total + h.astype(F32)
            yield
            x = x + TAU * jnp.dot(h, w_out[...], preferred_element_type=F32)
            yield
        else:
            hsum[rows, :] = total + h.astype(F32) * mask()[:, 0:1]


def run_together(steps, lag):
    steps = list(steps)
    live, tick = set(range(len(steps))), 0
    while live:
        for i in sorted(live):
            if tick >= lag * i and next(steps[i], 1) == 1:
                live.discard(i)
        tick += 1


def state_copies(source, target, sems, use, part, rows):
    copies = []
    for i, (a, b) in enumerate(zip(source, target)):
        if i == 1 and use < 2:
            continue
        at = (rows, slice(None)) if i == 1 else (use, rows, slice(None))
        copies.append(pltpu.make_async_copy(a.at[at], b.at[at], sems.at[part, use, i]))
    return copies


def pack_strip(n, levels, k, o, air, out, ni, nj):
    base, cm, cd = side_rows((k - o + 4) % 4, ni, nj)
    for d in range(2):
        copy_rows(out, d * n, air, base + cd * d + cm * (n - 1), -cm, n)
    turn_winds(out, (0, 2 * n), o, levels)


def pack_kernel(n, levels, turn, air, s1, s3, rows, columns, sems):
    o = turn[0, 0]
    feats = air.shape[2]
    width = columns.shape[1] // 2

    def pack(buffer, copies):
        for copy in copies:
            copy.start()
        for copy in copies:
            copy.wait()
        ni, nj = buffer.shape[:2]
        for k, out in ((1, s1), (3, s3)):
            pack_strip(n, levels, k, o, buffer.reshape(ni * nj, feats), out, ni, nj)

    @pl.when(o % 2 == 1)
    def _():
        pack(rows, [pltpu.make_async_copy(air.at[pl.ds(n - 2 if e else 0, 2)], rows.at[pl.ds(2 * e, 2)], sems.at[e])
                    for e in range(2)])

    @pl.when(o % 2 == 0)
    def _():
        pack(columns, [pltpu.make_async_copy(air.at[:, pl.ds(n - width if e else 0, width), :],
                                             columns.at[:, pl.ds(width * e, width), :], sems.at[e])
                       for e in range(2)])


def pack_with_corners_kernel(n, levels, turn, air, h1, h3, order, s0, s2):
    del order
    pack_strip(n, levels, 0, turn[0, 0], air, s0, n, n)
    pack_strip(n, levels, 2, turn[0, 0], air, s2, n, n)
    s0[2 * n : 2 * n + 1, :] = h1[n - 1 : n, :]
    s0[2 * n + 1 : 2 * n + 2, :] = h3[0:1, :]
    s2[2 * n : 2 * n + 1, :] = h1[0:1, :]
    s2[2 * n + 1 : 2 * n + 2, :] = h3[n - 1 : n, :]


def inner_transport_kernel(n, levels, turn, air_rows, moved, own, token, q_one, face_lead, face_sub):
    o = turn[0, 0]
    air = air_rows.reshape(n, n, air_rows.shape[1])
    winds = ((0, 1.0), (1, 1.0))
    transport(air, q_one, face_lead, face_sub, 1, n - 1, winds, levels)
    transport(q_one, moved, face_lead, face_sub, 2, n - 2, winds, levels)
    for k in range(4):
        base, cm, cd = side_rows((k - o + 4) % 4, n)
        for d in range(4):
            copy_rows(own, (k * 4 + d) * n, air_rows, base + cd * d, cm, n)
        turn_winds(own, (k * 4 * n, 4 * n), o, levels)
    token[...] = jnp.zeros_like(token)


def cost_mask(n, cost, mask):
    diagonal = lax.broadcasted_iota(jnp.int32, (n, n), 0) == lax.broadcasted_iota(jnp.int32, (n, n), 1)

    def mask_row(i, carry):
        two = jnp.broadcast_to((cost[pl.ds(i, 1), :] == 2).astype(F32), (n, n))
        column = jnp.sum(jnp.where(diagonal, two, 0.0), axis=1, keepdims=True)
        mask[pl.ds(pl.multiple_of(i * n, 8), n), :] = jnp.broadcast_to(column, (n, LANES))
        return carry

    lax.fori_loop(0, n, mask_row, 0, unroll=8)


PARTS = 2
LAG = 0


def inner_parts(n):
    inner = n - 4
    size = inner // PARTS * n
    return [(part, part * size, size) for part in range(PARTS)]


def inner_network_kernel(n, dest, turn, moved, cost, w_in, w_out, n_o, s_o, g_o, h_o, outgoing, mask_rim,
                         normed, scale, slope, hidden, hsum, mask, sems):
    state, out = (normed, scale, slope, hidden), (n_o, s_o, g_o, h_o)
    feats = moved.shape[2]
    cost_mask(n, cost, mask)
    for k in range(4):
        base, cm, cd = side_rows((k - turn[0, 0] + 4) % 4, n)
        for d in range(2):
            copy_rows(mask_rim, (k * 2 + d) * n, mask, base + cd * d, cm, n)
    copies = []
    steps = []
    for part, start, size in inner_parts(n):
        rows = slice(start, start + size)
        x = lambda start=start, size=size: moved[2 + start // n : 2 + (start + size) // n, :, :].reshape(size, feats)
        m = lambda start=start, size=size: mask[2 * n + start : 2 * n + start + size, :]

        def kept(use, part=part, rows=pl.ds(start, size)):
            for copy in state_copies(state, out, sems, use, part, rows):
                copy.start()
                copies.append(copy)

        steps.append(network_forward(x, m, w_in, w_out, state, hsum, rows, kept))
    run_together(steps, LAG)

    def place(i, carry):
        for j in range(2, n - 2):
            outgoing[pl.ds(dest[i, j], 1), :] = hsum[pl.ds((i - 2) * n + j, 1), :]
        return carry

    lax.fori_loop(2, n - 2, place, 0)
    for copy in copies:
        copy.wait()


def rim_kernel(n, levels, turn, dest, h0, h1, h2, h3, own, mask_rim, w_in, w_out, before,
               n_o, s_o, g_o, h_o, outgoing, sent,
               normed, scale, slope, hidden, sems,
               cells_wide, cells_slim, lead_wide, sub_wide, lead_slim, sub_slim, x_rim, hsum):
    del before
    state, out = (normed, scale, slope, hidden), (n_o, s_o, g_o, h_o)
    o = turn[0, 0]
    halo = (h0, h1, h2, h3)
    sides = [
        [ref.at[k // 2] for ref in (lead_slim, sub_slim)] + [cells_slim.at[k // 2, step] for step in range(3)]
        if k % 2
        else [ref.at[k // 2] for ref in (lead_wide, sub_wide)] + [cells_wide.at[k // 2, step] for step in range(3)]
        for k in range(4)
    ]
    for k, (_, _, src, _, _) in enumerate(sides):
        for depth in range(6):
            d = depth - 2
            row = halo[k][(1 - depth) * n : (2 - depth) * n, :] if d < 0 else own[(k * 4 + d) * n : (k * 4 + d + 1) * n, :]
            src[depth, 0:n, :] = row
            if k % 2 == 0:
                src[depth, n + 2 : n + 8, :] = row[0:6, :]
                src[depth, n + 8 : n + 14, :] = row[n - 6 : n, :]
                for e in range(2):
                    if d < 0:
                        at = 2 * n + k // 2
                        src[depth, n + 1 - e : n + 2 - e, :] = halo[k][at : at + 1, :]
                        at = 2 * n + 1 - k // 2
                        src[depth, n + 14 + e : n + 15 + e, :] = halo[k][at : at + 1, :]
                    else:
                        at = e * n + n - 1 - d
                        src[depth, n + 1 - e : n + 2 - e, :] = halo[(k + 1) % 4][at : at + 1, :]
                        at = e * n + d
                        src[depth, n + 14 + e : n + 15 + e, :] = halo[(k + 3) % 4][at : at + 1, :]
    for k, (lead, sub, src, one, _) in enumerate(sides):
        transport(src, one, lead, sub, 1, 5, SIDE_WINDS[k], levels)
    for k, (lead, sub, _, one, two) in enumerate(sides):
        transport(one, two, lead, sub, 2, 4, SIDE_WINDS[k], levels)
    for k, (_, _, _, _, two) in enumerate(sides):
        for d in range(2):
            at = (k * 2 + d) * n
            x_rim[at : at + n, :] = two[2 + d, 0:n, :]
            if k % 2 == 0:
                x_rim[at : at + 2, :] = two[2 + d, n + 2 : n + 4, :]
                x_rim[at + n - 2 : at + n, :] = two[2 + d, n + 12 : n + 14, :]
    turn_winds(x_rim, (0, 8 * n), (4 - o) % 4, levels)
    copies = []

    def kept(use):
        for copy in state_copies(state, out, sems, use, 0, pl.ds(0, 8 * n)):
            copy.start()
            copies.append(copy)

    halves = ((slice(0, 4 * n), lambda use: None), (slice(4 * n, 8 * n), kept))
    run_together([
        network_forward(lambda r=r: x_rim[r, :], lambda r=r: mask_rim[r, :], w_in, w_out, state, hsum, r, done)
        for r, done in halves
    ], 0)
    for k in range(4):
        (bi, di, mi), (bj, dj, mj) = side_cells((k - o + 4) % 4, n, n)
        skip = 2 * (k % 2)
        for d in range(2):
            for m in range(skip, n - skip):
                at = (k * 2 + d) * n + m
                row = dest[bi + di * d + mi * m, bj + dj * d + mj * m]
                outgoing[pl.ds(row, 1), :] = hsum[at : at + 1, :]
    copies.append(pltpu.make_async_copy(outgoing, sent, sems.at[1, 0, 0]))
    copies[-1].start()
    for copy in copies:
        copy.wait()


def contract_rows(a, b):
    return lax.dot_general(a, b, (((0,), (0,)), ((), ())), preferred_element_type=F32)


def contract_last(a, b):
    return lax.dot_general(a, b, (((1,), (1,)), ((), ())), preferred_element_type=F32)


def network_backward(cot, valid, w_in, w_out, state, err_out, err_in, rows, at, arrived):
    normed, scale, slope = state
    arrived("cotangent")
    cot = cot() * valid
    grad = cot * scale[rows, 0:1]
    for use in (2, 1, 0):
        e = (TAU * grad).astype(BF16)
        err_out[use, at, :] = e
        yield
        back = contract_last(e, w_out[...])
        yield
        arrived(("slope", use))
        inner = (back * slope[use, rows, :]).astype(BF16)
        err_in[use, rows, :] = inner
        yield
        if use > 0:
            d = contract_last(inner, w_in[...])
            yield
            arrived(("normed", use))
            unit = normed[use, rows, :].astype(F32)
            d = scale[rows, 32 * use : 32 * use + 1] * (d - unit * jnp.mean(d * unit, axis=1, keepdims=True))
            grad = (cot if use == 2 else grad) + d


def exchange_order(groups, tiles, tile_first):
    bits = lambda axis, low, count: [(axis, low << b) for b in range(((count // low) - 1).bit_length())]
    plane = [bits("grp", 2, groups), [("tile", 1)]]
    first, second = plane[::-1] if tile_first else plane
    return [("grp", 1)] + first + second + bits("tile", 2, tiles)


def store_pieces(grid_shape, me, order, grad, keep, send):
    groups, tiles = grid_shape
    rows = grad.shape[0] // (groups * tiles)
    for g in range(groups):
        for t in range(tiles):
            p = g * tiles + t
            away = {"grp": me[0] ^ g, "tile": me[1] ^ t}
            at = 0
            for axis, bit in order[1:]:
                at = at * 2 + (away[axis] // bit) % 2

            def store(ref, p=p, at=at):
                for c in range(grad.shape[1] // COL):
                    ref[at, c * rows : (c + 1) * rows, :] = grad[p * rows : (p + 1) * rows, c * COL : (c + 1) * COL]

            pl.when(away["grp"] % 2 == 0)(functools.partial(store, keep))
            pl.when(away["grp"] % 2 == 1)(functools.partial(store, send))


def backward_kernel(n, grid_shape, order, me, turn, cot_in, in_weights, out_weights, in_ni, in_si, in_gi, in_hi,
                    in_nr, in_sr, in_gr, in_hr, keep, send, err_out, h, n_i, s_i, g_i, n_r, s_r, g_r, sems,
                    w_in, w_out, ei_i, ei_r, cot, cot_rim, grad_in):
    o = turn[0, 0]
    parts = inner_parts(n)
    inner = (n - 4) * n
    edge = 2 * n
    pairs = ((in_ni, n_i), (in_nr, n_r)), ((in_gi, g_i), (in_gr, g_r))
    normed = lambda use: [(a.at[use], b.at[use]) for a, b in pairs[0]]
    slope = lambda use: [(a.at[use], b.at[use]) for a, b in pairs[1]]
    plan = [
        ("cotangent", [(out_weights, w_out), (cot_in, cot), (in_si, s_i), (in_sr, s_r)]),
        (("slope", 2), [(in_weights, w_in), *slope(2)]),
        (("normed", 2), normed(2)),
        (("slope", 1), slope(1)),
        (("normed", 1), normed(1)),
        (("slope", 0), slope(0)),
        ("rest", [*normed(0), (in_hi, h.at[:, pl.ds(0, inner), :]), (in_hr, h.at[:, pl.ds(inner, 8 * n), :])]),
    ]
    index = 0
    flight = []

    def start_next():
        nonlocal index
        if plan:
            name, refs = plan.pop(0)
            copies = []
            for source, target in refs:
                copies.append(pltpu.make_async_copy(source, target, sems.at[index]))
                copies[-1].start()
                index += 1
            flight.append((name, copies))

    def arrived(name):
        if flight and flight[0][0] == name:
            for copy in flight.pop(0)[1]:
                copy.wait()
            start_next()

    start_next()
    start_next()
    start_next()
    steps = []
    for part, start, size in parts:
        at = slice(edge + start, edge + start + size)
        j = lax.broadcasted_iota(jnp.int32, (size, 1), 0) % n
        valid = ((j >= 2) & (j < n - 2)).astype(F32)
        rows = slice(start, start + size)
        steps.append(network_backward(lambda at=at: cot[at, :], valid, w_in, w_out, (n_i, s_i, g_i), err_out, ei_i,
                                      rows, rows, arrived))

    def rim_cotangent():
        for k in range(4):
            base, cm, cd = side_rows((k - o + 4) % 4, n)
            for d in range(2):
                copy_rows(cot_rim, (k * 2 + d) * n, cot, base + cd * d, cm, n)
        return cot_rim[...]

    e = lax.broadcasted_iota(jnp.int32, (8 * n, 1), 0)
    m = e % n
    valid = (((e // (2 * n)) % 2 == 0) | ((m >= 2) & (m < n - 2))).astype(F32)
    steps.append(network_backward(rim_cotangent, valid, w_in, w_out, (n_r, s_r, g_r), err_out, ei_r,
                                  slice(0, 8 * n), slice(inner, inner + 8 * n), arrived))
    run_together(steps, LAG)
    arrived("rest")
    flat = lambda ref: ref[...].reshape(ref.shape[0] * ref.shape[1], ref.shape[2])
    grad_in[...] = contract_rows(flat(n_i), flat(ei_i)) + contract_rows(flat(n_r), flat(ei_r))
    store_pieces(grid_shape, me, order, grad_in, keep, send)


def output_gradient_kernel(grid_shape, order, me, err_out, h, keep, send, grad_out):
    flat = lambda ref: ref[...].reshape(ref.shape[0] * ref.shape[1], ref.shape[2])
    grad_out[...] = contract_rows(flat(h), flat(err_out))
    store_pieces(grid_shape, me, order, grad_out, keep, send)


def exchange_sums(keep, send, order, sizes):
    for axis, bit in order:
        keep = keep + lax.ppermute(send, axis, [(i, i ^ bit) for i in range(sizes[axis])])
        if keep.shape[0] > 1:
            half = keep.shape[0] // 2
            keep, send = keep[:half], keep[half:]
    return keep, send


def output_kernel(rows, w_out, out):
    x = rows[...]
    high = x.astype(BF16)
    low = (x - high.astype(F32)).astype(BF16)
    w = w_out[...]
    out[...] = TAU * (jnp.dot(high, w, preferred_element_type=F32) + jnp.dot(low, w, preferred_element_type=F32))


def shift_perm(count, by):
    return [(i, (i + by) % count) for i in range(count)]


def joint_perm(groups, tiles, move):
    return [(g * tiles + t, (lambda h: h[0] * tiles + h[1])(move(g, t))) for g in range(groups) for t in range(tiles)]


def per_device(air_state, cotangent, cost_count, assignment, orientation, weight_in, weight_out):
    groups, tiles = lax.axis_size("grp"), lax.axis_size("tile")
    count = groups * tiles
    n, feats = air_state.shape[0], air_state.shape[2]
    units = weight_in.shape[1]
    levels = feats // V
    cells, rim, inner = n * n, 8 * n, (n - 4) * n
    period = next(c for c in range(1, feats // LANES + 1) if c * LANES % levels == 0)
    shape = jax.ShapeDtypeStruct

    air_rows = air_state.reshape(cells, feats)
    cot_rows = cotangent.reshape(cells, feats)
    both = ("grp", "tile")
    stay = lambda x: pltpu.with_memory_space_constraint(x, pltpu.HBM)

    def state(space, rows):
        return [
            space((3, rows, feats), BF16),
            space((rows, LANES), F32),
            space((3, rows, units), F32),
            space((3, rows, units), BF16),
        ]

    parts = len(inner_parts(n))
    strips = pl.pallas_call(
        functools.partial(pack_kernel, n, levels),
        out_shape=[shape((2 * n, feats), F32)] * 2,
        in_specs=[SMEM, HBM],
        out_specs=[VMEM] * 2,
        scratch_shapes=[
            pltpu.VMEM((4, n, feats), F32),
            pltpu.VMEM((n, 16, feats), F32),
            pltpu.SemaphoreType.DMA((2,)),
        ],
        compiler_params=params(8),
        name="pack_strips",
    )(orientation, stay(air_state))
    from_left = lax.ppermute(strips[1], "grp", shift_perm(groups, 1))
    from_right = lax.ppermute(strips[0], "grp", shift_perm(groups, -1))

    moved, own, token = pl.pallas_call(
        functools.partial(inner_transport_kernel, n, levels),
        out_shape=[
            pltpu.VMEM((n, n, feats), F32),
            pltpu.VMEM((16 * n, feats), F32),
            shape((8, LANES), F32),
        ],
        in_specs=[SMEM, VMEM],
        out_specs=[VMEM] * 3,
        scratch_shapes=[
            pltpu.VMEM((n, n, feats), F32),
            pltpu.VMEM((8, n, period * LANES), F32),
            pltpu.VMEM((7, n, period * LANES), F32),
        ],
        compiler_params=params(10),
        cost_estimate=pl.CostEstimate(flops=60 * cells * feats, bytes_accessed=16 << 20, transcendentals=0),
        name="inner_transport",
    )(orientation, air_rows)

    strips = pl.pallas_call(
        functools.partial(pack_with_corners_kernel, n, levels),
        out_shape=[shape((2 * n + 8, feats), F32)] * 2,
        in_specs=[SMEM] + [VMEM] * 4,
        out_specs=[VMEM] * 2,
        compiler_params=params(8),
        name="pack_strips_corners",
    )(orientation, air_rows, from_left, from_right, token)
    from_above = lax.ppermute(strips[1], "tile", shift_perm(tiles, 1))
    from_below = lax.ppermute(strips[0], "tile", shift_perm(tiles, -1))

    *saved_inner, outgoing, mask_rim = pl.pallas_call(
        functools.partial(inner_network_kernel, n),
        out_shape=[*state(pltpu.HBM, inner), pltpu.VMEM((cells, units), F32), pltpu.VMEM((rim, LANES), F32)],
        in_specs=[SMEM] * 2 + [VMEM] * 4,
        out_specs=[HBM] * 4 + [VMEM] * 2,
        scratch_shapes=[
            *state(pltpu.VMEM, inner),
            pltpu.VMEM((inner, units), F32),
            pltpu.VMEM((cells, LANES), F32),
            pltpu.SemaphoreType.DMA((parts, 3, 4)),
        ],
        compiler_params=params(24),
        cost_estimate=pl.CostEstimate(
            flops=10 * inner * feats * units, bytes_accessed=16 << 20, transcendentals=3 * inner * units
        ),
        name="inner_network",
    )(assignment, orientation, moved, cost_count, weight_in, weight_out)

    wide, slim = n + 16, n
    *saved_rim, _, outgoing = pl.pallas_call(
        functools.partial(rim_kernel, n, levels),
        out_shape=[*state(pltpu.HBM, rim), pltpu.VMEM((cells, units), F32), pltpu.HBM((cells, units), F32)],
        in_specs=[SMEM, SMEM] + [VMEM] * 9,
        out_specs=[HBM] * 4 + [VMEM, HBM],
        input_output_aliases={10: 4},
        scratch_shapes=[*state(pltpu.VMEM, rim), pltpu.SemaphoreType.DMA((2, 3, 4))]
        + [pltpu.VMEM((2, 3, 6, wide, feats), F32), pltpu.VMEM((2, 3, 6, slim, feats), F32)]
        + [pltpu.VMEM((2, rows, wide, period * LANES), F32) for rows in (5, 4)]
        + [pltpu.VMEM((2, rows, slim, period * LANES), F32) for rows in (5, 4)]
        + [pltpu.VMEM((rim, feats), F32), pltpu.VMEM((rim, units), F32)],
        compiler_params=params(26),
        cost_estimate=pl.CostEstimate(
            flops=10 * rim * feats * units, bytes_accessed=20 << 20, transcendentals=3 * rim * units
        ),
        name="rim_columns",
    )(orientation, assignment, from_above, from_left, from_below, from_right, own, mask_rim, weight_in, weight_out, outgoing)

    arrived = lax.all_to_all(
        outgoing.reshape(count, cells // count, units), both, split_axis=0, concat_axis=0, tiled=True
    ).reshape(cells, units)

    me = jnp.stack([lax.axis_index("grp"), lax.axis_index("tile")]).astype(jnp.int32)
    saved = lambda rows: state(pltpu.VMEM, rows)[:3]
    halves = lambda rows, columns: [shape((count // 2, rows // count * (columns // COL), COL), F32)] * 2
    orders = [exchange_order(groups, tiles, tile_first) for tile_first in (False, True)]
    *pieces_in, err_out, hidden = pl.pallas_call(
        functools.partial(backward_kernel, n, (groups, tiles), orders[0]),
        out_shape=[
            *halves(feats, units),
            pltpu.VMEM((3, inner + rim, feats), BF16),
            pltpu.VMEM((3, inner + rim, units), BF16),
        ],
        in_specs=[SMEM, SMEM] + [HBM] * 11,
        out_specs=[VMEM] * 4,
        scratch_shapes=[
            *saved(inner),
            *saved(rim),
            pltpu.SemaphoreType.DMA((19,)),
            pltpu.VMEM((feats, units), BF16),
            pltpu.VMEM((units, feats), BF16),
            pltpu.VMEM((3, inner, units), BF16),
            pltpu.VMEM((3, rim, units), BF16),
            pltpu.VMEM((cells, feats), F32),
            pltpu.VMEM((rim, feats), F32),
            pltpu.VMEM((feats, units), F32),
        ],
        compiler_params=params(36),
        cost_estimate=pl.CostEstimate(flops=16 * cells * feats * units, bytes_accessed=20 << 20, transcendentals=0),
        name="columns_backward",
    )(me, orientation, *map(stay, (cot_rows, weight_in, weight_out, *saved_inner, *saved_rim)))
    pieces_out = pl.pallas_call(
        functools.partial(output_gradient_kernel, (groups, tiles), orders[1]),
        out_shape=halves(units, feats),
        in_specs=[SMEM, VMEM, VMEM],
        out_specs=[VMEM] * 2,
        scratch_shapes=[pltpu.VMEM((units, feats), F32)],
        compiler_params=params(24),
        cost_estimate=pl.CostEstimate(flops=6 * cells * feats * units, bytes_accessed=8 << 20, transcendentals=0),
        name="output_gradient",
    )(me, err_out, hidden)

    flat = lambda part, rows: part.reshape(-1, rows, COL).transpose(1, 0, 2).reshape(-1)
    sizes = {"grp": groups, "tile": tiles}
    far = [pair for pair in orders[0] if pair[0] == "tile" and pair[1] > 1]
    near = len(orders[0]) - len(far)
    sums = [exchange_sums(*pieces, order[:near], sizes) for pieces, order in zip((pieces_in, pieces_out), orders)]
    split = sums[0][0].shape[1]
    keep, _ = exchange_sums(*(jnp.concatenate(pair, axis=1) for pair in zip(*sums)), far, sizes)
    summed_in, summed_out = flat(keep[0, :split], feats // count), flat(keep[0, split:], units // count)

    block = cells // 4
    tendency = pl.pallas_call(
        output_kernel,
        out_shape=shape((cells, feats), F32),
        grid=(cells // block,),
        in_specs=[pl.BlockSpec((block, units), lambda i: (i, 0)), pl.BlockSpec((units, feats), lambda i: (0, 0))],
        out_specs=pl.BlockSpec((block, feats), lambda i: (i, 0)),
        compiler_params=params(32),
        cost_estimate=pl.CostEstimate(flops=4 * cells * feats * units, bytes_accessed=6 << 20, transcendentals=0),
        name="tendency_rows",
    )(arrived, weight_out)
    return (tendency, summed_in, summed_out)


def solution(mesh):
    in_specs = (
        P("tile", "grp", None),
        P("tile", "grp", None),
        P("tile", "grp"),
        P("tile", "grp"),
        P("tile", "grp"),
        P(),
        P(),
    )
    out_specs = (P(("grp", "tile"), None), P(("grp", "tile")), P(("grp", "tile")))
    return jax.shard_map(
        per_device, mesh=mesh, in_specs=in_specs, out_specs=out_specs, check_vma=False
    )
```

```python
import functools
import jax
import jax.numpy as jnp
from jax import lax
from jax.experimental import pallas as pl
from jax.experimental.pallas import tpu as pltpu
from jax.sharding import PartitionSpec as P

V = 8
TAU = 0.5
COURANT = 0.1
EPS = 1e-06
LANES = 128
F32 = jnp.float32
BF16 = jnp.bfloat16
SIDE_WINDS = (((0, 1.0), (1, 1.0)), ((1, 1.0), (0, -1.0)), ((0, -1.0), (1, -1.0)), ((1, -1.0), (0, 1.0)))

VMEM = pl.BlockSpec(memory_space=pltpu.VMEM)
HBM = pl.BlockSpec(memory_space=pltpu.HBM)
SMEM = pl.BlockSpec(memory_space=pltpu.SMEM)


def params(mib):
    return pltpu.CompilerParams(vmem_limit_bytes=mib * 1024 * 1024)


def side_cells(k, n):
    pick = lambda a, b, c, e: jnp.where(k == 0, a, jnp.where(k == 1, b, jnp.where(k == 2, c, e)))
    return (pick(0, n - 1, n - 1, 0), pick(1, 0, -1, 0), pick(0, -1, 0, 1)), (
        pick(0, 0, n - 1, n - 1), pick(0, 1, 0, -1), pick(1, 0, -1, 0))


def side_rows(k, n):
    (bi, di, mi), (bj, dj, mj) = side_cells(k, n)
    return bi * n + bj, mi * n + mj, di * n + dj


def turn_winds(ref, rows, quarter, levels):
    start, size = rows
    width = -(-2 * levels // LANES) * LANES
    w = ref[start : start + size, 0:width]
    lane = lax.broadcasted_iota(jnp.int32, w.shape, 1)
    swapped = jnp.where(lane < levels, pltpu.roll(w, width - levels, 1), pltpu.roll(w, levels, 1))
    cos = ((quarter == 0).astype(F32) - (quarter == 2).astype(F32))
    sin = ((quarter == 1).astype(F32) - (quarter == 3).astype(F32))
    turned = w * cos + swapped * jnp.where(lane < levels, -sin, sin)
    ref[start : start + size, 0:width] = jnp.where(lane < 2 * levels, turned, w)


def copy_rows(dst, dst_base, src, cell, step, count):
    def body(s, carry):
        dst[pl.ds(dst_base + s, 1), :] = src[pl.ds(cell + s * step, 1), :]
        return carry

    lax.fori_loop(0, count, body, 0, unroll=8)


def wind_row(src, a, which, levels):
    start = which * levels
    chunk, off = start // LANES, start % LANES
    first = src[a, :, chunk * LANES : (chunk + 1) * LANES]
    if off == 0:
        return first
    second = src[a, :, (chunk + 1) * LANES : (chunk + 2) * LANES]
    lane = lax.broadcasted_iota(jnp.int32, first.shape, 1)
    shift = LANES - off
    return jnp.where(lane < shift, pltpu.roll(first, shift, 1), pltpu.roll(second, shift, 1))


def repeat_levels(face, levels, chunks):
    lane = lax.broadcasted_iota(jnp.int32, face.shape, 1)
    rolls = {0: face}
    out = []
    for c in range(chunks):
        result, at = None, 0
        while at < LANES:
            index = (c * LANES + at) % levels
            shift = (at - index) % LANES
            if shift not in rolls:
                rolls[shift] = pltpu.roll(face, shift, 1)
            result = rolls[shift] if result is None else jnp.where(lane < at, result, rolls[shift])
            at += levels - index
        out.append(result)
    return out


def transport(src, dst, face_lead, face_sub, lo, hi, winds, levels):
    (lead, lead_sign), (sub, sub_sign) = winds
    size, feats = src.shape[1], src.shape[2]
    chunks = feats // LANES
    period = face_lead.shape[2] // LANES
    block = next(b for b in range(face_sub.shape[0], 0, -1) if (hi - lo) % b == 0)

    def store(ref, at, face):
        for c, part in enumerate(repeat_levels(face, levels, period)):
            ref[at, :, c * LANES : (c + 1) * LANES] = part

    def body(b, carry):
        first = lo + b * block
        for r in range(block + 1):
            wind = wind_row(src, first - 1 + r, lead, levels) + wind_row(src, first + r, lead, levels)
            store(face_lead, r, (0.5 * COURANT * lead_sign) * wind)
        for r in range(block):
            wind = wind_row(src, first + r, sub, levels)
            store(face_sub, r, (0.5 * COURANT * sub_sign) * (wind + pltpu.roll(wind, size - 1, 0)))
        for c3 in range(period):
            lanes3 = slice(c3 * LANES, (c3 + 1) * LANES)
            group = [slice(c * LANES, (c + 1) * LANES) for c in range(c3, chunks, period)]
            face = face_lead[0, :, lanes3]
            q = [src[first, :, lanes] for lanes in group]
            before = [face * jnp.where(face > 0.0, src[first - 1, :, lanes], here) for lanes, here in zip(group, q)]
            for r in range(block):
                face, side = face_lead[r + 1, :, lanes3], face_sub[r, :, lanes3]
                for i, lanes in enumerate(group):
                    ahead = src[first + r + 1, :, lanes]
                    flux = face * jnp.where(face > 0.0, q[i], ahead)
                    cross = side * jnp.where(side > 0.0, q[i], pltpu.roll(q[i], size - 1, 0))
                    dst[first + r, :, lanes] = q[i] - ((flux - before[i]) + (cross - pltpu.roll(cross, 1, 0)))
                    q[i], before[i] = ahead, flux
        return carry

    if hi - lo == block:
        body(0, 0)
    else:
        lax.fori_loop(0, (hi - lo) // block, body, 0)


def network_forward(x, mask, w_in, w_out, state, hsum, rows, kept):
    normed, scale, slope, hidden = state
    x, total = x(), None
    for use in range(3):
        inv = lax.rsqrt(jnp.mean(x * x, axis=1, keepdims=True) + EPS)
        unit = (x * inv).astype(BF16)
        normed[use, rows, :] = unit
        if use == 0:
            packed = mask()
            lane = lax.broadcasted_iota(jnp.int32, packed.shape, 1)
        else:
            packed = jnp.where(lane < 32 * use, packed, inv)
        yield
        p = jnp.dot(unit, w_in[...], preferred_element_type=F32)
        yield
        s = 0.5 + 0.5 * jnp.tanh(0.5 * p)
        silu = p * s
        slope[use, rows, :] = s + silu * (1.0 - s)
        h = silu.astype(BF16)
        hidden[use, rows, :] = h
        if use == 2:
            scale[rows, :] = packed
        kept(use)
        if use < 2:
            total = h.astype(F32) if use == 0 else total + h.astype(F32)
            yield
            x = x + TAU * jnp.dot(h, w_out[...], preferred_element_type=F32)
            yield
        else:
            hsum[rows, :] = total + h.astype(F32) * mask()[:, 0:1]


def run_together(steps, lag):
    steps = list(steps)
    live, tick = set(range(len(steps))), 0
    while live:
        for i in sorted(live):
            if tick >= lag * i and next(steps[i], 1) == 1:
                live.discard(i)
        tick += 1


def state_copies(source, target, sems, use, part, rows):
    copies = []
    for i, (a, b) in enumerate(zip(source, target)):
        if i == 1 and use < 2:
            continue
        at = (rows, slice(None)) if i == 1 else (use, rows, slice(None))
        copies.append(pltpu.make_async_copy(a.at[at], b.at[at], sems.at[part, use, i]))
    return copies


def pack_strip(n, levels, k, o, air, out):
    base, cm, cd = side_rows((k - o + 4) % 4, n)
    for d in range(2):
        copy_rows(out, d * n, air, base + cd * d + cm * (n - 1), -cm, n)
    turn_winds(out, (0, 2 * n), o, levels)


def pack_kernel(n, levels, turn, air, s1, s3):
    pack_strip(n, levels, 1, turn[0, 0], air, s1)
    pack_strip(n, levels, 3, turn[0, 0], air, s3)


def pack_with_corners_kernel(n, levels, turn, air, h1, h3, order, s0, s2):
    del order
    pack_strip(n, levels, 0, turn[0, 0], air, s0)
    pack_strip(n, levels, 2, turn[0, 0], air, s2)
    s0[2 * n : 2 * n + 1, :] = h1[n - 1 : n, :]
    s0[2 * n + 1 : 2 * n + 2, :] = h3[0:1, :]
    s2[2 * n : 2 * n + 1, :] = h1[0:1, :]
    s2[2 * n + 1 : 2 * n + 2, :] = h3[n - 1 : n, :]


def inner_transport_kernel(n, levels, turn, air_rows, moved, own, token, q_one, face_lead, face_sub):
    o = turn[0, 0]
    air = air_rows.reshape(n, n, air_rows.shape[1])
    winds = ((0, 1.0), (1, 1.0))
    transport(air, q_one, face_lead, face_sub, 1, n - 1, winds, levels)
    transport(q_one, moved, face_lead, face_sub, 2, n - 2, winds, levels)
    for k in range(4):
        base, cm, cd = side_rows((k - o + 4) % 4, n)
        for d in range(4):
            copy_rows(own, (k * 4 + d) * n, air_rows, base + cd * d, cm, n)
        turn_winds(own, (k * 4 * n, 4 * n), o, levels)
    token[...] = jnp.zeros_like(token)


def cost_mask(n, cost, mask):
    diagonal = lax.broadcasted_iota(jnp.int32, (n, n), 0) == lax.broadcasted_iota(jnp.int32, (n, n), 1)

    def mask_row(i, carry):
        two = jnp.broadcast_to((cost[pl.ds(i, 1), :] == 2).astype(F32), (n, n))
        column = jnp.sum(jnp.where(diagonal, two, 0.0), axis=1, keepdims=True)
        mask[pl.ds(pl.multiple_of(i * n, 8), n), :] = jnp.broadcast_to(column, (n, LANES))
        return carry

    lax.fori_loop(0, n, mask_row, 0, unroll=8)


PARTS = 2
LAG = 0


def inner_parts(n):
    inner = n - 4
    size = inner // PARTS * n
    return [(part, part * size, size) for part in range(PARTS)]


def inner_network_kernel(n, dest, turn, moved, cost, w_in, w_out, n_o, s_o, g_o, h_o, outgoing, mask_rim,
                         normed, scale, slope, hidden, hsum, mask, sems):
    state, out = (normed, scale, slope, hidden), (n_o, s_o, g_o, h_o)
    feats = moved.shape[2]
    cost_mask(n, cost, mask)
    for k in range(4):
        base, cm, cd = side_rows((k - turn[0, 0] + 4) % 4, n)
        for d in range(2):
            copy_rows(mask_rim, (k * 2 + d) * n, mask, base + cd * d, cm, n)
    copies = []
    steps = []
    for part, start, size in inner_parts(n):
        rows = slice(start, start + size)
        x = lambda start=start, size=size: moved[2 + start // n : 2 + (start + size) // n, :, :].reshape(size, feats)
        m = lambda start=start, size=size: mask[2 * n + start : 2 * n + start + size, :]

        def kept(use, part=part, rows=pl.ds(start, size)):
            for copy in state_copies(state, out, sems, use, part, rows):
                copy.start()
                copies.append(copy)

        steps.append(network_forward(x, m, w_in, w_out, state, hsum, rows, kept))
    run_together(steps, LAG)

    def place(i, carry):
        for j in range(2, n - 2):
            outgoing[pl.ds(dest[i, j], 1), :] = hsum[pl.ds((i - 2) * n + j, 1), :]
        return carry

    lax.fori_loop(2, n - 2, place, 0)
    for copy in copies:
        copy.wait()


def rim_kernel(n, levels, turn, dest, h0, h1, h2, h3, own, mask_rim, w_in, w_out, before,
               n_o, s_o, g_o, h_o, outgoing, sent,
               normed, scale, slope, hidden, sems,
               cells_wide, cells_slim, lead_wide, sub_wide, lead_slim, sub_slim, x_rim, hsum):
    del before
    state, out = (normed, scale, slope, hidden), (n_o, s_o, g_o, h_o)
    o = turn[0, 0]
    halo = (h0, h1, h2, h3)
    wide = [lead_wide, sub_wide] + [cells_wide.at[step] for step in range(3)]
    slim = [lead_slim, sub_slim] + [cells_slim.at[step] for step in range(3)]
    for k in range(4):
        lead, sub, src, one, two = slim if k % 2 else wide
        for depth in range(6):
            d = depth - 2
            row = halo[k][(1 - depth) * n : (2 - depth) * n, :] if d < 0 else own[(k * 4 + d) * n : (k * 4 + d + 1) * n, :]
            src[depth, 0:n, :] = row
            if k % 2 == 0:
                src[depth, n + 2 : n + 8, :] = row[0:6, :]
                src[depth, n + 8 : n + 14, :] = row[n - 6 : n, :]
                for e in range(2):
                    if d < 0:
                        at = 2 * n + k // 2
                        src[depth, n + 1 - e : n + 2 - e, :] = halo[k][at : at + 1, :]
                        at = 2 * n + 1 - k // 2
                        src[depth, n + 14 + e : n + 15 + e, :] = halo[k][at : at + 1, :]
                    else:
                        at = e * n + n - 1 - d
                        src[depth, n + 1 - e : n + 2 - e, :] = halo[(k + 1) % 4][at : at + 1, :]
                        at = e * n + d
                        src[depth, n + 14 + e : n + 15 + e, :] = halo[(k + 3) % 4][at : at + 1, :]
        transport(src, one, lead, sub, 1, 5, SIDE_WINDS[k], levels)
        transport(one, two, lead, sub, 2, 4, SIDE_WINDS[k], levels)
        for d in range(2):
            at = (k * 2 + d) * n
            x_rim[at : at + n, :] = two[2 + d, 0:n, :]
            if k % 2 == 0:
                x_rim[at : at + 2, :] = two[2 + d, n + 2 : n + 4, :]
                x_rim[at + n - 2 : at + n, :] = two[2 + d, n + 12 : n + 14, :]
    turn_winds(x_rim, (0, 8 * n), (4 - o) % 4, levels)
    copies = []

    def kept(use):
        for copy in state_copies(state, out, sems, use, 0, pl.ds(0, 8 * n)):
            copy.start()
            copies.append(copy)

    halves = ((slice(0, 4 * n), lambda use: None), (slice(4 * n, 8 * n), kept))
    run_together([
        network_forward(lambda r=r: x_rim[r, :], lambda r=r: mask_rim[r, :], w_in, w_out, state, hsum, r, done)
        for r, done in halves
    ], 0)
    for k in range(4):
        (bi, di, mi), (bj, dj, mj) = side_cells((k - o + 4) % 4, n)
        skip = 2 * (k % 2)
        for d in range(2):
            for m in range(skip, n - skip):
                at = (k * 2 + d) * n + m
                row = dest[bi + di * d + mi * m, bj + dj * d + mj * m]
                outgoing[pl.ds(row, 1), :] = hsum[at : at + 1, :]
    copies.append(pltpu.make_async_copy(outgoing, sent, sems.at[1, 0, 0]))
    copies[-1].start()
    for copy in copies:
        copy.wait()


def contract_rows(a, b):
    return lax.dot_general(a, b, (((0,), (0,)), ((), ())), preferred_element_type=F32)


def contract_last(a, b):
    return lax.dot_general(a, b, (((1,), (1,)), ((), ())), preferred_element_type=F32)


def network_backward(cot, valid, w_in, w_out, state, err_out, err_in, rows, at, arrived):
    normed, scale, slope = state
    arrived("cotangent")
    cot = cot() * valid
    grad = cot * scale[rows, 0:1]
    for use in (2, 1, 0):
        e = (TAU * grad).astype(BF16)
        err_out[use, at, :] = e
        yield
        back = contract_last(e, w_out[...])
        yield
        arrived(("slope", use))
        inner = (back * slope[use, rows, :]).astype(BF16)
        err_in[use, rows, :] = inner
        yield
        if use > 0:
            d = contract_last(inner, w_in[...])
            yield
            arrived(("normed", use))
            unit = normed[use, rows, :].astype(F32)
            d = scale[rows, 32 * use : 32 * use + 1] * (d - unit * jnp.mean(d * unit, axis=1, keepdims=True))
            grad = (cot if use == 2 else grad) + d


def exchange_order(groups, tiles, tile_first):
    bits = lambda axis, low, count: [(axis, low << b) for b in range(((count // low) - 1).bit_length())]
    plane = [bits("grp", 2, groups), [("tile", 1)]]
    first, second = plane[::-1] if tile_first else plane
    return [("grp", 1)] + first + second + bits("tile", 2, tiles)


def store_pieces(grid_shape, me, order, grad, keep, send):
    groups, tiles = grid_shape
    rows = grad.shape[0] // (groups * tiles)
    for g in range(groups):
        for t in range(tiles):
            p = g * tiles + t
            away = {"grp": me[0] ^ g, "tile": me[1] ^ t}
            at = 0
            for axis, bit in order[1:]:
                at = at * 2 + (away[axis] // bit) % 2

            def store(ref, p=p, at=at):
                chunks = grad.shape[1] // LANES
                for c in range(chunks):
                    part = grad[p * rows : (p + 1) * rows, c * LANES : (c + 1) * LANES]
                    ref[at, pl.ds(c, rows, stride=chunks), :] = part

            pl.when(away["grp"] % 2 == 0)(functools.partial(store, keep))
            pl.when(away["grp"] % 2 == 1)(functools.partial(store, send))


def backward_kernel(n, grid_shape, order, me, turn, cot_in, in_weights, out_weights, in_ni, in_si, in_gi, in_hi,
                    in_nr, in_sr, in_gr, in_hr, keep, send, err_out, h, n_i, s_i, g_i, n_r, s_r, g_r, sems,
                    w_in, w_out, ei_i, ei_r, cot, cot_rim, grad_in):
    o = turn[0, 0]
    parts = inner_parts(n)
    inner = (n - 4) * n
    edge = 2 * n
    pairs = ((in_ni, n_i), (in_nr, n_r)), ((in_gi, g_i), (in_gr, g_r))
    normed = lambda use: [(a.at[use], b.at[use]) for a, b in pairs[0]]
    slope = lambda use: [(a.at[use], b.at[use]) for a, b in pairs[1]]
    plan = [
        ("cotangent", [(out_weights, w_out), (cot_in, cot), (in_si, s_i), (in_sr, s_r)]),
        (("slope", 2), [(in_weights, w_in), *slope(2)]),
        (("normed", 2), normed(2)),
        (("slope", 1), slope(1)),
        (("normed", 1), normed(1)),
        (("slope", 0), slope(0)),
        ("rest", [*normed(0), (in_hi, h.at[:, pl.ds(0, inner), :]), (in_hr, h.at[:, pl.ds(inner, 8 * n), :])]),
    ]
    index = 0
    flight = []

    def start_next():
        nonlocal index
        if plan:
            name, refs = plan.pop(0)
            copies = []
            for source, target in refs:
                copies.append(pltpu.make_async_copy(source, target, sems.at[index]))
                copies[-1].start()
                index += 1
            flight.append((name, copies))

    def arrived(name):
        if flight and flight[0][0] == name:
            for copy in flight.pop(0)[1]:
                copy.wait()
            start_next()

    start_next()
    start_next()
    start_next()
    steps = []
    for part, start, size in parts:
        at = slice(edge + start, edge + start + size)
        j = lax.broadcasted_iota(jnp.int32, (size, 1), 0) % n
        valid = ((j >= 2) & (j < n - 2)).astype(F32)
        rows = slice(start, start + size)
        steps.append(network_backward(lambda at=at: cot[at, :], valid, w_in, w_out, (n_i, s_i, g_i), err_out, ei_i,
                                      rows, rows, arrived))

    def rim_cotangent():
        for k in range(4):
            base, cm, cd = side_rows((k - o + 4) % 4, n)
            for d in range(2):
                copy_rows(cot_rim, (k * 2 + d) * n, cot, base + cd * d, cm, n)
        return cot_rim[...]

    e = lax.broadcasted_iota(jnp.int32, (8 * n, 1), 0)
    m = e % n
    valid = (((e // (2 * n)) % 2 == 0) | ((m >= 2) & (m < n - 2))).astype(F32)
    steps.append(network_backward(rim_cotangent, valid, w_in, w_out, (n_r, s_r, g_r), err_out, ei_r,
                                  slice(0, 8 * n), slice(inner, inner + 8 * n), arrived))
    run_together(steps, LAG)
    arrived("rest")
    flat = lambda ref: ref[...].reshape(ref.shape[0] * ref.shape[1], ref.shape[2])
    grad_in[...] = contract_rows(flat(n_i), flat(ei_i)) + contract_rows(flat(n_r), flat(ei_r))
    store_pieces(grid_shape, me, order, grad_in, keep, send)


def output_gradient_kernel(grid_shape, order, me, err_out, h, keep, send, grad_out):
    flat = lambda ref: ref[...].reshape(ref.shape[0] * ref.shape[1], ref.shape[2])
    grad_out[...] = contract_rows(flat(h), flat(err_out))
    store_pieces(grid_shape, me, order, grad_out, keep, send)


def exchange_sums(keep, send, order, sizes):
    for axis, bit in order:
        keep = keep + lax.ppermute(send, axis, [(i, i ^ bit) for i in range(sizes[axis])])
        half = keep.shape[0] // 2
        keep, send = keep[:half], keep[half:]
    return keep, send


def output_kernel(rows, w_out, out):
    x = rows[...]
    high = x.astype(BF16)
    low = (x - high.astype(F32)).astype(BF16)
    w = w_out[...]
    out[...] = TAU * (jnp.dot(high, w, preferred_element_type=F32) + jnp.dot(low, w, preferred_element_type=F32))


def shift_perm(count, by):
    return [(i, (i + by) % count) for i in range(count)]


def joint_perm(groups, tiles, move):
    return [(g * tiles + t, (lambda h: h[0] * tiles + h[1])(move(g, t))) for g in range(groups) for t in range(tiles)]


def per_device(air_state, cotangent, cost_count, assignment, orientation, weight_in, weight_out):
    groups, tiles = lax.axis_size("grp"), lax.axis_size("tile")
    count = groups * tiles
    n, feats = air_state.shape[0], air_state.shape[2]
    units = weight_in.shape[1]
    levels = feats // V
    cells, rim, inner = n * n, 8 * n, (n - 4) * n
    period = next(c for c in range(1, feats // LANES + 1) if c * LANES % levels == 0)
    shape = jax.ShapeDtypeStruct

    air_rows = air_state.reshape(cells, feats)
    cot_rows = cotangent.reshape(cells, feats)
    both = ("grp", "tile")
    stay = lambda x: pltpu.with_memory_space_constraint(x, pltpu.HBM)

    def state(space, rows):
        return [
            space((3, rows, feats), BF16),
            space((rows, LANES), F32),
            space((3, rows, units), F32),
            space((3, rows, units), BF16),
        ]

    parts = len(inner_parts(n))
    strips = pl.pallas_call(
        functools.partial(pack_kernel, n, levels),
        out_shape=[shape((2 * n, feats), F32)] * 2,
        in_specs=[SMEM, VMEM],
        out_specs=[VMEM] * 2,
        compiler_params=params(8),
        name="pack_strips",
    )(orientation, air_rows)
    from_left = lax.ppermute(strips[1], "grp", shift_perm(groups, 1))
    from_right = lax.ppermute(strips[0], "grp", shift_perm(groups, -1))

    moved, own, token = pl.pallas_call(
        functools.partial(inner_transport_kernel, n, levels),
        out_shape=[
            pltpu.VMEM((n, n, feats), F32),
            pltpu.VMEM((16 * n, feats), F32),
            shape((8, LANES), F32),
        ],
        in_specs=[SMEM, VMEM],
        out_specs=[VMEM] * 3,
        scratch_shapes=[
            pltpu.VMEM((n, n, feats), F32),
            pltpu.VMEM((8, n, period * LANES), F32),
            pltpu.VMEM((7, n, period * LANES), F32),
        ],
        compiler_params=params(10),
        cost_estimate=pl.CostEstimate(flops=60 * cells * feats, bytes_accessed=16 << 20, transcendentals=0),
        name="inner_transport",
    )(orientation, air_rows)

    strips = pl.pallas_call(
        functools.partial(pack_with_corners_kernel, n, levels),
        out_shape=[shape((2 * n + 8, feats), F32)] * 2,
        in_specs=[SMEM] + [VMEM] * 4,
        out_specs=[VMEM] * 2,
        compiler_params=params(8),
        name="pack_strips_corners",
    )(orientation, air_rows, from_left, from_right, token)
    from_above = lax.ppermute(strips[1], "tile", shift_perm(tiles, 1))
    from_below = lax.ppermute(strips[0], "tile", shift_perm(tiles, -1))

    *saved_inner, outgoing, mask_rim = pl.pallas_call(
        functools.partial(inner_network_kernel, n),
        out_shape=[*state(pltpu.HBM, inner), pltpu.VMEM((cells, units), F32), pltpu.VMEM((rim, LANES), F32)],
        in_specs=[SMEM] * 2 + [VMEM] * 4,
        out_specs=[HBM] * 4 + [VMEM] * 2,
        scratch_shapes=[
            *state(pltpu.VMEM, inner),
            pltpu.VMEM((inner, units), F32),
            pltpu.VMEM((cells, LANES), F32),
            pltpu.SemaphoreType.DMA((parts, 3, 4)),
        ],
        compiler_params=params(24),
        cost_estimate=pl.CostEstimate(
            flops=10 * inner * feats * units, bytes_accessed=16 << 20, transcendentals=3 * inner * units
        ),
        name="inner_network",
    )(assignment, orientation, moved, cost_count, weight_in, weight_out)

    wide, slim = n + 16, n
    *saved_rim, _, outgoing = pl.pallas_call(
        functools.partial(rim_kernel, n, levels),
        out_shape=[*state(pltpu.HBM, rim), pltpu.VMEM((cells, units), F32), pltpu.HBM((cells, units), F32)],
        in_specs=[SMEM, SMEM] + [VMEM] * 9,
        out_specs=[HBM] * 4 + [VMEM, HBM],
        input_output_aliases={10: 4},
        scratch_shapes=[*state(pltpu.VMEM, rim), pltpu.SemaphoreType.DMA((2, 3, 4))]
        + [pltpu.VMEM((3, 6, wide, feats), F32), pltpu.VMEM((3, 6, slim, feats), F32)]
        + [pltpu.VMEM((rows, wide, period * LANES), F32) for rows in (5, 4)]
        + [pltpu.VMEM((rows, slim, period * LANES), F32) for rows in (5, 4)]
        + [pltpu.VMEM((rim, feats), F32), pltpu.VMEM((rim, units), F32)],
        compiler_params=params(16),
        cost_estimate=pl.CostEstimate(
            flops=10 * rim * feats * units, bytes_accessed=20 << 20, transcendentals=3 * rim * units
        ),
        name="rim_columns",
    )(orientation, assignment, from_above, from_left, from_below, from_right, own, mask_rim, weight_in, weight_out, outgoing)

    arrived = lax.all_to_all(
        outgoing.reshape(count, cells // count, units), both, split_axis=0, concat_axis=0, tiled=True
    ).reshape(cells, units)

    me = jnp.stack([lax.axis_index("grp"), lax.axis_index("tile")]).astype(jnp.int32)
    saved = lambda rows: state(pltpu.VMEM, rows)[:3]
    halves = [shape((count // 2, feats * units // count // LANES, LANES), F32)] * 2
    orders = [exchange_order(groups, tiles, tile_first) for tile_first in (False, True)]
    *pieces_in, err_out, hidden = pl.pallas_call(
        functools.partial(backward_kernel, n, (groups, tiles), orders[0]),
        out_shape=[
            *halves,
            pltpu.VMEM((3, inner + rim, feats), BF16),
            pltpu.VMEM((3, inner + rim, units), BF16),
        ],
        in_specs=[SMEM, SMEM] + [HBM] * 11,
        out_specs=[VMEM] * 4,
        scratch_shapes=[
            *saved(inner),
            *saved(rim),
            pltpu.SemaphoreType.DMA((19,)),
            pltpu.VMEM((feats, units), BF16),
            pltpu.VMEM((units, feats), BF16),
            pltpu.VMEM((3, inner, units), BF16),
            pltpu.VMEM((3, rim, units), BF16),
            pltpu.VMEM((cells, feats), F32),
            pltpu.VMEM((rim, feats), F32),
            pltpu.VMEM((feats, units), F32),
        ],
        compiler_params=params(36),
        cost_estimate=pl.CostEstimate(flops=16 * cells * feats * units, bytes_accessed=20 << 20, transcendentals=0),
        name="columns_backward",
    )(me, orientation, *map(stay, (cot_rows, weight_in, weight_out, *saved_inner, *saved_rim)))
    pieces_out = pl.pallas_call(
        functools.partial(output_gradient_kernel, (groups, tiles), orders[1]),
        out_shape=halves,
        in_specs=[SMEM, VMEM, VMEM],
        out_specs=[VMEM] * 2,
        scratch_shapes=[pltpu.VMEM((units, feats), F32)],
        compiler_params=params(24),
        cost_estimate=pl.CostEstimate(flops=6 * cells * feats * units, bytes_accessed=8 << 20, transcendentals=0),
        name="output_gradient",
    )(me, err_out, hidden)

    sizes = {"grp": groups, "tile": tiles}
    far = [pair for pair in orders[0] if pair[0] == "tile" and pair[1] > 1]
    near = len(orders[0]) - len(far)
    sums = [exchange_sums(*pieces, order[:near], sizes) for pieces, order in zip((pieces_in, pieces_out), orders)]
    split = sums[0][0].shape[1]
    keep, send = (jnp.concatenate(pair, axis=1) for pair in zip(*sums))
    keep, send = exchange_sums(keep, send, far[:-1], sizes)

    block = cells // 4
    tendency = pl.pallas_call(
        output_kernel,
        out_shape=shape((cells, feats), F32),
        grid=(cells // block,),
        in_specs=[pl.BlockSpec((block, units), lambda i: (i, 0)), pl.BlockSpec((units, feats), lambda i: (0, 0))],
        out_specs=pl.BlockSpec((block, feats), lambda i: (i, 0)),
        compiler_params=params(32),
        cost_estimate=pl.CostEstimate(flops=4 * cells * feats * units, bytes_accessed=6 << 20, transcendentals=0),
        name="tendency_rows",
    )(arrived, weight_out)
    (axis, bit), = far[-1:]
    arriving = lax.ppermute(send, axis, [(i, i ^ bit) for i in range(sizes[axis])])
    keep, tendency = lax.optimization_barrier((keep, tendency))
    keep = keep + arriving
    summed_in, summed_out = keep[0, :split].reshape(-1), keep[0, split:].reshape(-1)
    return (tendency, summed_in, summed_out)


def solution(mesh):
    in_specs = (
        P("tile", "grp", None),
        P("tile", "grp", None),
        P("tile", "grp"),
        P("tile", "grp"),
        P("tile", "grp"),
        P(),
        P(),
    )
    out_specs = (P(("grp", "tile"), None), P(("grp", "tile")), P(("grp", "tile")))
    return jax.shard_map(
        per_device, mesh=mesh, in_specs=in_specs, out_specs=out_specs, check_vma=False
    )
```

```python
import functools
import jax
import jax.numpy as jnp
from jax import lax
from jax.experimental import pallas as pl
from jax.experimental.pallas import tpu as pltpu
from jax.sharding import PartitionSpec as P

V = 8
TAU = 0.5
COURANT = 0.1
EPS = 1e-06
LANES = 128
F32 = jnp.float32
BF16 = jnp.bfloat16
SIDE_WINDS = (((0, 1.0), (1, 1.0)), ((1, 1.0), (0, -1.0)), ((0, -1.0), (1, -1.0)), ((1, -1.0), (0, 1.0)))

VMEM = pl.BlockSpec(memory_space=pltpu.VMEM)
HBM = pl.BlockSpec(memory_space=pltpu.HBM)
SMEM = pl.BlockSpec(memory_space=pltpu.SMEM)


def params(mib):
    return pltpu.CompilerParams(vmem_limit_bytes=mib * 1024 * 1024)


def side_cells(k, n):
    pick = lambda a, b, c, e: jnp.where(k == 0, a, jnp.where(k == 1, b, jnp.where(k == 2, c, e)))
    return (pick(0, n - 1, n - 1, 0), pick(1, 0, -1, 0), pick(0, -1, 0, 1)), (
        pick(0, 0, n - 1, n - 1), pick(0, 1, 0, -1), pick(1, 0, -1, 0))


def side_rows(k, n):
    (bi, di, mi), (bj, dj, mj) = side_cells(k, n)
    return bi * n + bj, mi * n + mj, di * n + dj


def turn_winds(ref, rows, quarter, levels):
    start, size = rows
    width = -(-2 * levels // LANES) * LANES
    w = ref[start : start + size, 0:width]
    lane = lax.broadcasted_iota(jnp.int32, w.shape, 1)
    swapped = jnp.where(lane < levels, pltpu.roll(w, width - levels, 1), pltpu.roll(w, levels, 1))
    cos = ((quarter == 0).astype(F32) - (quarter == 2).astype(F32))
    sin = ((quarter == 1).astype(F32) - (quarter == 3).astype(F32))
    turned = w * cos + swapped * jnp.where(lane < levels, -sin, sin)
    ref[start : start + size, 0:width] = jnp.where(lane < 2 * levels, turned, w)


def copy_rows(dst, dst_base, src, cell, step, count):
    def body(s, carry):
        dst[pl.ds(dst_base + s, 1), :] = src[pl.ds(cell + s * step, 1), :]
        return carry

    lax.fori_loop(0, count, body, 0, unroll=8)


def wind_row(src, a, which, levels):
    start = which * levels
    chunk, off = start // LANES, start % LANES
    first = src[a, :, chunk * LANES : (chunk + 1) * LANES]
    if off == 0:
        return first
    second = src[a, :, (chunk + 1) * LANES : (chunk + 2) * LANES]
    lane = lax.broadcasted_iota(jnp.int32, first.shape, 1)
    shift = LANES - off
    return jnp.where(lane < shift, pltpu.roll(first, shift, 1), pltpu.roll(second, shift, 1))


def repeat_levels(face, levels, chunks):
    lane = lax.broadcasted_iota(jnp.int32, face.shape, 1)
    rolls = {0: face}
    out = []
    for c in range(chunks):
        result, at = None, 0
        while at < LANES:
            index = (c * LANES + at) % levels
            shift = (at - index) % LANES
            if shift not in rolls:
                rolls[shift] = pltpu.roll(face, shift, 1)
            result = rolls[shift] if result is None else jnp.where(lane < at, result, rolls[shift])
            at += levels - index
        out.append(result)
    return out


def transport(src, dst, face_lead, face_sub, lo, hi, winds, levels):
    (lead, lead_sign), (sub, sub_sign) = winds
    size, feats = src.shape[1], src.shape[2]
    chunks = feats // LANES
    period = face_lead.shape[2] // LANES
    block = next(b for b in range(face_sub.shape[0], 0, -1) if (hi - lo) % b == 0)

    def store(ref, at, face):
        for c, part in enumerate(repeat_levels(face, levels, period)):
            ref[at, :, c * LANES : (c + 1) * LANES] = part

    def body(b, carry):
        first = lo + b * block
        for r in range(block + 1):
            wind = wind_row(src, first - 1 + r, lead, levels) + wind_row(src, first + r, lead, levels)
            store(face_lead, r, (0.5 * COURANT * lead_sign) * wind)
        for r in range(block):
            wind = wind_row(src, first + r, sub, levels)
            store(face_sub, r, (0.5 * COURANT * sub_sign) * (wind + pltpu.roll(wind, size - 1, 0)))
        for c3 in range(period):
            lanes3 = slice(c3 * LANES, (c3 + 1) * LANES)
            group = [slice(c * LANES, (c + 1) * LANES) for c in range(c3, chunks, period)]
            face = face_lead[0, :, lanes3]
            q = [src[first, :, lanes] for lanes in group]
            before = [face * jnp.where(face > 0.0, src[first - 1, :, lanes], here) for lanes, here in zip(group, q)]
            for r in range(block):
                face, side = face_lead[r + 1, :, lanes3], face_sub[r, :, lanes3]
                for i, lanes in enumerate(group):
                    ahead = src[first + r + 1, :, lanes]
                    flux = face * jnp.where(face > 0.0, q[i], ahead)
                    cross = side * jnp.where(side > 0.0, q[i], pltpu.roll(q[i], size - 1, 0))
                    dst[first + r, :, lanes] = q[i] - ((flux - before[i]) + (cross - pltpu.roll(cross, 1, 0)))
                    q[i], before[i] = ahead, flux
        return carry

    if hi - lo == block:
        body(0, 0)
    else:
        lax.fori_loop(0, (hi - lo) // block, body, 0)


def network_forward(x, mask, w_in, w_out, state, hsum, rows, kept):
    normed, scale, slope, hidden = state
    x, total = x(), None
    for use in range(3):
        inv = lax.rsqrt(jnp.mean(x * x, axis=1, keepdims=True) + EPS)
        unit = (x * inv).astype(BF16)
        normed[use, rows, :] = unit
        if use == 0:
            packed = mask()
            lane = lax.broadcasted_iota(jnp.int32, packed.shape, 1)
        else:
            packed = jnp.where(lane < 32 * use, packed, inv)
        yield
        p = jnp.dot(unit, w_in[...], preferred_element_type=F32)
        yield
        s = 0.5 + 0.5 * jnp.tanh(0.5 * p)
        silu = p * s
        slope[use, rows, :] = s + silu * (1.0 - s)
        h = silu.astype(BF16)
        hidden[use, rows, :] = h
        if use == 2:
            scale[rows, :] = packed
        kept(use)
        if use < 2:
            total = h.astype(F32) if use == 0 else total + h.astype(F32)
            yield
            x = x + TAU * jnp.dot(h, w_out[...], preferred_element_type=F32)
            yield
        else:
            hsum[rows, :] = total + h.astype(F32) * mask()[:, 0:1]


def run_together(steps, lag):
    steps = list(steps)
    live, tick = set(range(len(steps))), 0
    while live:
        for i in sorted(live):
            if tick >= lag * i and next(steps[i], 1) == 1:
                live.discard(i)
        tick += 1


def state_copies(source, target, sems, use, part, rows):
    copies = []
    for i, (a, b) in enumerate(zip(source, target)):
        if i == 1 and use < 2:
            continue
        at = (rows, slice(None)) if i == 1 else (use, rows, slice(None))
        copies.append(pltpu.make_async_copy(a.at[at], b.at[at], sems.at[part, use, i]))
    return copies


def pack_strip(n, levels, k, o, air, out):
    base, cm, cd = side_rows((k - o + 4) % 4, n)
    for d in range(2):
        copy_rows(out, d * n, air, base + cd * d + cm * (n - 1), -cm, n)
    turn_winds(out, (0, 2 * n), o, levels)


def pack_kernel(n, levels, turn, air, s1, s3):
    pack_strip(n, levels, 1, turn[0, 0], air, s1)
    pack_strip(n, levels, 3, turn[0, 0], air, s3)


def pack_with_corners_kernel(n, levels, turn, air, h1, h3, order, s0, s2):
    del order
    pack_strip(n, levels, 0, turn[0, 0], air, s0)
    pack_strip(n, levels, 2, turn[0, 0], air, s2)
    s0[2 * n : 2 * n + 1, :] = h1[n - 1 : n, :]
    s0[2 * n + 1 : 2 * n + 2, :] = h3[0:1, :]
    s2[2 * n : 2 * n + 1, :] = h1[0:1, :]
    s2[2 * n + 1 : 2 * n + 2, :] = h3[n - 1 : n, :]


def inner_transport_kernel(n, levels, turn, air_rows, moved, own, token, q_one, face_lead, face_sub):
    o = turn[0, 0]
    air = air_rows.reshape(n, n, air_rows.shape[1])
    winds = ((0, 1.0), (1, 1.0))
    transport(air, q_one, face_lead, face_sub, 1, n - 1, winds, levels)
    transport(q_one, moved, face_lead, face_sub, 2, n - 2, winds, levels)
    for k in range(4):
        base, cm, cd = side_rows((k - o + 4) % 4, n)
        for d in range(4):
            copy_rows(own, (k * 4 + d) * n, air_rows, base + cd * d, cm, n)
        turn_winds(own, (k * 4 * n, 4 * n), o, levels)
    token[...] = jnp.zeros_like(token)


def cost_mask(n, cost, mask):
    diagonal = lax.broadcasted_iota(jnp.int32, (n, n), 0) == lax.broadcasted_iota(jnp.int32, (n, n), 1)

    def mask_row(i, carry):
        two = jnp.broadcast_to((cost[pl.ds(i, 1), :] == 2).astype(F32), (n, n))
        column = jnp.sum(jnp.where(diagonal, two, 0.0), axis=1, keepdims=True)
        mask[pl.ds(pl.multiple_of(i * n, 8), n), :] = jnp.broadcast_to(column, (n, LANES))
        return carry

    lax.fori_loop(0, n, mask_row, 0, unroll=8)


PARTS = 2
LAG = 0
INNER_LAG = 3


def inner_parts(n):
    inner = n - 4
    size = inner // PARTS * n
    return [(part, part * size, size) for part in range(PARTS)]


def inner_network_kernel(n, dest, turn, moved, cost, w_in, w_out, n_o, s_o, g_o, h_o, outgoing, mask_rim,
                         normed, scale, slope, hidden, hsum, mask, sems):
    state, out = (normed, scale, slope, hidden), (n_o, s_o, g_o, h_o)
    feats = moved.shape[2]
    cost_mask(n, cost, mask)
    for k in range(4):
        base, cm, cd = side_rows((k - turn[0, 0] + 4) % 4, n)
        for d in range(2):
            copy_rows(mask_rim, (k * 2 + d) * n, mask, base + cd * d, cm, n)
    copies = []

    def part_steps(network, start, size):
        yield from network
        for i in range(start // n, (start + size) // n):
            if i % 2 == 0:
                yield
            for j in range(2, n - 2):
                outgoing[pl.ds(dest[2 + i, j], 1), :] = hsum[i * n + j : i * n + j + 1, :]

    steps = []
    for part, start, size in inner_parts(n):
        rows = slice(start, start + size)
        x = lambda start=start, size=size: moved[2 + start // n : 2 + (start + size) // n, :, :].reshape(size, feats)
        m = lambda start=start, size=size: mask[2 * n + start : 2 * n + start + size, :]

        def kept(use, part=part, rows=pl.ds(start, size)):
            for copy in state_copies(state, out, sems, use, part, rows):
                copy.start()
                copies.append(copy)

        steps.append(part_steps(network_forward(x, m, w_in, w_out, state, hsum, rows, kept), start, size))
    run_together(steps, INNER_LAG)
    for copy in copies:
        copy.wait()


def rim_kernel(n, levels, turn, dest, h0, h1, h2, h3, own, mask_rim, w_in, w_out, before,
               n_o, s_o, g_o, h_o, outgoing, sent,
               normed, scale, slope, hidden, sems,
               cells_wide, cells_slim, lead_wide, sub_wide, lead_slim, sub_slim, x_rim, hsum):
    del before
    state, out = (normed, scale, slope, hidden), (n_o, s_o, g_o, h_o)
    o = turn[0, 0]
    halo = (h0, h1, h2, h3)
    wide = [lead_wide, sub_wide] + [cells_wide.at[step] for step in range(3)]
    slim = [lead_slim, sub_slim] + [cells_slim.at[step] for step in range(3)]
    for k in range(4):
        lead, sub, src, one, two = slim if k % 2 else wide
        for depth in range(6):
            d = depth - 2
            row = halo[k][(1 - depth) * n : (2 - depth) * n, :] if d < 0 else own[(k * 4 + d) * n : (k * 4 + d + 1) * n, :]
            src[depth, 0:n, :] = row
            if k % 2 == 0:
                src[depth, n + 2 : n + 8, :] = row[0:6, :]
                src[depth, n + 8 : n + 14, :] = row[n - 6 : n, :]
                for e in range(2):
                    if d < 0:
                        at = 2 * n + k // 2
                        src[depth, n + 1 - e : n + 2 - e, :] = halo[k][at : at + 1, :]
                        at = 2 * n + 1 - k // 2
                        src[depth, n + 14 + e : n + 15 + e, :] = halo[k][at : at + 1, :]
                    else:
                        at = e * n + n - 1 - d
                        src[depth, n + 1 - e : n + 2 - e, :] = halo[(k + 1) % 4][at : at + 1, :]
                        at = e * n + d
                        src[depth, n + 14 + e : n + 15 + e, :] = halo[(k + 3) % 4][at : at + 1, :]
        transport(src, one, lead, sub, 1, 5, SIDE_WINDS[k], levels)
        transport(one, two, lead, sub, 2, 4, SIDE_WINDS[k], levels)
        for d in range(2):
            at = (k * 2 + d) * n
            x_rim[at : at + n, :] = two[2 + d, 0:n, :]
            if k % 2 == 0:
                x_rim[at : at + 2, :] = two[2 + d, n + 2 : n + 4, :]
                x_rim[at + n - 2 : at + n, :] = two[2 + d, n + 12 : n + 14, :]
    turn_winds(x_rim, (0, 8 * n), (4 - o) % 4, levels)
    copies = []

    def kept(use):
        for copy in state_copies(state, out, sems, use, 0, pl.ds(0, 8 * n)):
            copy.start()
            copies.append(copy)

    halves = ((slice(0, 4 * n), lambda use: None), (slice(4 * n, 8 * n), kept))
    run_together([
        network_forward(lambda r=r: x_rim[r, :], lambda r=r: mask_rim[r, :], w_in, w_out, state, hsum, r, done)
        for r, done in halves
    ], 0)
    for k in range(4):
        (bi, di, mi), (bj, dj, mj) = side_cells((k - o + 4) % 4, n)
        skip = 2 * (k % 2)
        for d in range(2):
            for m in range(skip, n - skip):
                at = (k * 2 + d) * n + m
                row = dest[bi + di * d + mi * m, bj + dj * d + mj * m]
                outgoing[pl.ds(row, 1), :] = hsum[at : at + 1, :]
    copies.append(pltpu.make_async_copy(outgoing, sent, sems.at[1, 0, 0]))
    copies[-1].start()
    for copy in copies:
        copy.wait()


def contract_rows(a, b):
    return lax.dot_general(a, b, (((0,), (0,)), ((), ())), preferred_element_type=F32)


def contract_last(a, b):
    return lax.dot_general(a, b, (((1,), (1,)), ((), ())), preferred_element_type=F32)


def network_backward(cot, valid, w_in, w_out, state, err_out, err_in, rows, at, arrived):
    normed, scale, slope = state
    arrived("cotangent")
    cot = cot() * valid
    grad = cot * scale[rows, 0:1]
    for use in (2, 1, 0):
        e = (TAU * grad).astype(BF16)
        err_out[use, at, :] = e
        yield
        back = contract_last(e, w_out[...])
        yield
        arrived(("slope", use))
        inner = (back * slope[use, rows, :]).astype(BF16)
        err_in[use, rows, :] = inner
        yield
        if use > 0:
            d = contract_last(inner, w_in[...])
            yield
            arrived(("normed", use))
            unit = normed[use, rows, :].astype(F32)
            d = scale[rows, 32 * use : 32 * use + 1] * (d - unit * jnp.mean(d * unit, axis=1, keepdims=True))
            grad = (cot if use == 2 else grad) + d


def exchange_order(groups, tiles, tile_first):
    bits = lambda axis, low, count: [(axis, low << b) for b in range(((count // low) - 1).bit_length())]
    plane = [bits("grp", 2, groups), [("tile", 1)]]
    first, second = plane[::-1] if tile_first else plane
    return [("grp", 1)] + first + second + bits("tile", 2, tiles)


def store_pieces(grid_shape, me, order, grad, keep, send):
    groups, tiles = grid_shape
    rows = grad.shape[0] // (groups * tiles)
    for g in range(groups):
        for t in range(tiles):
            p = g * tiles + t
            away = {"grp": me[0] ^ g, "tile": me[1] ^ t}
            at = 0
            for axis, bit in order[1:]:
                at = at * 2 + (away[axis] // bit) % 2

            def store(ref, p=p, at=at):
                chunks = grad.shape[1] // LANES
                for c in range(chunks):
                    part = grad[p * rows : (p + 1) * rows, c * LANES : (c + 1) * LANES]
                    ref[at, pl.ds(c, rows, stride=chunks), :] = part

            pl.when(away["grp"] % 2 == 0)(functools.partial(store, keep))
            pl.when(away["grp"] % 2 == 1)(functools.partial(store, send))


def backward_kernel(n, grid_shape, order, me, turn, cot_in, in_weights, out_weights, in_ni, in_si, in_gi, in_hi,
                    in_nr, in_sr, in_gr, in_hr, keep, send, err_out, h, n_i, s_i, g_i, n_r, s_r, g_r, sems,
                    w_in, w_out, ei_i, ei_r, cot, cot_rim, grad_in):
    o = turn[0, 0]
    parts = inner_parts(n)
    inner = (n - 4) * n
    edge = 2 * n
    pairs = ((in_ni, n_i), (in_nr, n_r)), ((in_gi, g_i), (in_gr, g_r))
    normed = lambda use: [(a.at[use], b.at[use]) for a, b in pairs[0]]
    slope = lambda use: [(a.at[use], b.at[use]) for a, b in pairs[1]]
    plan = [
        ("cotangent", [(out_weights, w_out), (cot_in, cot), (in_si, s_i), (in_sr, s_r)]),
        (("slope", 2), [(in_weights, w_in), *slope(2)]),
        (("normed", 2), normed(2)),
        (("slope", 1), slope(1)),
        (("normed", 1), normed(1)),
        (("slope", 0), slope(0)),
        ("rest", [*normed(0), (in_hi, h.at[:, pl.ds(0, inner), :]), (in_hr, h.at[:, pl.ds(inner, 8 * n), :])]),
    ]
    index = 0
    flight = []

    def start_next():
        nonlocal index
        if plan:
            name, refs = plan.pop(0)
            copies = []
            for source, target in refs:
                copies.append(pltpu.make_async_copy(source, target, sems.at[index]))
                copies[-1].start()
                index += 1
            flight.append((name, copies))

    def arrived(name):
        if flight and flight[0][0] == name:
            for copy in flight.pop(0)[1]:
                copy.wait()
            start_next()

    start_next()
    start_next()
    start_next()
    steps = []
    for part, start, size in parts:
        at = slice(edge + start, edge + start + size)
        j = lax.broadcasted_iota(jnp.int32, (size, 1), 0) % n
        valid = ((j >= 2) & (j < n - 2)).astype(F32)
        rows = slice(start, start + size)
        steps.append(network_backward(lambda at=at: cot[at, :], valid, w_in, w_out, (n_i, s_i, g_i), err_out, ei_i,
                                      rows, rows, arrived))

    def rim_cotangent():
        for k in range(4):
            base, cm, cd = side_rows((k - o + 4) % 4, n)
            for d in range(2):
                copy_rows(cot_rim, (k * 2 + d) * n, cot, base + cd * d, cm, n)
        return cot_rim[...]

    e = lax.broadcasted_iota(jnp.int32, (8 * n, 1), 0)
    m = e % n
    valid = (((e // (2 * n)) % 2 == 0) | ((m >= 2) & (m < n - 2))).astype(F32)
    steps.append(network_backward(rim_cotangent, valid, w_in, w_out, (n_r, s_r, g_r), err_out, ei_r,
                                  slice(0, 8 * n), slice(inner, inner + 8 * n), arrived))
    run_together(steps, LAG)
    arrived("rest")
    flat = lambda ref: ref[...].reshape(ref.shape[0] * ref.shape[1], ref.shape[2])
    grad_in[...] = contract_rows(flat(n_i), flat(ei_i)) + contract_rows(flat(n_r), flat(ei_r))
    store_pieces(grid_shape, me, order, grad_in, keep, send)


def output_gradient_kernel(grid_shape, order, me, err_out, h, keep, send, grad_out):
    flat = lambda ref: ref[...].reshape(ref.shape[0] * ref.shape[1], ref.shape[2])
    grad_out[...] = contract_rows(flat(h), flat(err_out))
    store_pieces(grid_shape, me, order, grad_out, keep, send)


def exchange_sums(keep, send, order, sizes):
    for axis, bit in order:
        keep = keep + lax.ppermute(send, axis, [(i, i ^ bit) for i in range(sizes[axis])])
        half = keep.shape[0] // 2
        keep, send = keep[:half], keep[half:]
    return keep, send


def output_kernel(rows, w_out, out):
    x = rows[...]
    high = x.astype(BF16)
    low = (x - high.astype(F32)).astype(BF16)
    w = w_out[...]
    out[...] = TAU * (jnp.dot(high, w, preferred_element_type=F32) + jnp.dot(low, w, preferred_element_type=F32))


def shift_perm(count, by):
    return [(i, (i + by) % count) for i in range(count)]


def joint_perm(groups, tiles, move):
    return [(g * tiles + t, (lambda h: h[0] * tiles + h[1])(move(g, t))) for g in range(groups) for t in range(tiles)]


def per_device(air_state, cotangent, cost_count, assignment, orientation, weight_in, weight_out):
    groups, tiles = lax.axis_size("grp"), lax.axis_size("tile")
    count = groups * tiles
    n, feats = air_state.shape[0], air_state.shape[2]
    units = weight_in.shape[1]
    levels = feats // V
    cells, rim, inner = n * n, 8 * n, (n - 4) * n
    period = next(c for c in range(1, feats // LANES + 1) if c * LANES % levels == 0)
    shape = jax.ShapeDtypeStruct

    air_rows = air_state.reshape(cells, feats)
    cot_rows = cotangent.reshape(cells, feats)
    both = ("grp", "tile")
    stay = lambda x: pltpu.with_memory_space_constraint(x, pltpu.HBM)

    def state(space, rows):
        return [
            space((3, rows, feats), BF16),
            space((rows, LANES), F32),
            space((3, rows, units), F32),
            space((3, rows, units), BF16),
        ]

    parts = len(inner_parts(n))
    strips = pl.pallas_call(
        functools.partial(pack_kernel, n, levels),
        out_shape=[shape((2 * n, feats), F32)] * 2,
        in_specs=[SMEM, VMEM],
        out_specs=[VMEM] * 2,
        compiler_params=params(8),
        name="pack_strips",
    )(orientation, air_rows)
    from_left = lax.ppermute(strips[1], "grp", shift_perm(groups, 1))
    from_right = lax.ppermute(strips[0], "grp", shift_perm(groups, -1))

    moved, own, token = pl.pallas_call(
        functools.partial(inner_transport_kernel, n, levels),
        out_shape=[
            pltpu.VMEM((n, n, feats), F32),
            pltpu.VMEM((16 * n, feats), F32),
            shape((8, LANES), F32),
        ],
        in_specs=[SMEM, VMEM],
        out_specs=[VMEM] * 3,
        scratch_shapes=[
            pltpu.VMEM((n, n, feats), F32),
            pltpu.VMEM((8, n, period * LANES), F32),
            pltpu.VMEM((7, n, period * LANES), F32),
        ],
        compiler_params=params(10),
        cost_estimate=pl.CostEstimate(flops=60 * cells * feats, bytes_accessed=16 << 20, transcendentals=0),
        name="inner_transport",
    )(orientation, air_rows)

    strips = pl.pallas_call(
        functools.partial(pack_with_corners_kernel, n, levels),
        out_shape=[shape((2 * n + 8, feats), F32)] * 2,
        in_specs=[SMEM] + [VMEM] * 4,
        out_specs=[VMEM] * 2,
        compiler_params=params(8),
        name="pack_strips_corners",
    )(orientation, air_rows, from_left, from_right, token)
    from_above = lax.ppermute(strips[1], "tile", shift_perm(tiles, 1))
    from_below = lax.ppermute(strips[0], "tile", shift_perm(tiles, -1))

    *saved_inner, outgoing, mask_rim = pl.pallas_call(
        functools.partial(inner_network_kernel, n),
        out_shape=[*state(pltpu.HBM, inner), pltpu.VMEM((cells, units), F32), pltpu.VMEM((rim, LANES), F32)],
        in_specs=[SMEM] * 2 + [VMEM] * 4,
        out_specs=[HBM] * 4 + [VMEM] * 2,
        scratch_shapes=[
            *state(pltpu.VMEM, inner),
            pltpu.VMEM((inner, units), F32),
            pltpu.VMEM((cells, LANES), F32),
            pltpu.SemaphoreType.DMA((parts, 3, 4)),
        ],
        compiler_params=params(24),
        cost_estimate=pl.CostEstimate(
            flops=10 * inner * feats * units, bytes_accessed=16 << 20, transcendentals=3 * inner * units
        ),
        name="inner_network",
    )(assignment, orientation, moved, cost_count, weight_in, weight_out)

    wide, slim = n + 16, n
    *saved_rim, _, outgoing = pl.pallas_call(
        functools.partial(rim_kernel, n, levels),
        out_shape=[*state(pltpu.HBM, rim), pltpu.VMEM((cells, units), F32), pltpu.HBM((cells, units), F32)],
        in_specs=[SMEM, SMEM] + [VMEM] * 9,
        out_specs=[HBM] * 4 + [VMEM, HBM],
        input_output_aliases={10: 4},
        scratch_shapes=[*state(pltpu.VMEM, rim), pltpu.SemaphoreType.DMA((2, 3, 4))]
        + [pltpu.VMEM((3, 6, wide, feats), F32), pltpu.VMEM((3, 6, slim, feats), F32)]
        + [pltpu.VMEM((rows, wide, period * LANES), F32) for rows in (5, 4)]
        + [pltpu.VMEM((rows, slim, period * LANES), F32) for rows in (5, 4)]
        + [pltpu.VMEM((rim, feats), F32), pltpu.VMEM((rim, units), F32)],
        compiler_params=params(16),
        cost_estimate=pl.CostEstimate(
            flops=10 * rim * feats * units, bytes_accessed=20 << 20, transcendentals=3 * rim * units
        ),
        name="rim_columns",
    )(orientation, assignment, from_above, from_left, from_below, from_right, own, mask_rim, weight_in, weight_out, outgoing)

    arrived = lax.all_to_all(
        outgoing.reshape(count, cells // count, units), both, split_axis=0, concat_axis=0, tiled=True
    ).reshape(cells, units)

    me = jnp.stack([lax.axis_index("grp"), lax.axis_index("tile")]).astype(jnp.int32)
    saved = lambda rows: state(pltpu.VMEM, rows)[:3]
    halves = [shape((count // 2, feats * units // count // LANES, LANES), F32)] * 2
    orders = [exchange_order(groups, tiles, tile_first) for tile_first in (False, True)]
    *pieces_in, err_out, hidden = pl.pallas_call(
        functools.partial(backward_kernel, n, (groups, tiles), orders[0]),
        out_shape=[
            *halves,
            pltpu.VMEM((3, inner + rim, feats), BF16),
            pltpu.VMEM((3, inner + rim, units), BF16),
        ],
        in_specs=[SMEM, SMEM] + [HBM] * 11,
        out_specs=[VMEM] * 4,
        scratch_shapes=[
            *saved(inner),
            *saved(rim),
            pltpu.SemaphoreType.DMA((19,)),
            pltpu.VMEM((feats, units), BF16),
            pltpu.VMEM((units, feats), BF16),
            pltpu.VMEM((3, inner, units), BF16),
            pltpu.VMEM((3, rim, units), BF16),
            pltpu.VMEM((cells, feats), F32),
            pltpu.VMEM((rim, feats), F32),
            pltpu.VMEM((feats, units), F32),
        ],
        compiler_params=params(36),
        cost_estimate=pl.CostEstimate(flops=16 * cells * feats * units, bytes_accessed=20 << 20, transcendentals=0),
        name="columns_backward",
    )(me, orientation, *map(stay, (cot_rows, weight_in, weight_out, *saved_inner, *saved_rim)))
    pieces_out = pl.pallas_call(
        functools.partial(output_gradient_kernel, (groups, tiles), orders[1]),
        out_shape=halves,
        in_specs=[SMEM, VMEM, VMEM],
        out_specs=[VMEM] * 2,
        scratch_shapes=[pltpu.VMEM((units, feats), F32)],
        compiler_params=params(24),
        cost_estimate=pl.CostEstimate(flops=6 * cells * feats * units, bytes_accessed=8 << 20, transcendentals=0),
        name="output_gradient",
    )(me, err_out, hidden)

    sizes = {"grp": groups, "tile": tiles}
    far = [pair for pair in orders[0] if pair[0] == "tile" and pair[1] > 1]
    near = len(orders[0]) - len(far)
    sums = [exchange_sums(*pieces, order[:near], sizes) for pieces, order in zip((pieces_in, pieces_out), orders)]
    split = sums[0][0].shape[1]
    keep, send = (jnp.concatenate(pair, axis=1) for pair in zip(*sums))
    keep, send = exchange_sums(keep, send, far[:-1], sizes)

    block = cells // 4
    tendency = pl.pallas_call(
        output_kernel,
        out_shape=shape((cells, feats), F32),
        grid=(cells // block,),
        in_specs=[pl.BlockSpec((block, units), lambda i: (i, 0)), pl.BlockSpec((units, feats), lambda i: (0, 0))],
        out_specs=pl.BlockSpec((block, feats), lambda i: (i, 0)),
        compiler_params=params(32),
        cost_estimate=pl.CostEstimate(flops=4 * cells * feats * units, bytes_accessed=6 << 20, transcendentals=0),
        name="tendency_rows",
    )(arrived, weight_out)
    (axis, bit), = far[-1:]
    arriving = lax.ppermute(send, axis, [(i, i ^ bit) for i in range(sizes[axis])])
    keep, tendency = lax.optimization_barrier((keep, tendency))
    keep = keep + arriving
    summed_in, summed_out = keep[0, :split].reshape(-1), keep[0, split:].reshape(-1)
    return (tendency, summed_in, summed_out)


def solution(mesh):
    in_specs = (
        P("tile", "grp", None),
        P("tile", "grp", None),
        P("tile", "grp"),
        P("tile", "grp"),
        P("tile", "grp"),
        P(),
        P(),
    )
    out_specs = (P(("grp", "tile"), None), P(("grp", "tile")), P(("grp", "tile")))
    return jax.shard_map(
        per_device, mesh=mesh, in_specs=in_specs, out_specs=out_specs, check_vma=False
    )
```

```python
import functools
import jax
import jax.numpy as jnp
from jax import lax
from jax.experimental import pallas as pl
from jax.experimental.pallas import tpu as pltpu
from jax.sharding import PartitionSpec as P

V = 8
TAU = 0.5
COURANT = 0.1
EPS = 1e-06
LANES = 128
F32 = jnp.float32
BF16 = jnp.bfloat16
SIDE_WINDS = (((0, 1.0), (1, 1.0)), ((1, 1.0), (0, -1.0)), ((0, -1.0), (1, -1.0)), ((1, -1.0), (0, 1.0)))

VMEM = pl.BlockSpec(memory_space=pltpu.VMEM)
HBM = pl.BlockSpec(memory_space=pltpu.HBM)
SMEM = pl.BlockSpec(memory_space=pltpu.SMEM)


def params(mib):
    return pltpu.CompilerParams(vmem_limit_bytes=mib * 1024 * 1024)


def side_cells(k, n):
    pick = lambda a, b, c, e: jnp.where(k == 0, a, jnp.where(k == 1, b, jnp.where(k == 2, c, e)))
    return (pick(0, n - 1, n - 1, 0), pick(1, 0, -1, 0), pick(0, -1, 0, 1)), (
        pick(0, 0, n - 1, n - 1), pick(0, 1, 0, -1), pick(1, 0, -1, 0))


def side_rows(k, n):
    (bi, di, mi), (bj, dj, mj) = side_cells(k, n)
    return bi * n + bj, mi * n + mj, di * n + dj


def turn_winds(ref, rows, quarter, levels):
    start, size = rows
    width = -(-2 * levels // LANES) * LANES
    w = ref[start : start + size, 0:width]
    lane = lax.broadcasted_iota(jnp.int32, w.shape, 1)
    swapped = jnp.where(lane < levels, pltpu.roll(w, width - levels, 1), pltpu.roll(w, levels, 1))
    cos = ((quarter == 0).astype(F32) - (quarter == 2).astype(F32))
    sin = ((quarter == 1).astype(F32) - (quarter == 3).astype(F32))
    turned = w * cos + swapped * jnp.where(lane < levels, -sin, sin)
    ref[start : start + size, 0:width] = jnp.where(lane < 2 * levels, turned, w)


def copy_rows(dst, dst_base, src, cell, step, count):
    def body(s, carry):
        dst[pl.ds(dst_base + s, 1), :] = src[pl.ds(cell + s * step, 1), :]
        return carry

    lax.fori_loop(0, count, body, 0, unroll=count)


def wind_row(src, a, which, levels):
    start = which * levels
    chunk, off = start // LANES, start % LANES
    first = src[a, :, chunk * LANES : (chunk + 1) * LANES]
    if off == 0:
        return first
    second = src[a, :, (chunk + 1) * LANES : (chunk + 2) * LANES]
    lane = lax.broadcasted_iota(jnp.int32, first.shape, 1)
    shift = LANES - off
    return jnp.where(lane < shift, pltpu.roll(first, shift, 1), pltpu.roll(second, shift, 1))


def repeat_levels(face, levels, chunks):
    lane = lax.broadcasted_iota(jnp.int32, face.shape, 1)
    rolls = {0: face}
    out = []
    for c in range(chunks):
        result, at = None, 0
        while at < LANES:
            index = (c * LANES + at) % levels
            shift = (at - index) % LANES
            if shift not in rolls:
                rolls[shift] = pltpu.roll(face, shift, 1)
            result = rolls[shift] if result is None else jnp.where(lane < at, result, rolls[shift])
            at += levels - index
        out.append(result)
    return out


def transport(src, dst, face_lead, face_sub, lo, hi, winds, levels):
    (lead, lead_sign), (sub, sub_sign) = winds
    size, feats = src.shape[1], src.shape[2]
    chunks = feats // LANES
    period = face_lead.shape[2] // LANES
    block = next(b for b in range(face_sub.shape[0], 0, -1) if (hi - lo) % b == 0)

    def store(ref, at, face):
        for c, part in enumerate(repeat_levels(face, levels, period)):
            ref[at, :, c * LANES : (c + 1) * LANES] = part

    def body(b, carry):
        first = lo + b * block
        for r in range(block + 1):
            wind = wind_row(src, first - 1 + r, lead, levels) + wind_row(src, first + r, lead, levels)
            store(face_lead, r, (0.5 * COURANT * lead_sign) * wind)
        for r in range(block):
            wind = wind_row(src, first + r, sub, levels)
            store(face_sub, r, (0.5 * COURANT * sub_sign) * (wind + pltpu.roll(wind, size - 1, 0)))
        for c3 in range(period):
            lanes3 = slice(c3 * LANES, (c3 + 1) * LANES)
            group = [slice(c * LANES, (c + 1) * LANES) for c in range(c3, chunks, period)]
            face = face_lead[0, :, lanes3]
            q = [src[first, :, lanes] for lanes in group]
            before = [face * jnp.where(face > 0.0, src[first - 1, :, lanes], here) for lanes, here in zip(group, q)]
            for r in range(block):
                face, side = face_lead[r + 1, :, lanes3], face_sub[r, :, lanes3]
                for i, lanes in enumerate(group):
                    ahead = src[first + r + 1, :, lanes]
                    flux = face * jnp.where(face > 0.0, q[i], ahead)
                    cross = side * jnp.where(side > 0.0, q[i], pltpu.roll(q[i], size - 1, 0))
                    dst[first + r, :, lanes] = q[i] - ((flux - before[i]) + (cross - pltpu.roll(cross, 1, 0)))
                    q[i], before[i] = ahead, flux
        return carry

    if hi - lo == block:
        body(0, 0)
    else:
        lax.fori_loop(0, (hi - lo) // block, body, 0)


def network_forward(x, mask, w_in, w_out, state, hsum, rows, kept):
    normed, scale, slope, hidden = state
    x, total = x(), None
    for use in range(3):
        inv = lax.rsqrt(jnp.mean(x * x, axis=1, keepdims=True) + EPS)
        unit = (x * inv).astype(BF16)
        normed[use, rows, :] = unit
        if use == 0:
            packed = mask()
            lane = lax.broadcasted_iota(jnp.int32, packed.shape, 1)
        else:
            packed = jnp.where(lane < 32 * use, packed, inv)
        yield
        p = jnp.dot(unit, w_in[...], preferred_element_type=F32)
        yield
        s = 0.5 + 0.5 * jnp.tanh(0.5 * p)
        silu = p * s
        slope[use, rows, :] = s + silu * (1.0 - s)
        h = silu.astype(BF16)
        hidden[use, rows, :] = h
        if use == 2:
            scale[rows, :] = packed
        kept(use)
        if use < 2:
            total = h.astype(F32) if use == 0 else total + h.astype(F32)
            yield
            x = x + TAU * jnp.dot(h, w_out[...], preferred_element_type=F32)
            yield
        else:
            hsum[rows, :] = total + h.astype(F32) * mask()[:, 0:1]


def run_together(steps, lag):
    steps = list(steps)
    live, tick = set(range(len(steps))), 0
    while live:
        for i in sorted(live):
            if tick >= lag * i and next(steps[i], 1) == 1:
                live.discard(i)
        tick += 1


def state_copies(source, target, sems, use, part, rows):
    copies = []
    for i, (a, b) in enumerate(zip(source, target)):
        if i == 1 and use < 2:
            continue
        at = (rows, slice(None)) if i == 1 else (use, rows, slice(None))
        copies.append(pltpu.make_async_copy(a.at[at], b.at[at], sems.at[part, use, i]))
    return copies


def pack_strip(n, levels, k, o, air, out):
    base, cm, cd = side_rows((k - o + 4) % 4, n)
    for d in range(2):
        copy_rows(out, d * n, air, base + cd * d + cm * (n - 1), -cm, n)
    turn_winds(out, (0, 2 * n), o, levels)


def pack_kernel(n, levels, turn, air, s1, s3):
    pack_strip(n, levels, 1, turn[0, 0], air, s1)
    pack_strip(n, levels, 3, turn[0, 0], air, s3)


def pack_with_corners_kernel(n, levels, turn, air, h1, h3, order, s0, s2):
    del order
    pack_strip(n, levels, 0, turn[0, 0], air, s0)
    pack_strip(n, levels, 2, turn[0, 0], air, s2)
    s0[2 * n : 2 * n + 1, :] = h1[n - 1 : n, :]
    s0[2 * n + 1 : 2 * n + 2, :] = h3[0:1, :]
    s2[2 * n : 2 * n + 1, :] = h1[0:1, :]
    s2[2 * n + 1 : 2 * n + 2, :] = h3[n - 1 : n, :]


def inner_transport_kernel(n, levels, turn, air_rows, moved, own, token, q_one, face_lead, face_sub):
    o = turn[0, 0]
    air = air_rows.reshape(n, n, air_rows.shape[1])
    winds = ((0, 1.0), (1, 1.0))
    transport(air, q_one, face_lead, face_sub, 1, n - 1, winds, levels)
    transport(q_one, moved, face_lead, face_sub, 2, n - 2, winds, levels)
    for k in range(4):
        base, cm, cd = side_rows((k - o + 4) % 4, n)
        for d in range(4):
            copy_rows(own, (k * 4 + d) * n, air_rows, base + cd * d, cm, n)
        turn_winds(own, (k * 4 * n, 4 * n), o, levels)
    token[...] = jnp.zeros_like(token)


def cost_mask(n, cost, mask):
    diagonal = lax.broadcasted_iota(jnp.int32, (n, n), 0) == lax.broadcasted_iota(jnp.int32, (n, n), 1)

    def mask_row(i, carry):
        two = jnp.broadcast_to((cost[pl.ds(i, 1), :] == 2).astype(F32), (n, n))
        column = jnp.sum(jnp.where(diagonal, two, 0.0), axis=1, keepdims=True)
        mask[pl.ds(pl.multiple_of(i * n, 8), n), :] = jnp.broadcast_to(column, (n, LANES))
        return carry

    lax.fori_loop(0, n, mask_row, 0, unroll=8)


PARTS = 2
LAG = 0
INNER_LAG = 3


def inner_parts(n):
    inner = n - 4
    size = inner // PARTS * n
    return [(part, part * size, size) for part in range(PARTS)]


def inner_network_kernel(n, dest, turn, moved, cost, w_in, w_out, n_o, s_o, g_o, h_o, outgoing, mask_rim,
                         normed, scale, slope, hidden, hsum, mask, sems):
    state, out = (normed, scale, slope, hidden), (n_o, s_o, g_o, h_o)
    feats = moved.shape[2]
    cost_mask(n, cost, mask)
    for k in range(4):
        base, cm, cd = side_rows((k - turn[0, 0] + 4) % 4, n)
        for d in range(2):
            copy_rows(mask_rim, (k * 2 + d) * n, mask, base + cd * d, cm, n)
    copies = []

    def part_steps(network, start, size):
        yield from network
        for i in range(start // n, (start + size) // n):
            if i % 2 == 0:
                yield
            for j in range(2, n - 2):
                outgoing[pl.ds(dest[2 + i, j], 1), :] = hsum[i * n + j : i * n + j + 1, :]

    steps = []
    for part, start, size in inner_parts(n):
        rows = slice(start, start + size)
        x = lambda start=start, size=size: moved[2 + start // n : 2 + (start + size) // n, :, :].reshape(size, feats)
        m = lambda start=start, size=size: mask[2 * n + start : 2 * n + start + size, :]

        def kept(use, part=part, rows=pl.ds(start, size)):
            for copy in state_copies(state, out, sems, use, part, rows):
                copy.start()
                copies.append(copy)

        steps.append(part_steps(network_forward(x, m, w_in, w_out, state, hsum, rows, kept), start, size))
    run_together(steps, INNER_LAG)
    for copy in copies:
        copy.wait()


def rim_kernel(n, levels, turn, dest, h0, h1, h2, h3, own, mask_rim, w_in, w_out, before,
               n_o, s_o, g_o, h_o, outgoing, sent,
               normed, scale, slope, hidden, sems,
               cells_wide, cells_slim, lead_wide, sub_wide, lead_slim, sub_slim, x_rim, hsum):
    del before
    state, out = (normed, scale, slope, hidden), (n_o, s_o, g_o, h_o)
    o = turn[0, 0]
    halo = (h0, h1, h2, h3)
    wide = [lead_wide, sub_wide] + [cells_wide.at[step] for step in range(3)]
    slim = [lead_slim, sub_slim] + [cells_slim.at[step] for step in range(3)]
    for k in range(4):
        lead, sub, src, one, two = slim if k % 2 else wide
        for depth in range(6):
            d = depth - 2
            row = halo[k][(1 - depth) * n : (2 - depth) * n, :] if d < 0 else own[(k * 4 + d) * n : (k * 4 + d + 1) * n, :]
            src[depth, 0:n, :] = row
            if k % 2 == 0:
                src[depth, n + 2 : n + 8, :] = row[0:6, :]
                src[depth, n + 8 : n + 14, :] = row[n - 6 : n, :]
                for e in range(2):
                    if d < 0:
                        at = 2 * n + k // 2
                        src[depth, n + 1 - e : n + 2 - e, :] = halo[k][at : at + 1, :]
                        at = 2 * n + 1 - k // 2
                        src[depth, n + 14 + e : n + 15 + e, :] = halo[k][at : at + 1, :]
                    else:
                        at = e * n + n - 1 - d
                        src[depth, n + 1 - e : n + 2 - e, :] = halo[(k + 1) % 4][at : at + 1, :]
                        at = e * n + d
                        src[depth, n + 14 + e : n + 15 + e, :] = halo[(k + 3) % 4][at : at + 1, :]
        transport(src, one, lead, sub, 1, 5, SIDE_WINDS[k], levels)
        transport(one, two, lead, sub, 2, 4, SIDE_WINDS[k], levels)
        for d in range(2):
            at = (k * 2 + d) * n
            x_rim[at : at + n, :] = two[2 + d, 0:n, :]
            if k % 2 == 0:
                x_rim[at : at + 2, :] = two[2 + d, n + 2 : n + 4, :]
                x_rim[at + n - 2 : at + n, :] = two[2 + d, n + 12 : n + 14, :]
    turn_winds(x_rim, (0, 8 * n), (4 - o) % 4, levels)
    copies = []

    def kept(use):
        for copy in state_copies(state, out, sems, use, 0, pl.ds(0, 8 * n)):
            copy.start()
            copies.append(copy)

    halves = ((slice(0, 4 * n), lambda use: None), (slice(4 * n, 8 * n), kept))
    run_together([
        network_forward(lambda r=r: x_rim[r, :], lambda r=r: mask_rim[r, :], w_in, w_out, state, hsum, r, done)
        for r, done in halves
    ], 0)
    for k in range(4):
        (bi, di, mi), (bj, dj, mj) = side_cells((k - o + 4) % 4, n)
        skip = 2 * (k % 2)
        for d in range(2):
            for m in range(skip, n - skip):
                at = (k * 2 + d) * n + m
                row = dest[bi + di * d + mi * m, bj + dj * d + mj * m]
                outgoing[pl.ds(row, 1), :] = hsum[at : at + 1, :]
    copies.append(pltpu.make_async_copy(outgoing, sent, sems.at[1, 0, 0]))
    copies[-1].start()
    for copy in copies:
        copy.wait()


def contract_rows(a, b):
    return lax.dot_general(a, b, (((0,), (0,)), ((), ())), preferred_element_type=F32)


def contract_last(a, b):
    return lax.dot_general(a, b, (((1,), (1,)), ((), ())), preferred_element_type=F32)


def network_backward(cot, valid, w_in, w_out, state, err_out, err_in, rows, at, arrived):
    normed, scale, slope = state
    arrived("cotangent")
    cot = cot() * valid
    grad = cot * scale[rows, 0:1]
    for use in (2, 1, 0):
        e = (TAU * grad).astype(BF16)
        err_out[use, at, :] = e
        yield
        back = contract_last(e, w_out[...])
        yield
        arrived(("slope", use))
        inner = (back * slope[use, rows, :]).astype(BF16)
        err_in[use, rows, :] = inner
        yield
        if use > 0:
            d = contract_last(inner, w_in[...])
            yield
            arrived(("normed", use))
            unit = normed[use, rows, :].astype(F32)
            d = scale[rows, 32 * use : 32 * use + 1] * (d - unit * jnp.mean(d * unit, axis=1, keepdims=True))
            grad = (cot if use == 2 else grad) + d


def exchange_order(groups, tiles, tile_first):
    bits = lambda axis, low, count: [(axis, low << b) for b in range(((count // low) - 1).bit_length())]
    plane = [bits("grp", 2, groups), [("tile", 1)]]
    first, second = plane[::-1] if tile_first else plane
    return [("grp", 1)] + first + second + bits("tile", 2, tiles)


def store_pieces(grid_shape, me, order, grad, keep, send):
    groups, tiles = grid_shape
    rows = grad.shape[0] // (groups * tiles)
    for g in range(groups):
        for t in range(tiles):
            p = g * tiles + t
            away = {"grp": me[0] ^ g, "tile": me[1] ^ t}
            at = 0
            for axis, bit in order[1:]:
                at = at * 2 + (away[axis] // bit) % 2

            def store(ref, p=p, at=at):
                chunks = grad.shape[1] // LANES
                for c in range(chunks):
                    part = grad[p * rows : (p + 1) * rows, c * LANES : (c + 1) * LANES]
                    ref[at, pl.ds(c, rows, stride=chunks), :] = part

            pl.when(away["grp"] % 2 == 0)(functools.partial(store, keep))
            pl.when(away["grp"] % 2 == 1)(functools.partial(store, send))


def backward_kernel(n, grid_shape, order, me, turn, cot_in, in_weights, out_weights, in_ni, in_si, in_gi, in_hi,
                    in_nr, in_sr, in_gr, in_hr, keep, send, err_out, h, n_i, s_i, g_i, n_r, s_r, g_r, sems,
                    w_in, w_out, ei_i, ei_r, cot, cot_rim, grad_in):
    o = turn[0, 0]
    parts = inner_parts(n)
    inner = (n - 4) * n
    edge = 2 * n
    pairs = ((in_ni, n_i), (in_nr, n_r)), ((in_gi, g_i), (in_gr, g_r))
    normed = lambda use: [(a.at[use], b.at[use]) for a, b in pairs[0]]
    slope = lambda use: [(a.at[use], b.at[use]) for a, b in pairs[1]]
    plan = [
        ("cotangent", [(out_weights, w_out), (cot_in, cot), (in_si, s_i), (in_sr, s_r)]),
        (("slope", 2), [(in_weights, w_in), *slope(2)]),
        (("normed", 2), normed(2)),
        (("slope", 1), slope(1)),
        (("normed", 1), normed(1)),
        (("slope", 0), slope(0)),
        ("rest", [*normed(0), (in_hi, h.at[:, pl.ds(0, inner), :]), (in_hr, h.at[:, pl.ds(inner, 8 * n), :])]),
    ]
    index = 0
    flight = []

    def start_next():
        nonlocal index
        if plan:
            name, refs = plan.pop(0)
            copies = []
            for source, target in refs:
                copies.append(pltpu.make_async_copy(source, target, sems.at[index]))
                copies[-1].start()
                index += 1
            flight.append((name, copies))

    def arrived(name):
        if flight and flight[0][0] == name:
            for copy in flight.pop(0)[1]:
                copy.wait()
            start_next()

    start_next()
    start_next()
    start_next()
    steps = []
    for part, start, size in parts:
        at = slice(edge + start, edge + start + size)
        j = lax.broadcasted_iota(jnp.int32, (size, 1), 0) % n
        valid = ((j >= 2) & (j < n - 2)).astype(F32)
        rows = slice(start, start + size)
        steps.append(network_backward(lambda at=at: cot[at, :], valid, w_in, w_out, (n_i, s_i, g_i), err_out, ei_i,
                                      rows, rows, arrived))

    def rim_cotangent():
        for k in range(4):
            base, cm, cd = side_rows((k - o + 4) % 4, n)
            for d in range(2):
                copy_rows(cot_rim, (k * 2 + d) * n, cot, base + cd * d, cm, n)
        return cot_rim[...]

    e = lax.broadcasted_iota(jnp.int32, (8 * n, 1), 0)
    m = e % n
    valid = (((e // (2 * n)) % 2 == 0) | ((m >= 2) & (m < n - 2))).astype(F32)
    steps.append(network_backward(rim_cotangent, valid, w_in, w_out, (n_r, s_r, g_r), err_out, ei_r,
                                  slice(0, 8 * n), slice(inner, inner + 8 * n), arrived))
    run_together(steps, LAG)
    arrived("rest")
    flat = lambda ref: ref[...].reshape(ref.shape[0] * ref.shape[1], ref.shape[2])
    grad_in[...] = contract_rows(flat(n_i), flat(ei_i)) + contract_rows(flat(n_r), flat(ei_r))
    store_pieces(grid_shape, me, order, grad_in, keep, send)


def output_gradient_kernel(grid_shape, order, me, err_out, h, keep, send, grad_out):
    flat = lambda ref: ref[...].reshape(ref.shape[0] * ref.shape[1], ref.shape[2])
    grad_out[...] = contract_rows(flat(h), flat(err_out))
    store_pieces(grid_shape, me, order, grad_out, keep, send)


def exchange_sums(keep, send, order, sizes):
    for axis, bit in order:
        keep = keep + lax.ppermute(send, axis, [(i, i ^ bit) for i in range(sizes[axis])])
        half = keep.shape[0] // 2
        keep, send = keep[:half], keep[half:]
    return keep, send


def output_kernel(rows, w_out, out):
    x = rows[...]
    high = x.astype(BF16)
    low = (x - high.astype(F32)).astype(BF16)
    w = w_out[...]
    out[...] = TAU * (jnp.dot(high, w, preferred_element_type=F32) + jnp.dot(low, w, preferred_element_type=F32))


def shift_perm(count, by):
    return [(i, (i + by) % count) for i in range(count)]


def joint_perm(groups, tiles, move):
    return [(g * tiles + t, (lambda h: h[0] * tiles + h[1])(move(g, t))) for g in range(groups) for t in range(tiles)]


def per_device(air_state, cotangent, cost_count, assignment, orientation, weight_in, weight_out):
    groups, tiles = lax.axis_size("grp"), lax.axis_size("tile")
    count = groups * tiles
    n, feats = air_state.shape[0], air_state.shape[2]
    units = weight_in.shape[1]
    levels = feats // V
    cells, rim, inner = n * n, 8 * n, (n - 4) * n
    period = next(c for c in range(1, feats // LANES + 1) if c * LANES % levels == 0)
    shape = jax.ShapeDtypeStruct

    air_rows = air_state.reshape(cells, feats)
    cot_rows = cotangent.reshape(cells, feats)
    both = ("grp", "tile")
    stay = lambda x: pltpu.with_memory_space_constraint(x, pltpu.HBM)

    def state(space, rows):
        return [
            space((3, rows, feats), BF16),
            space((rows, LANES), F32),
            space((3, rows, units), F32),
            space((3, rows, units), BF16),
        ]

    parts = len(inner_parts(n))
    strips = pl.pallas_call(
        functools.partial(pack_kernel, n, levels),
        out_shape=[shape((2 * n, feats), F32)] * 2,
        in_specs=[SMEM, VMEM],
        out_specs=[VMEM] * 2,
        compiler_params=params(8),
        name="pack_strips",
    )(orientation, air_rows)
    from_left = lax.ppermute(strips[1], "grp", shift_perm(groups, 1))
    from_right = lax.ppermute(strips[0], "grp", shift_perm(groups, -1))

    moved, own, token = pl.pallas_call(
        functools.partial(inner_transport_kernel, n, levels),
        out_shape=[
            pltpu.VMEM((n, n, feats), F32),
            pltpu.VMEM((16 * n, feats), F32),
            shape((8, LANES), F32),
        ],
        in_specs=[SMEM, VMEM],
        out_specs=[VMEM] * 3,
        scratch_shapes=[
            pltpu.VMEM((n, n, feats), F32),
            pltpu.VMEM((8, n, period * LANES), F32),
            pltpu.VMEM((7, n, period * LANES), F32),
        ],
        compiler_params=params(10),
        cost_estimate=pl.CostEstimate(flops=60 * cells * feats, bytes_accessed=16 << 20, transcendentals=0),
        name="inner_transport",
    )(orientation, air_rows)

    strips = pl.pallas_call(
        functools.partial(pack_with_corners_kernel, n, levels),
        out_shape=[shape((2 * n + 8, feats), F32)] * 2,
        in_specs=[SMEM] + [VMEM] * 4,
        out_specs=[VMEM] * 2,
        compiler_params=params(8),
        name="pack_strips_corners",
    )(orientation, air_rows, from_left, from_right, token)
    from_above = lax.ppermute(strips[1], "tile", shift_perm(tiles, 1))
    from_below = lax.ppermute(strips[0], "tile", shift_perm(tiles, -1))

    *saved_inner, outgoing, mask_rim = pl.pallas_call(
        functools.partial(inner_network_kernel, n),
        out_shape=[*state(pltpu.HBM, inner), pltpu.VMEM((cells, units), F32), pltpu.VMEM((rim, LANES), F32)],
        in_specs=[SMEM] * 2 + [VMEM] * 4,
        out_specs=[HBM] * 4 + [VMEM] * 2,
        scratch_shapes=[
            *state(pltpu.VMEM, inner),
            pltpu.VMEM((inner, units), F32),
            pltpu.VMEM((cells, LANES), F32),
            pltpu.SemaphoreType.DMA((parts, 3, 4)),
        ],
        compiler_params=params(24),
        cost_estimate=pl.CostEstimate(
            flops=10 * inner * feats * units, bytes_accessed=16 << 20, transcendentals=3 * inner * units
        ),
        name="inner_network",
    )(assignment, orientation, moved, cost_count, weight_in, weight_out)

    wide, slim = n + 16, n
    *saved_rim, _, outgoing = pl.pallas_call(
        functools.partial(rim_kernel, n, levels),
        out_shape=[*state(pltpu.HBM, rim), pltpu.VMEM((cells, units), F32), pltpu.HBM((cells, units), F32)],
        in_specs=[SMEM, SMEM] + [VMEM] * 9,
        out_specs=[HBM] * 4 + [VMEM, HBM],
        input_output_aliases={10: 4},
        scratch_shapes=[*state(pltpu.VMEM, rim), pltpu.SemaphoreType.DMA((2, 3, 4))]
        + [pltpu.VMEM((3, 6, wide, feats), F32), pltpu.VMEM((3, 6, slim, feats), F32)]
        + [pltpu.VMEM((rows, wide, period * LANES), F32) for rows in (5, 4)]
        + [pltpu.VMEM((rows, slim, period * LANES), F32) for rows in (5, 4)]
        + [pltpu.VMEM((rim, feats), F32), pltpu.VMEM((rim, units), F32)],
        compiler_params=params(16),
        cost_estimate=pl.CostEstimate(
            flops=10 * rim * feats * units, bytes_accessed=20 << 20, transcendentals=3 * rim * units
        ),
        name="rim_columns",
    )(orientation, assignment, from_above, from_left, from_below, from_right, own, mask_rim, weight_in, weight_out, outgoing)

    arrived = lax.all_to_all(
        outgoing.reshape(count, cells // count, units), both, split_axis=0, concat_axis=0, tiled=True
    ).reshape(cells, units)

    me = jnp.stack([lax.axis_index("grp"), lax.axis_index("tile")]).astype(jnp.int32)
    saved = lambda rows: state(pltpu.VMEM, rows)[:3]
    halves = [shape((count // 2, feats * units // count // LANES, LANES), F32)] * 2
    orders = [exchange_order(groups, tiles, tile_first) for tile_first in (False, True)]
    *pieces_in, err_out, hidden = pl.pallas_call(
        functools.partial(backward_kernel, n, (groups, tiles), orders[0]),
        out_shape=[
            *halves,
            pltpu.VMEM((3, inner + rim, feats), BF16),
            pltpu.VMEM((3, inner + rim, units), BF16),
        ],
        in_specs=[SMEM, SMEM] + [HBM] * 11,
        out_specs=[VMEM] * 4,
        scratch_shapes=[
            *saved(inner),
            *saved(rim),
            pltpu.SemaphoreType.DMA((19,)),
            pltpu.VMEM((feats, units), BF16),
            pltpu.VMEM((units, feats), BF16),
            pltpu.VMEM((3, inner, units), BF16),
            pltpu.VMEM((3, rim, units), BF16),
            pltpu.VMEM((cells, feats), F32),
            pltpu.VMEM((rim, feats), F32),
            pltpu.VMEM((feats, units), F32),
        ],
        compiler_params=params(36),
        cost_estimate=pl.CostEstimate(flops=16 * cells * feats * units, bytes_accessed=20 << 20, transcendentals=0),
        name="columns_backward",
    )(me, orientation, *map(stay, (cot_rows, weight_in, weight_out, *saved_inner, *saved_rim)))
    pieces_out = pl.pallas_call(
        functools.partial(output_gradient_kernel, (groups, tiles), orders[1]),
        out_shape=halves,
        in_specs=[SMEM, VMEM, VMEM],
        out_specs=[VMEM] * 2,
        scratch_shapes=[pltpu.VMEM((units, feats), F32)],
        compiler_params=params(24),
        cost_estimate=pl.CostEstimate(flops=6 * cells * feats * units, bytes_accessed=8 << 20, transcendentals=0),
        name="output_gradient",
    )(me, err_out, hidden)

    sizes = {"grp": groups, "tile": tiles}
    far = [pair for pair in orders[0] if pair[0] == "tile" and pair[1] > 1]
    near = len(orders[0]) - len(far)
    sums = [exchange_sums(*pieces, order[:near], sizes) for pieces, order in zip((pieces_in, pieces_out), orders)]
    split = sums[0][0].shape[1]
    keep, send = (jnp.concatenate(pair, axis=1) for pair in zip(*sums))
    keep, send = exchange_sums(keep, send, far[:-1], sizes)

    block = cells // 4
    tendency = pl.pallas_call(
        output_kernel,
        out_shape=shape((cells, feats), F32),
        grid=(cells // block,),
        in_specs=[pl.BlockSpec((block, units), lambda i: (i, 0)), pl.BlockSpec((units, feats), lambda i: (0, 0))],
        out_specs=pl.BlockSpec((block, feats), lambda i: (i, 0)),
        compiler_params=params(32),
        cost_estimate=pl.CostEstimate(flops=4 * cells * feats * units, bytes_accessed=6 << 20, transcendentals=0),
        name="tendency_rows",
    )(arrived, weight_out)
    (axis, bit), = far[-1:]
    arriving = lax.ppermute(send, axis, [(i, i ^ bit) for i in range(sizes[axis])])
    keep, tendency = lax.optimization_barrier((keep, tendency))
    keep = keep + arriving
    summed_in, summed_out = keep[0, :split].reshape(-1), keep[0, split:].reshape(-1)
    return (tendency, summed_in, summed_out)


def solution(mesh):
    in_specs = (
        P("tile", "grp", None),
        P("tile", "grp", None),
        P("tile", "grp"),
        P("tile", "grp"),
        P("tile", "grp"),
        P(),
        P(),
    )
    out_specs = (P(("grp", "tile"), None), P(("grp", "tile")), P(("grp", "tile")))
    return jax.shard_map(
        per_device, mesh=mesh, in_specs=in_specs, out_specs=out_specs, check_vma=False
    )
```
